32 devices in a mesh: clip: 8 (over z, x), win: 4 (over y, core).
Axes of the slice: x: 2, y: 2, z: 4, core: 2. Of those that a mesh axis runs over, the one named last changes fastest.
Arguments:
- tokens: bfloat16 [8, 20, 256, 1024], P('clip', 'win'), may hold values from -6 to 6
- condition: bfloat16 [8, 1024], P('clip'), may hold values from -6 to 6
- slot_order: int32 [8, 20], P('clip'), may hold values from 0 to 19, each once within a row
- rel_index: int32 [320, 320], replicated, may hold values from 0 to 2047
- w_qkv: bfloat16 [1024, 3072], replicated, may hold values from -0.1875 to 0.1875
- b_query: bfloat16 [1024], replicated, may hold values from -4 to 4
- b_value: bfloat16 [1024], replicated, may hold values from -3 to 3
- w_out: bfloat16 [1024, 1024], replicated, may hold values from -0.75 to 0.75
- b_out: bfloat16 [1024], replicated, may hold values from -3 to 3
- w_up: bfloat16 [1024, 4096], replicated, may hold values from -0.1875 to 0.1875
- b_up: bfloat16 [4096], replicated, may hold values from -3 to 3
- w_down: bfloat16 [4096, 1024], replicated, may hold values from -0.09375 to 0.09375
- b_down: bfloat16 [1024], replicated, may hold values from -3 to 3
- w_ada: bfloat16 [1024, 6144], replicated, may hold values from -0.1875 to 0.1875
- b_ada: bfloat16 [6144], replicated, may hold values from -3 to 3
- rel_table: float32 [2048, 16], replicated, may hold values from -5 to 5
- grad_out: bfloat16 [8, 20, 256, 1024], P('clip', 'win'), may hold values from -6 to 6
Outputs:
- block_out: bfloat16 [8, 20, 256, 1024], P('clip', 'win')
- grad_tokens: bfloat16 [8, 20, 256, 1024], P('clip', 'win')
- grad_w_qkv: float32 [1024, 3072], P('clip')
- grad_b_query: float32 [1024], P('clip')
- grad_b_value: float32 [1024], P('clip')
- grad_w_out: float32 [1024, 1024], P('clip')
- grad_b_out: float32 [1024], P('clip')
- grad_w_up: float32 [1024, 4096], P('clip')
- grad_b_up: float32 [4096], P('clip')
- grad_w_down: float32 [4096, 1024], P('clip')
- grad_b_down: float32 [1024], P('clip')
- grad_w_ada: float32 [1024, 6144], P('clip')
- grad_b_ada: float32 [6144], P('clip')
- grad_rel_table: float32 [2048, 16], P('clip')
The draws below stay inside these ranges and needn't reach their ends.
Inputs may be any that keep to these rules, and one draw needn't show every extreme that they name: Each row of slot_order is a permutation of 0 to 19.
All inputs are finite; a program needn't handle non-finite values.
Results may differ from the reference program's by a relative error of at most 0.015.
Values may be sent and summed in bfloat16 or wider, within the bound.
No kernel may reach another device: no remote copies, remote signals or barrier semaphores. Data moves between devices by JAX's collectives and lax.ppermute only.
A program may use at most 320 MiB of HBM per device.

```python
import math
import jax
import jax.numpy as jnp
from jax import lax

D = 1024
HEADS = 16
HEAD = 64
FF = 4096
FRAMES = 5
SW = 4
NREL = 2048
WST = 8
SPT = 256
WTOK = 320
SLOTS = 20
CLIPS = 8


def set_ends(drawn, own_key, least, top_value):
    longest = drawn.shape.index(max(drawn.shape))
    spots = []
    for shift in (0, 1):
        where = [jax.random.randint(jax.random.fold_in(own_key, axis), (), 0, length) for axis, length in enumerate(drawn.shape)]
        where[longest] = (where[longest] + shift) % drawn.shape[longest]
        spots.append(tuple(where))
    return drawn.at[spots[0]].set(least).at[spots[1]].set(top_value)


def strengthened(drawn, key, source, target, blocks, factor):
    def block_of(position):
        return (jnp.arange(drawn.shape[position]) // (drawn.shape[position] // blocks)).reshape((-1,) + (1,) * (drawn.ndim - 1 - position))

    near = jax.random.permutation(key, blocks)[block_of(target)]
    other_side = (block_of(target) + blocks // 2) % blocks
    return jnp.where((block_of(source) == near) | (block_of(source) == other_side), factor * drawn, drawn)


def level_of(own_key, dims, pieces, smallest, high):
    factor_of, own = 1.0, jax.random.fold_in(own_key, 6)
    for position, blocks in pieces:
        heights = jnp.exp(jax.random.uniform(jax.random.fold_in(own, position), (blocks,), jnp.float32, smallest / len(pieces), high / len(pieces)))
        factor_of = factor_of * jnp.repeat(heights, dims[position] // blocks).reshape([-1 if axis == position else 1 for axis in range(len(dims))])
    return factor_of


def centred(rng, extent, deviation, reach, shards=(), dtype=jnp.bfloat16):
    factor_of = level_of(rng, extent, shards, -0.22, 0.18) if shards else 1.0
    drawn = jax.random.normal(rng, extent, jnp.float32) * deviation * factor_of
    return jnp.minimum(jnp.maximum(drawn, -reach), reach).astype(dtype)


def noise_with(own_key, extent, deviation, most, pieces, heavy, held_as=jnp.bfloat16):
    values = deviation * jax.random.normal(own_key, extent, jnp.float32)
    if pieces:
        values = values * level_of(own_key, extent, pieces, -0.22, 0.18)
    return jnp.clip(strengthened(values, jax.random.fold_in(own_key, 3), *heavy), -most, most).astype(held_as)


def setup_inputs(seed: int = 0) -> dict:
    keys = jax.random.split(jax.random.key(seed), 18)
    tokens = centred(keys[0], (CLIPS, SLOTS, SPT, D), 1.0, 6.0, ((0, 8), (1, 4)))
    condition = centred(keys[1], (CLIPS, D), 1.0, 6.0, ((0, 8),))
    slot_order = jax.vmap(lambda own: jax.random.permutation(own, SLOTS))(jax.random.split(keys[2], CLIPS)).reshape((CLIPS, SLOTS)).astype(jnp.int32)
    rel_index = set_ends(jax.random.randint(keys[3], (WTOK, WTOK), 0, NREL), jax.random.fold_in(keys[3], 1), 0, NREL - 1).astype(jnp.int32)
    w_qkv = centred(keys[4], (D, 3 * D), D ** -0.5, 0.1875)
    b_query = centred(keys[5], (D,), 1.0, 4.0)
    b_value = centred(keys[6], (D,), 0.5, 3.0)
    w_out = centred(keys[7], (D, D), (D // 16) ** -0.5, 0.75)
    b_out = centred(keys[8], (D,), 0.5, 3.0)
    w_up = centred(keys[9], (D, FF), D ** -0.5, 0.1875)
    b_up = centred(keys[10], (FF,), 0.5, 3.0)
    w_down = centred(keys[11], (FF, D), FF ** -0.5, 0.09375)
    b_down = centred(keys[12], (D,), 0.5, 3.0)
    w_ada = centred(keys[13], (D, 6 * D), D ** -0.5, 0.1875)
    b_ada = centred(keys[14], (6 * D,), 0.5, 3.0)
    rel_table = centred(keys[15], (NREL, HEADS), 1.0, 5.0, (), jnp.float32)
    grad_out = noise_with(keys[16], (CLIPS, SLOTS, SPT, D), 1.0, 6.0, ((0, 8), (1, 4)), (0, 3, 8, 2.0))
    return {"tokens": tokens, "condition": condition, "slot_order": slot_order, "rel_index": rel_index, "w_qkv": w_qkv, "b_query": b_query, "b_value": b_value, "w_out": w_out, "b_out": b_out, "w_up": w_up, "b_up": b_up, "w_down": w_down, "b_down": b_down, "w_ada": w_ada, "b_ada": b_ada, "rel_table": rel_table, "grad_out": grad_out}


@jax.custom_vjp
def low(v):
    return lax.optimization_barrier(v.astype(jnp.bfloat16)).astype(jnp.float32)

@jax.custom_vjp
def low_back(v):
    return v

def low_keep(v):
    return (low(v), None)

def low_pass(kept, grad):
    return (grad,)

def back_keep(v):
    return (v, None)

def back_low(kept, grad):
    return (low(grad),)
low.defvjp(low_keep, low_pass)
low_back.defvjp(back_keep, back_low)

def matmul(left, right):
    return jnp.dot(left, right, precision=lax.Precision.HIGHEST)

def normalize(values):
    average = lax.optimization_barrier(jnp.mean(values, axis=-1, keepdims=True))
    centered = values - average
    variance = lax.optimization_barrier(jnp.mean(centered * centered, axis=-1, keepdims=True))
    return centered * lax.rsqrt(variance + 1e-06)

def to_windows(slot_rows, order_row):
    channels = slot_rows.shape[-1]
    inverse = jnp.argsort(order_row).astype(jnp.int32)
    arranged = jnp.take(slot_rows, inverse, axis=0)
    arranged = arranged.reshape(FRAMES, SW, 2, WST, 2, WST, channels)
    arranged = arranged.transpose(1, 2, 4, 0, 3, 5, 6)
    return arranged.reshape(SW * 4, WTOK, channels)

def from_windows(window_rows, order_row):
    channels = window_rows.shape[-1]
    arranged = window_rows.reshape(SW, 2, 2, FRAMES, WST, WST, channels)
    arranged = arranged.transpose(3, 0, 1, 4, 2, 5, 6).reshape(SLOTS, SPT, channels)
    return jnp.take(arranged, order_row.astype(jnp.int32), axis=0)

def attend(queries, keys_all, values, pos_bias):
    scores = jnp.einsum('wqhe,wkhe->whqk', queries, keys_all, precision=lax.Precision.HIGHEST) * (1.0 / math.sqrt(HEAD))
    scores = low_back(scores + pos_bias[None])
    weights_soft = jax.nn.softmax(scores, axis=-1)
    return jnp.einsum('whqk,wkhe->wqhe', low(weights_soft), values, precision=lax.Precision.HIGHEST)

def clip_forward(clip_tokens, clip_condition, params, order_row, rel_index):
    w_qkv, b_query, b_value, w_out, b_out, w_up, b_up, w_down, b_down, w_ada, b_ada, rel_table = params
    modulation = matmul(low(jax.nn.silu(clip_condition))[None], w_ada)[0] + b_ada
    shift_one, scale_one, gate_one, shift_two, scale_two, gate_two = jnp.split(modulation, 6)
    inputs_flat = clip_tokens.reshape(SLOTS * SPT, D)
    normed = low_back(low(normalize(inputs_flat) * (1.0 + scale_one) + shift_one))
    qkv_bias = jnp.concatenate([b_query, jnp.zeros_like(b_query), b_value])
    projected = low_back(low(matmul(normed, w_qkv) + qkv_bias))
    windows = to_windows(projected.reshape(SLOTS, SPT, 3 * D), order_row)
    queries, keys_all, values = jnp.split(windows, 3, axis=-1)
    head_shape = (SW * 4, WTOK, HEADS, HEAD)
    pos_bias = jnp.transpose(rel_table[rel_index], (2, 0, 1))
    attended = attend(queries.reshape(head_shape), keys_all.reshape(head_shape), values.reshape(head_shape), pos_bias)
    attended = low_back(low(attended.reshape(SW * 4, WTOK, D)))
    returned = from_windows(attended, order_row).reshape(SLOTS * SPT, D)
    branch = low_back(matmul(returned, w_out) + b_out)
    residual_one = inputs_flat + gate_one * branch
    normed_two = low(normalize(residual_one) * (1.0 + scale_two) + shift_two)
    hidden = low_back(matmul(normed_two, w_up) + b_up)
    activated = low(jax.nn.gelu(hidden, approximate=True))
    mixed_out = low_back(matmul(activated, w_down) + b_down)
    return (residual_one + gate_two * mixed_out).reshape(SLOTS, SPT, D)

def reference(tokens, condition, slot_order, rel_index, w_qkv, b_query, b_value, w_out, b_out, w_up, b_up, w_down, b_down, w_ada, b_ada, rel_table, grad_out):
    params = tuple((weight_arr.astype(jnp.float32) for weight_arr in (w_qkv, b_query, b_value, w_out, b_out, w_up, b_up, w_down, b_down, w_ada, b_ada, rel_table)))

    def step_clip(totals, inputs):
        clip_tokens, clip_condition, order_row, cotangent = inputs
        cond_float = clip_condition.astype(jnp.float32)

        def forward(tokens_in, params_in):
            return clip_forward(tokens_in, cond_float, params_in, order_row, rel_index)
        output, pullback = jax.vjp(forward, clip_tokens.astype(jnp.float32), params)
        grad_in, grad_params = pullback(cotangent.astype(jnp.float32))
        totals = jax.tree.map(jnp.add, totals, grad_params)
        return (totals, (output.astype(jnp.bfloat16), grad_in.astype(jnp.bfloat16)))
    zeros_init = jax.tree.map(jnp.zeros_like, params)
    totals, (outputs, grads_in) = lax.scan(step_clip, zeros_init, (tokens, condition, slot_order, grad_out))
    return (outputs, grads_in, totals[0], totals[1], totals[2], totals[3], totals[4], totals[5], totals[6], totals[7], totals[8], totals[9], totals[10], totals[11])
```

```python
import functools
import math

import jax
import jax.numpy as jnp
from jax import lax
from jax.experimental import pallas as pl
from jax.experimental.pallas import tpu as pltpu
from jax.sharding import PartitionSpec as P

HEAD = 64
FRAMES = 5
WST = 8
PIECE = WST * WST
UNIT = 256
LANES = 128
VMEM_LIMIT = 60 * 1024 * 1024
f32 = jnp.float32
bf16 = jnp.bfloat16
GELU_C = math.sqrt(2.0 / math.pi)
GELU_A = 0.044715


def dot_nn(a, b):
    return jnp.dot(a, b, preferred_element_type=f32)


def dot_nt(a, b):
    return lax.dot_general(a, b, (((1,), (1,)), ((), ())), preferred_element_type=f32)


def dot_tn(a, b):
    return lax.dot_general(a, b, (((0,), (0,)), ((), ())), preferred_element_type=f32)


def params():
    return pltpu.CompilerParams(vmem_limit_bytes=VMEM_LIMIT)


def cost(micros):
    return pl.CostEstimate(
        flops=int(micros * 1.0e9), bytes_accessed=int(micros * 2.0e6), transcendentals=0
    )


def hat_of(rows):
    average = jnp.mean(rows, axis=-1, keepdims=True)
    centered = rows - average
    variance = jnp.mean(centered * centered, axis=-1, keepdims=True)
    inv_std = lax.rsqrt(variance + 1e-06)
    return centered * inv_std, inv_std


def norm_back(grad_hat, hat_rows, inv_std):
    first_mean = jnp.mean(grad_hat, axis=-1, keepdims=True)
    second_mean = jnp.mean(grad_hat * hat_rows, axis=-1, keepdims=True)
    return inv_std * (grad_hat - first_mean - hat_rows * second_mean)


def whole(shape):
    zeros = (0,) * len(shape)
    return pl.BlockSpec(shape, lambda *unused: zeros, pipeline_mode=pl.Buffered(1))


def bias_kernel(idx_ref, tab_ref, out_ref, scr_ref):
    lows = lax.broadcasted_iota(jnp.int32, (256, idx_ref.shape[1]), 0)
    tab = tab_ref[...]
    half = tab.shape[0] // 2
    heads = 16
    tiles = idx_ref.shape[1] // LANES
    win = out_ref.shape[2] // 2
    for i in range(8):
        idx = idx_ref[pl.ds(i, 1), :]
        low = idx & 255
        high = idx >> 8
        onehot = jnp.where(lows == low, 1.0, 0.0).astype(bf16)
        got = dot_nn(tab, onehot)
        got = got[:half] + got[half:]
        acc = got[:heads]
        for c in range(1, half // heads):
            acc = jnp.where(high == c, got[c * heads : (c + 1) * heads], acc)
        for t in range(tiles):
            scr_ref[t, pl.ds(i, heads, stride=8), :] = acc[:, t * LANES : (t + 1) * LANES]
    for pair in range(heads // 2):
        rows = []
        for h in range(2):
            at = (2 * pair + h) * 8
            rows.append(
                jnp.concatenate([scr_ref[t, at : at + 8, :] for t in range(tiles)], axis=1)[:, :win]
            )
        out_ref[pair] = jnp.concatenate(rows, axis=1)


def bias_gather(idx, table):
    rows, win = idx.shape
    padded = -(-win // LANES) * LANES
    buckets, heads = table.shape
    upper_f = lax.reduce_precision(table, 8, 7)
    lower = (table - upper_f).astype(bf16)

    def arrange(t):
        return t.reshape(-1, 256, heads).transpose(0, 2, 1).reshape(-1, 256)

    tab = jnp.concatenate([arrange(upper_f.astype(bf16)), arrange(lower)], axis=0)
    idx = jnp.pad(idx, ((0, 0), (0, padded - win)))
    return pl.pallas_call(
        bias_kernel,
        grid=(rows // 8,),
        in_specs=[pl.BlockSpec((8, padded), lambda i: (i, 0)), whole(tab.shape)],
        out_specs=pl.BlockSpec((heads // 2, 8, 2 * win), lambda i: (0, i, 0)),
        out_shape=jax.ShapeDtypeStruct((heads // 2, rows, 2 * win), f32),
        scratch_shapes=[pltpu.VMEM((padded // LANES, 8 * heads, LANES), f32)],
        name="bias_gather",
        compiler_params=params(),
        cost_estimate=cost(18),
    )(idx, tab)


def bucket_kernel(idx_ref, ss_ref, out_ref, acc_ref, scr_ref):
    @pl.when(pl.program_id(0) == 0)
    def _():
        acc_ref[...] = jnp.zeros_like(acc_ref)

    padded = idx_ref.shape[1]
    tiles = padded // LANES
    pairs = ss_ref.shape[0]
    heads = 2 * pairs
    win = ss_ref.shape[2] // 2
    lows = lax.broadcasted_iota(jnp.int32, (256, padded), 0)
    zero = jnp.zeros((8, padded - win), f32)
    for pair in range(pairs):
        sums = ss_ref[pair]
        for h in range(2):
            part = jnp.concatenate([sums[:, h * win : (h + 1) * win], zero], axis=1)
            at = (2 * pair + h) * 8
            for t in range(tiles):
                scr_ref[t, at : at + 8, :] = part[:, t * LANES : (t + 1) * LANES]
    total = acc_ref[...]
    for i in range(8):
        idx = idx_ref[pl.ds(i, 1), :]
        low = idx & 255
        high = idx >> 8
        onehot = jnp.where(lows == low, 1.0, 0.0).astype(bf16)
        sums = jnp.concatenate(
            [scr_ref[t, pl.ds(i, heads, stride=8), :] for t in range(tiles)], axis=1
        )
        spread = jnp.concatenate(
            [jnp.where(high == c, sums, 0.0) for c in range(acc_ref.shape[0] // heads)], axis=0
        )
        total += dot_nt(spread.astype(bf16), onehot)
    acc_ref[...] = total
    out_ref[...] = total


def bucket_sums(idx, sums, buckets):
    rows, win = idx.shape
    padded = -(-win // LANES) * LANES
    heads = 2 * sums.shape[0]
    idx = jnp.pad(idx, ((0, 0), (0, padded - win)))
    out_rows = buckets // 256 * heads
    out = pl.pallas_call(
        bucket_kernel,
        grid=(rows // 8,),
        in_specs=[
            pl.BlockSpec((8, padded), lambda i: (i, 0)),
            pl.BlockSpec((heads // 2, 8, 2 * win), lambda i: (0, i, 0)),
        ],
        out_specs=pl.BlockSpec((out_rows, 256), lambda i: (0, 0)),
        out_shape=jax.ShapeDtypeStruct((out_rows, 256), f32),
        scratch_shapes=[
            pltpu.VMEM((out_rows, 256), f32),
            pltpu.VMEM((padded // LANES, 8 * heads, LANES), f32),
        ],
        name="bucket_sums",
        compiler_params=params(),
        cost_estimate=cost(18),
    )(idx, sums)
    return out.reshape(-1, heads, 256)


def qkv_kernel(src_ref, a_ref, b_ref, c_ref, d_ref, mod_ref, bias_ref, w_ref, x_ref, n_ref, o_ref):
    rows = jnp.concatenate([r[0] for r in (a_ref, b_ref, c_ref, d_ref)], axis=0)
    x_ref[...] = rows
    hat_rows, unused = hat_of(rows.astype(f32))
    normed = (hat_rows * (1.0 + mod_ref[1:2, :]) + mod_ref[0:1, :]).astype(bf16)
    n_ref[...] = normed
    features = rows.shape[1]
    for j in range(w_ref.shape[1] // 512):
        cols = slice(j * 512, (j + 1) * 512)
        got = dot_nn(normed, w_ref[:, cols]) + bias_ref[0:1, cols]
        if (j + 1) * 512 <= features:
            got = got.astype(bf16).astype(f32) * (1.0 / math.sqrt(HEAD))
        o_ref[:, cols] = got.astype(bf16)


def slot_spec(features, t):
    return pl.BlockSpec((1, PIECE, features), lambda i, src, t=t: (src[4 * i + t], 0, 0))


def qkv_call(src, pieces, mod, qkv_bias, w_qkv):
    count, unused, features = pieces.shape
    rows = count * PIECE
    wide = w_qkv.shape[1]
    block = 4 * PIECE
    return pl.pallas_call(
        qkv_kernel,
        grid_spec=pltpu.PrefetchScalarGridSpec(
            num_scalar_prefetch=1,
            grid=(count // 4,),
            in_specs=[slot_spec(features, t) for t in range(4)]
            + [whole(mod.shape), whole(qkv_bias.shape), whole(w_qkv.shape)],
            out_specs=[
                pl.BlockSpec((block, features), lambda i, src: (i, 0)),
                pl.BlockSpec((block, features), lambda i, src: (i, 0)),
                pl.BlockSpec((block, wide), lambda i, src: (i, 0)),
            ],
        ),
        out_shape=[
            jax.ShapeDtypeStruct((rows, features), bf16),
            jax.ShapeDtypeStruct((rows, features), bf16),
            jax.ShapeDtypeStruct((rows, wide), bf16),
        ],
        name="norm_qkv",
        compiler_params=params(),
        cost_estimate=cost(12),
    )(src, pieces, pieces, pieces, pieces, mod, qkv_bias, w_qkv)


def split_pair(x, left):
    zero = jnp.zeros_like(x)
    return jnp.concatenate([jnp.where(left, x, zero), jnp.where(left, zero, x)], axis=0)


def values_ones(v, left):
    one = jnp.ones_like(v)
    zero = jnp.zeros_like(v)
    marks = jnp.concatenate([jnp.where(left, one, zero), jnp.where(left, zero, one)], axis=0)
    return jnp.concatenate([split_pair(v, left), marks], axis=1)


def attn_kernel(windows, core_ref, q_ref, k_ref, v_ref, mine_ref, other_ref, o_ref, p_ref, r_ref, b_ref):
    win = q_ref.shape[0] // windows
    half = win // 2
    left = lax.broadcasted_iota(jnp.int32, (win, LANES), 1) < HEAD
    first = core_ref[0] == 0
    b_ref[:half] = jnp.where(first, mine_ref[0], other_ref[0])
    b_ref[half:] = jnp.where(first, other_ref[0], mine_ref[0])
    lowest = jnp.float32(-jnp.inf)
    whole_tiles = win // LANES * LANES
    for u in range(windows):
        rows = slice(u * win, (u + 1) * win)
        keys = split_pair(k_ref[rows], left)
        vals = values_ones(v_ref[rows], left)
        s = dot_nt(q_ref[rows], keys) + b_ref[...]
        lo = s[:, :whole_tiles]
        mid = s[:, whole_tiles : whole_tiles + LANES]
        hi = s[:, whole_tiles + LANES :]
        top_lo = jnp.where(left, mid, lowest)
        top_hi = jnp.where(left, lowest, mid)
        for t in range(whole_tiles // LANES):
            cols = slice(t * LANES, (t + 1) * LANES)
            top_lo = jnp.maximum(top_lo, lo[:, cols])
            top_hi = jnp.maximum(top_hi, hi[:, cols])
        top_lo = jnp.max(top_lo, axis=1, keepdims=True)
        top_hi = jnp.max(top_hi, axis=1, keepdims=True)
        e = jnp.concatenate(
            [
                jnp.exp(lo - top_lo),
                jnp.exp(mid - jnp.where(left, top_lo, top_hi)),
                jnp.exp(hi - top_hi),
            ],
            axis=1,
        ).astype(bf16)
        p_ref[0, u] = e
        got = dot_nn(e, vals)
        r = 1.0 / got[:, LANES:]
        r_ref[rows] = r
        o_ref[rows] = (got[:, :LANES] * r).astype(bf16)


def attn_forward(core, qkv, bias_mine, bias_other, windows):
    rows = qkv.shape[0]
    win = rows // windows
    pairs = bias_mine.shape[0]
    features = qkv.shape[1] // 3

    def col(part):
        return pl.BlockSpec((rows, LANES), lambda h, c, part=part: (0, part * pairs + h))

    half_spec = pl.BlockSpec((1, win // 2, 2 * win), lambda h, c: (h, 0, 0))
    return pl.pallas_call(
        functools.partial(attn_kernel, windows),
        grid_spec=pltpu.PrefetchScalarGridSpec(
            num_scalar_prefetch=1,
            grid=(pairs,),
            in_specs=[col(0), col(1), col(2), half_spec, half_spec],
            out_specs=[
                col(0),
                pl.BlockSpec((1, windows, win, 2 * win), lambda h, c: (h, 0, 0, 0)),
                col(0),
            ],
            scratch_shapes=[pltpu.VMEM((win, 2 * win), f32)],
        ),
        out_shape=[
            jax.ShapeDtypeStruct((rows, features), bf16),
            jax.ShapeDtypeStruct((pairs, windows, win, 2 * win), bf16),
            jax.ShapeDtypeStruct((rows, features), f32),
        ],
        name="attn_forward",
        compiler_params=params(),
        cost_estimate=cost(18),
    )(core, qkv, qkv, qkv, bias_mine, bias_other)


def fold_delta(dx, lane):
    lower_half = (lane & 32) == 0
    dx = dx + jnp.where(lower_half, pltpu.roll(dx, LANES - 32, 1), pltpu.roll(dx, 32, 1))
    upper = dx.astype(bf16)
    lower = (dx - upper.astype(f32)).astype(bf16)
    return jnp.where(lower_half, upper, lower)


def attn_back_kernel(windows, q_ref, k_ref, v_ref, o_ref, do_ref, p_ref, r_ref, dq_ref, dk_ref, dv_ref, ss_ref):
    win = q_ref.shape[0] // windows
    lane = lax.broadcasted_iota(jnp.int32, (win, LANES), 1)
    left = lane < HEAD
    sums = None
    for u in range(windows):
        rows = slice(u * win, (u + 1) * win)
        keys = split_pair(k_ref[rows], left)
        vals = values_ones(v_ref[rows], left)
        up = (do_ref[rows].astype(f32) * r_ref[rows]).astype(bf16)
        delta = fold_delta(-(up.astype(f32) * o_ref[rows].astype(f32)), lane)
        d = dot_nt(jnp.concatenate([up, delta], axis=1), vals)
        p = p_ref[0, u]
        ds = p.astype(f32) * d
        sums = ds if sums is None else sums + ds
        low = ds.astype(bf16)
        dq_ref[rows] = (dot_nn(low, keys) * (1.0 / math.sqrt(HEAD))).astype(bf16)
        dk = dot_tn(low, q_ref[rows])
        dk_ref[rows] = jnp.where(left, dk[:win], dk[win:]).astype(bf16)
        dv = dot_tn(p, up)
        dv_ref[rows] = jnp.where(left, dv[:win], dv[win:]).astype(bf16)
    ss_ref[0] = sums


def attn_backward(qkv, attended, grad_att, probs, recips, windows, first, count):
    rows = qkv.shape[0]
    win = rows // windows
    pairs = probs.shape[0]

    def col(part):
        return pl.BlockSpec((rows, LANES), lambda h, part=part: (0, part * pairs + first + h))

    own = pl.BlockSpec((rows, LANES), lambda h: (0, h))
    grad_shape = jax.ShapeDtypeStruct((rows, count * LANES), bf16)
    return pl.pallas_call(
        functools.partial(attn_back_kernel, windows),
        grid=(count,),
        in_specs=[
            col(0),
            col(1),
            col(2),
            col(0),
            col(0),
            pl.BlockSpec((1, windows, win, 2 * win), lambda h: (first + h, 0, 0, 0)),
            col(0),
        ],
        out_specs=[own, own, own, pl.BlockSpec((1, win, 2 * win), lambda h: (h, 0, 0))],
        out_shape=[
            grad_shape,
            grad_shape,
            grad_shape,
            jax.ShapeDtypeStruct((count, win, 2 * win), f32),
        ],
        name="attn_backward",
        compiler_params=params(),
        cost_estimate=cost(3 * count),
    )(qkv, qkv, qkv, attended, grad_att, probs, recips)


def out_kernel(src_ref, a_ref, b_ref, c_ref, d_ref, att_ref, x_ref, mod_ref, bo_ref, w_ref, branch_ref, n_ref, gm_ref):
    branch = (dot_nn(att_ref[...], w_ref[...]) + bo_ref[...]).astype(bf16)
    branch_ref[...] = branch
    residual = x_ref[...].astype(f32) + mod_ref[2:3, :] * branch.astype(f32)
    hat_rows, unused = hat_of(residual)
    n_ref[...] = (hat_rows * (1.0 + mod_ref[4:5, :]) + mod_ref[3:4, :]).astype(bf16)
    up = jnp.concatenate([r[0] for r in (a_ref, b_ref, c_ref, d_ref)], axis=0)
    gm_ref[...] = (mod_ref[5:6, :] * up.astype(f32)).astype(bf16)


def out_call(src, pieces, attended, x_rows, mod, b_out, w_out):
    count, unused, features = pieces.shape
    rows = count * PIECE
    block = 4 * PIECE
    rows_spec = pl.BlockSpec((block, features), lambda i, src: (i, 0))
    sds = jax.ShapeDtypeStruct((rows, features), bf16)
    return pl.pallas_call(
        out_kernel,
        grid_spec=pltpu.PrefetchScalarGridSpec(
            num_scalar_prefetch=1,
            grid=(count // 4,),
            in_specs=[slot_spec(features, t) for t in range(4)]
            + [rows_spec, rows_spec, whole(mod.shape), whole(b_out.shape), whole(w_out.shape)],
            out_specs=[rows_spec, rows_spec, rows_spec],
        ),
        out_shape=[sds, sds, sds],
        name="out_norm",
        compiler_params=params(),
        cost_estimate=cost(6),
    )(src, pieces, pieces, pieces, pieces, attended, x_rows, mod, b_out, w_out)


def turn_kernel(order_ref, swap_ref, x_ref, out_ref):
    turned = x_ref[...].T
    half = turned.shape[0] // 2
    swap = swap_ref[0] == 1
    upper, lower = turned[:half], turned[half:]
    out_ref[0] = jnp.where(swap, lower, upper)
    out_ref[1] = jnp.where(swap, upper, lower)


def turn(order, swap, rows):
    count, features = rows.shape
    out = pl.pallas_call(
        turn_kernel,
        grid_spec=pltpu.PrefetchScalarGridSpec(
            num_scalar_prefetch=2,
            grid=(features // LANES,),
            in_specs=[pl.BlockSpec((count, LANES), lambda i, order, swap: (0, order[i]))],
            out_specs=pl.BlockSpec((2, LANES // 2, count), lambda i, order, swap: (0, i, 0)),
        ),
        out_shape=jax.ShapeDtypeStruct((2, features // 2, count), bf16),
        name="turn",
        compiler_params=params(),
        cost_estimate=cost(4),
    )(order, swap, rows)
    return out.reshape(features, count)


def ff_step(n_ref, gm_ref, nt_ref, gt_ref, wu_ref, bu_ref, wd_ref, up_refs, down_refs, bsum_ref, mixed_ref, back_ref, act_ref, gh_ref, first):
    rows = n_ref.shape[0]
    block = UNIT
    sums = None
    for c in range(rows // block):
        part = slice(c * block, (c + 1) * block)
        v = dot_nn(n_ref[part], wu_ref[...]) + bu_ref[0]
        v2 = v * v
        t = jnp.tanh(v * (GELU_C + (GELU_C * GELU_A) * v2))
        h = 0.5 + 0.5 * t
        act = (v * h).astype(bf16)
        slope = h + (0.5 * v) * (1.0 - t * t) * (GELU_C + (3.0 * GELU_C * GELU_A) * v2)
        gh = (dot_nt(gm_ref[part], wd_ref[...]) * slope).astype(bf16)
        act_ref[part] = act
        gh_ref[part] = gh
        piece = jnp.sum(gh.astype(f32), axis=0, keepdims=True)
        sums = piece if sums is None else sums + piece
        mixed = dot_nn(act, wd_ref[...])
        back = dot_nt(gh, wu_ref[...])

        @pl.when(first)
        def _():
            mixed_ref[part] = mixed
            back_ref[part] = back

        @pl.when(jnp.logical_not(first))
        def _():
            mixed_ref[part] += mixed
            back_ref[part] += back

    bsum_ref[0] = sums
    half = nt_ref.shape[0] // 2
    for k in range(2):
        part = slice(k * half, (k + 1) * half)
        up_refs[k][...] = dot_nn(nt_ref[part], gh_ref[...]).astype(bf16)
        down_refs[k][0] = dot_nn(gt_ref[part], act_ref[...]).astype(bf16)


def ff_first_kernel(fo_ref, co_ref, n_ref, gm_ref, nt_ref, gt_ref, wu_ref, bu_ref, wd_ref, u0, u1, d0, d1, bsum_ref, pm_ref, pb_ref, mixed_ref, back_ref, act_ref, gh_ref):
    step = pl.program_id(0)
    ff_step(n_ref, gm_ref, nt_ref, gt_ref, wu_ref, bu_ref, wd_ref, (u0, u1), (d0, d1), bsum_ref, mixed_ref, back_ref, act_ref, gh_ref, step == 0)

    @pl.when(step == pl.num_programs(0) - 1)
    def _():
        pm_ref[...] = mixed_ref[...].astype(bf16)
        pb_ref[...] = back_ref[...].astype(bf16)


def ff_specs(units, rows, features, fast):
    def clamp(i):
        return jnp.minimum(i, units - 1)

    ins = [
        whole((rows, features)),
        whole((rows, features)),
        whole((features, rows)),
        whole((features, rows)),
        pl.BlockSpec((features, UNIT), lambda i, fo, co, *more: (0, fo[clamp(i)])),
        pl.BlockSpec((1, 1, UNIT), lambda i, fo, co, *more: (fo[clamp(i)], 0, 0)),
        pl.BlockSpec((UNIT, features), lambda i, fo, co, *more: (fo[clamp(i)], 0)),
    ]
    up = pl.BlockSpec((features // 2, UNIT), lambda i, fo, co, *more: (0, co[clamp(i)]))
    down = pl.BlockSpec((1, features // 2, UNIT), lambda i, fo, co, *more: (clamp(i), 0, 0))
    outs = [up, up, down, down, pl.BlockSpec((1, 1, UNIT), lambda i, fo, co, *more: (co[clamp(i)], 0, 0))]
    shapes = [
        jax.ShapeDtypeStruct((features // 2, units * UNIT), bf16),
        jax.ShapeDtypeStruct((features // 2, units * UNIT), bf16),
        jax.ShapeDtypeStruct((units, features // 2, UNIT), bf16),
        jax.ShapeDtypeStruct((units, features // 2, UNIT), bf16),
        jax.ShapeDtypeStruct((units, 1, UNIT), f32),
    ]
    scratch = [
        pltpu.VMEM((rows, features), f32),
        pltpu.VMEM((rows, features), f32),
        pltpu.VMEM((rows, UNIT), bf16),
        pltpu.VMEM((rows, UNIT), bf16),
    ]
    return ins, outs, shapes, scratch


def ff_first(fo, co, normed, grad_mixed, normed_t, grad_t, w_up, b_up, w_down):
    units = fo.shape[0]
    rows, features = normed.shape
    ins, outs, shapes, scratch = ff_specs(units, rows, features, True)
    once = pl.BlockSpec((rows, features), lambda i, fo, co: (0, 0), pipeline_mode=pl.Buffered(1))
    return pl.pallas_call(
        ff_first_kernel,
        grid_spec=pltpu.PrefetchScalarGridSpec(
            num_scalar_prefetch=2,
            grid=(units,),
            in_specs=ins,
            out_specs=outs + [once, once],
            scratch_shapes=scratch,
        ),
        out_shape=shapes + [jax.ShapeDtypeStruct((rows, features), bf16)] * 2,
        name="ff_first",
        compiler_params=params(),
        cost_estimate=cost(40),
    )(fo, co, normed, grad_mixed, normed_t, grad_t, w_up, b_up, w_down)


def ff_second_kernel(units, fo_ref, co_ref, src_ref, n_ref, gm_ref, nt_ref, gt_ref, wu_ref, bu_ref, wd_ref, a_ref, b_ref, c_ref, d_ref, x_ref, branch_ref, pm_ref, pb_ref, mod_ref, bd_ref, u0, u1, d0, d1, bsum_ref, gres_ref, vec_ref, out_ref, mixed_ref, back_ref, act_ref, gh_ref, stage_ref, sem_ref):
    step = pl.program_id(0)

    @pl.when(step < units)
    def _():
        ff_step(n_ref, gm_ref, nt_ref, gt_ref, wu_ref, bu_ref, wd_ref, (u0, u1), (d0, d1), bsum_ref, mixed_ref, back_ref, act_ref, gh_ref, step == 0)

    @pl.when(step >= units)
    def _():
        e = step - units
        block = 4 * PIECE
        part = pl.ds(pl.multiple_of(e * block, block), block)
        mixed = mixed_ref[part] + pm_ref[...].astype(f32) + bd_ref[...]
        back = back_ref[part] + pb_ref[...].astype(f32)
        branch = branch_ref[...].astype(f32)
        gate_one = mod_ref[2:3, :]
        gate_two = mod_ref[5:6, :]
        residual = x_ref[...].astype(f32) + gate_one * branch
        hat_rows, inv_std = hat_of(residual)
        up = jnp.concatenate([r[0] for r in (a_ref, b_ref, c_ref, d_ref)], axis=0).astype(f32)
        block_out = (residual + gate_two * mixed).astype(bf16)
        stage_ref[part] = block_out
        for t in range(4):
            pltpu.make_async_copy(
                stage_ref.at[pl.ds(pl.multiple_of(e * block + t * PIECE, PIECE), PIECE)],
                out_ref.at[src_ref[4 * e + t]],
                sem_ref.at[4 * e + t],
            ).start()
        gres = up + norm_back(back * (1.0 + mod_ref[4:5, :]), hat_rows, inv_std)
        low = gres.astype(bf16)
        gres_ref[...] = low
        grad_branch = (gate_one * low.astype(f32)).astype(bf16).astype(f32)
        grad_mixed = (gate_two * up).astype(bf16).astype(f32)

        def total(values):
            return jnp.sum(values, axis=0, keepdims=True)

        pieces = jnp.concatenate(
            [
                total(gres * branch),
                total(back),
                total(back * hat_rows),
                total(up * mixed),
                total(grad_branch),
                total(grad_mixed),
                jnp.zeros((2, gate_one.shape[1]), f32),
            ],
            axis=0,
        )

        @pl.when(e == 0)
        def _():
            vec_ref[...] = pieces

        @pl.when(e > 0)
        def _():
            vec_ref[...] += pieces

    @pl.when(step == pl.num_programs(0) - 1)
    def _():
        for k in range(sem_ref.shape[0]):
            pltpu.make_async_copy(
                stage_ref.at[pl.ds(k * PIECE, PIECE)], out_ref.at[src_ref[k]], sem_ref.at[k]
            ).wait()


def ff_second(fo, co, src, normed, grad_mixed, normed_t, grad_t, w_up, b_up, w_down, pieces, x_rows, branch, part_mixed, part_back, mod, b_down):
    units = fo.shape[0]
    rows, features = normed.shape
    ins, outs, shapes, scratch = ff_specs(units, rows, features, True)
    block = 4 * PIECE

    def late(i):
        return jnp.maximum(i - units, 0)

    rows_spec = pl.BlockSpec((block, features), lambda i, *more: (late(i), 0))
    slots = [
        pl.BlockSpec((1, PIECE, features), lambda i, fo, co, src, t=t: (src[4 * late(i) + t], 0, 0))
        for t in range(4)
    ]
    return pl.pallas_call(
        functools.partial(ff_second_kernel, units),
        grid_spec=pltpu.PrefetchScalarGridSpec(
            num_scalar_prefetch=3,
            grid=(units + rows // block,),
            in_specs=ins
            + slots
            + [rows_spec, rows_spec, rows_spec, rows_spec, whole(mod.shape), whole(b_down.shape)],
            out_specs=outs
            + [
                rows_spec,
                pl.BlockSpec((8, features), lambda i, *more: (0, 0)),
                pl.BlockSpec(memory_space=pl.ANY),
            ],
            scratch_shapes=scratch
            + [pltpu.VMEM((rows, features), bf16), pltpu.SemaphoreType.DMA((rows // PIECE,))],
        ),
        out_shape=shapes
        + [
            jax.ShapeDtypeStruct((rows, features), bf16),
            jax.ShapeDtypeStruct((8, features), f32),
            jax.ShapeDtypeStruct(pieces.shape, bf16),
        ],
        name="ff_second",
        compiler_params=params(),
        cost_estimate=cost(50),
    )(fo, co, src, normed, grad_mixed, normed_t, grad_t, w_up, b_up, w_down, pieces, pieces, pieces, pieces, x_rows, branch, part_mixed, part_back, mod, b_down)


def out_back_kernel(blocks, gres_ref, mod_ref, w_ref, at_ref, do_ref, g0, g1, gb_ref):
    step = pl.program_id(0)

    @pl.when(step < blocks)
    def _():
        block = gres_ref.shape[0]
        low = (mod_ref[2:3, :] * gres_ref[...].astype(f32)).astype(bf16)
        gb_ref[pl.ds(pl.multiple_of(step * block, block), block)] = low
        do_ref[...] = dot_nt(low, w_ref[...]).astype(bf16)

    @pl.when(step >= blocks)
    def _():
        width = g0.shape[1]
        cols = pl.ds(pl.multiple_of((step - blocks) * width, width), width)
        half = g0.shape[0]
        right = gb_ref[:, cols]
        g0[...] = dot_nn(at_ref[:half], right).astype(bf16)
        g1[...] = dot_nn(at_ref[half:], right).astype(bf16)


def out_backward(gres, mod, w_out, attended_t):
    rows, features = gres.shape
    block = 4 * PIECE
    blocks = rows // block
    rows_spec = pl.BlockSpec((block, features), lambda i: (jnp.minimum(i, blocks - 1), 0))
    col_spec = pl.BlockSpec((features // 2, UNIT), lambda i: (0, jnp.maximum(i - blocks, 0)))
    grad = jax.ShapeDtypeStruct((features // 2, features), bf16)
    return pl.pallas_call(
        functools.partial(out_back_kernel, blocks),
        grid=(blocks + features // UNIT,),
        in_specs=[rows_spec, whole(mod.shape), whole(w_out.shape), whole(attended_t.shape)],
        out_specs=[rows_spec, col_spec, col_spec],
        out_shape=[jax.ShapeDtypeStruct((rows, features), bf16), grad, grad],
        scratch_shapes=[pltpu.VMEM((rows, features), bf16)],
        name="out_backward",
        compiler_params=params(),
        cost_estimate=cost(8),
    )(gres, mod, w_out, attended_t)


def qkv_weight_kernel(per, nt_ref, q_ref, k_ref, v_ref, g0, g1):
    step = pl.program_id(0)
    half = g0.shape[0]
    for part, ref in enumerate((q_ref, k_ref, v_ref)):

        @pl.when(step // per == part)
        def _(ref=ref):
            g0[...] = dot_nn(nt_ref[:half], ref[...]).astype(bf16)
            g1[...] = dot_nn(nt_ref[half:], ref[...]).astype(bf16)


def qkv_weight(normed_t, dq, dk, dv):
    features, rows = normed_t.shape
    wide = dq.shape[1]
    per = wide // UNIT

    def col(part):
        return pl.BlockSpec((rows, UNIT), lambda i: (0, jnp.clip(i - part * per, 0, per - 1)))

    out_spec = pl.BlockSpec((features // 2, UNIT), lambda i: (0, i))
    grad = jax.ShapeDtypeStruct((features // 2, 3 * wide), bf16)
    return pl.pallas_call(
        functools.partial(qkv_weight_kernel, per),
        grid=(3 * per,),
        in_specs=[whole(normed_t.shape), col(0), col(1), col(2)],
        out_specs=[out_spec, out_spec],
        out_shape=[grad, grad],
        name="qkv_weight",
        compiler_params=params(),
        cost_estimate=cost(5),
    )(normed_t, dq, dk, dv)


def qkv_back_kernel(src_ref, *refs):
    count = (len(refs) - 8) // 3
    grads = refs[: 3 * count]
    w_ref, x_ref, gres_ref, mod_ref, out_ref, vec_ref, stage_ref, sem_ref = refs[3 * count :]
    step = pl.program_id(0)
    block = x_ref.shape[0]
    features = x_ref.shape[1]
    back = None
    bias = []
    for part in range(3):
        pieces = [grads[part * count + k][...] for k in range(count)]
        joined = jnp.concatenate(pieces, axis=1)
        bias.append(jnp.sum(joined.astype(f32), axis=0, keepdims=True))
        got = dot_nt(joined, w_ref[:, part * features : (part + 1) * features])
        back = got if back is None else back + got
    back = back.astype(bf16).astype(f32)
    hat_rows, inv_std = hat_of(x_ref[...].astype(f32))
    grad = gres_ref[...].astype(f32) + norm_back(back * (1.0 + mod_ref[1:2, :]), hat_rows, inv_std)
    stage_ref[pl.ds(pl.multiple_of(step * block, block), block)] = grad.astype(bf16)
    for t in range(4):
        pltpu.make_async_copy(
            stage_ref.at[pl.ds(pl.multiple_of(step * block + t * PIECE, PIECE), PIECE)],
            out_ref.at[src_ref[4 * step + t]],
            sem_ref.at[4 * step + t],
        ).start()
    pieces = jnp.concatenate(
        [
            jnp.sum(back, axis=0, keepdims=True),
            jnp.sum(back * hat_rows, axis=0, keepdims=True),
            bias[0],
            bias[2],
            jnp.zeros((4, features), f32),
        ],
        axis=0,
    )

    @pl.when(step == 0)
    def _():
        vec_ref[...] = pieces

    @pl.when(step > 0)
    def _():
        vec_ref[...] += pieces

    @pl.when(step == pl.num_programs(0) - 1)
    def _():
        for k in range(sem_ref.shape[0]):
            pltpu.make_async_copy(
                stage_ref.at[pl.ds(k * PIECE, PIECE)], out_ref.at[src_ref[k]], sem_ref.at[k]
            ).wait()


def qkv_backward(src, grads, w_qkv, x_rows, gres, mod):
    rows, features = x_rows.shape
    block = 4 * PIECE
    rows_spec = pl.BlockSpec((block, features), lambda i, src: (i, 0))
    grad_specs = [
        pl.BlockSpec((block, g.shape[1]), lambda i, src: (i, 0)) for part in grads for g in part
    ]
    flat = [g for part in grads for g in part]
    return pl.pallas_call(
        qkv_back_kernel,
        grid_spec=pltpu.PrefetchScalarGridSpec(
            num_scalar_prefetch=1,
            grid=(rows // block,),
            in_specs=grad_specs + [whole(w_qkv.shape), rows_spec, rows_spec, whole(mod.shape)],
            out_specs=[
                pl.BlockSpec(memory_space=pl.ANY),
                pl.BlockSpec((8, features), lambda i, src: (0, 0)),
            ],
            scratch_shapes=[
                pltpu.VMEM((rows, features), bf16),
                pltpu.SemaphoreType.DMA((rows // PIECE,)),
            ],
        ),
        out_shape=[
            jax.ShapeDtypeStruct((rows // PIECE, PIECE, features), bf16),
            jax.ShapeDtypeStruct((8, features), f32),
        ],
        name="qkv_backward",
        compiler_params=params(),
        cost_estimate=cost(12),
    )(src, *flat, w_qkv, x_rows, gres, mod)


def flip(axis, bit):
    size = lax.axis_size(axis)
    return [(i, i ^ (1 << bit)) for i in range(size)]


def trade(array, axis, bit):
    return lax.ppermute(array, axis, flip(axis, bit))


def add_low(a, b):
    return (a.astype(f32) + b.astype(f32)).astype(bf16)


def reduce_relative(own, partner, clip_bits):
    got = trade(partner, "win", 0)
    half = own.shape[0] // 2
    for bit in range(clip_bits):
        keep = add_low(own[:half], got[:half])
        send = add_low(own[half:], got[half:])
        got = trade(send, "clip", bit)
        own = keep
        half //= 2
    own = add_low(own, got)
    got = trade(own, "win", 1)
    own = lax.reduce_precision(own.astype(f32) + got.astype(f32), 8, 7).astype(bf16)
    own = lax.optimization_barrier(own)
    other = trade(own, "win", 0)
    return own[0], other[0]


def ordered(core, own, other, axis):
    first = jnp.where(core == 0, own, other)
    second = jnp.where(core == 0, other, own)
    return jnp.stack([first, second], axis=axis).astype(f32)


def sum_over_win(vector):
    bits = lax.axis_size("win").bit_length() - 1
    for bit in range(bits):
        vector = vector + trade(vector, "win", bit)
    return vector


def gather_clip(vector):
    bits = lax.axis_size("clip").bit_length() - 1
    me = lax.axis_index("clip")
    rows = vector[None]
    for bit in range(bits):
        got = trade(rows, "clip", bit)
        upper = (me >> bit) & 1 == 1
        rows = jnp.where(upper, jnp.concatenate([got, rows]), jnp.concatenate([rows, got]))
    return rows


def to_quadrants(slot_rows):
    local_slots = slot_rows.shape[0]
    channels = slot_rows.shape[-1]
    arranged = slot_rows.reshape(local_slots, 2, WST, 2, WST, channels).transpose(1, 3, 0, 2, 4, 5)
    return arranged.reshape(4, local_slots, PIECE, channels)


def from_quadrants(received):
    local_slots = received.shape[1]
    channels = received.shape[-1]
    arranged = received.reshape(2, 2, local_slots, WST, WST, channels).transpose(2, 0, 3, 1, 4, 5)
    return arranged.reshape(local_slots, 4 * PIECE, channels)


def exchange(quadrants):
    return lax.all_to_all(quadrants, "win", split_axis=0, concat_axis=0, tiled=True)


def local(
    tokens,
    condition,
    slot_order,
    rel_index,
    w_qkv,
    b_query,
    b_value,
    w_out,
    b_out,
    w_up,
    b_up,
    w_down,
    b_down,
    w_ada,
    b_ada,
    rel_table,
    grad_out,
):
    features = tokens.shape[-1]
    clips = lax.axis_size("clip")
    clip_bits = clips.bit_length() - 1
    me = lax.axis_index("clip")
    core = lax.axis_index("win") & 1
    ff = w_up.shape[1]
    fast = features // clips == LANES and ff // clips == 2 * UNIT

    pieces = exchange(to_quadrants(tokens[0])).reshape(-1, PIECE, features)
    grad_pieces = exchange(to_quadrants(grad_out[0])).reshape(-1, PIECE, features)
    slots = pieces.shape[0]
    per_frame = slots // FRAMES
    order_row = slot_order[0]
    window_place = jnp.arange(slots, dtype=jnp.int32)
    wanted = (window_place % FRAMES) * per_frame + window_place // FRAMES
    src = jnp.sum(
        jnp.where(order_row[None, :] == wanted[:, None], window_place[None, :], 0), axis=1
    ).astype(jnp.int32)
    windows = per_frame
    win = FRAMES * PIECE

    half = win // 2
    idx_mine = lax.dynamic_slice_in_dim(rel_index, core * half, half, 0)
    bias_mine = bias_gather(idx_mine, rel_table)
    bias_other = trade(bias_mine, "win", 0)

    lifted = jax.nn.silu(condition.astype(f32)).astype(bf16)
    modulation = jnp.dot(lifted, w_ada, preferred_element_type=f32)[0] + b_ada
    mod = jnp.concatenate([modulation.reshape(6, features), jnp.zeros((2, features), f32)])

    qkv_bias = jnp.concatenate([b_query, jnp.zeros_like(b_query), b_value]).astype(f32)[None]
    x_rows, normed, qkv = qkv_call(src, pieces, mod, qkv_bias, w_qkv)
    core_arr = core.astype(jnp.int32)[None]
    attended, probs, recips = attn_forward(core_arr, qkv, bias_mine, bias_other, windows)
    branch, normed_two, grad_mixed = out_call(
        src, grad_pieces, attended, x_rows, mod, b_out.astype(f32)[None], w_out
    )

    places = jnp.arange(clips, dtype=jnp.int32)
    units = ff // (2 * UNIT)
    unit_places = jnp.arange(units, dtype=jnp.int32)
    identity = jnp.arange(features // LANES, dtype=jnp.int32)
    if fast:
        reverse = jnp.zeros_like(places)
        for bit in range(clip_bits):
            reverse = reverse | (((places >> (clip_bits - 1 - bit)) & 1) << bit)
        relative = me ^ reverse
        fo_first, fo_second = 2 * relative, 2 * relative + 1
        co_first = co_second = relative
        turn_rel = functools.partial(turn, relative, core_arr)
        turn_abs = functools.partial(turn, identity, core_arr)
    else:
        fo_first, fo_second = unit_places, unit_places + units
        co_first = co_second = unit_places
        turn_rel = turn_abs = lambda rows: rows.T
    normed_t = turn_rel(normed)
    attended_t = turn_rel(attended)
    normed_two_t = turn_rel(normed_two)
    grad_mixed_t = turn_abs(grad_mixed)
    b_up_rows = b_up.astype(f32).reshape(-1, 1, UNIT)
    up_a0, up_a1, down_a0, down_a1, bsum_a, part_mixed, part_back = ff_first(
        fo_first, co_first, normed_two, grad_mixed, normed_two_t, grad_mixed_t, w_up, b_up_rows, w_down
    )
    up_b0, up_b1, down_b0, down_b1, bsum_b, gres, early, out_pieces = ff_second(
        fo_second, co_second, src, normed_two, grad_mixed, normed_two_t, grad_mixed_t,
        w_up, b_up_rows, w_down, grad_pieces, x_rows, branch, part_mixed, part_back,
        mod, b_down.astype(f32)[None],
    )
    local_slots = tokens.shape[1]
    piece_shape = (-1, local_slots, PIECE, features)
    block_out = from_quadrants(exchange(out_pieces.reshape(piece_shape))).reshape(tokens.shape)

    grad_att, out_g0, out_g1 = out_backward(gres, mod, w_out, attended_t)
    pairs = probs.shape[0]
    dq_a, dk_a, dv_a, ss_a = attn_backward(qkv, attended, grad_att, probs, recips, windows, 0, pairs // 2)
    qkv_a0, qkv_a1 = qkv_weight(normed_t, dq_a, dk_a, dv_a)
    dq_b, dk_b, dv_b, ss_b = attn_backward(
        qkv, attended, grad_att, probs, recips, windows, pairs // 2, pairs // 2
    )
    qkv_b0, qkv_b1 = qkv_weight(normed_t, dq_b, dk_b, dv_b)
    token_pieces, late = qkv_backward(
        src, ((dq_a, dq_b), (dk_a, dk_b), (dv_a, dv_b)), w_qkv, x_rows, gres, mod
    )
    grad_tokens = from_quadrants(exchange(token_pieces.reshape(piece_shape))).reshape(tokens.shape)

    scores = jnp.concatenate([ss_a, ss_b], axis=0)
    send_scores = lax.dynamic_slice_in_dim(scores, (1 - core) * half, half, 1)
    keep_scores = lax.dynamic_slice_in_dim(scores, core * half, half, 1)
    keep_scores = keep_scores + trade(send_scores, "win", 0)
    buckets = rel_table.shape[0]
    rel_sums = sum_over_win(bucket_sums(idx_mine, keep_scores, buckets))
    heads = rel_sums.shape[1]
    rel_rows = buckets // clips
    rel_sums = rel_sums.transpose(0, 2, 1).reshape(clips, rel_rows, heads)
    for bit in reversed(range(clip_bits)):
        side = (me >> bit) & 1
        parts = rel_sums.reshape(2, -1, rel_rows, heads)
        keep = lax.dynamic_index_in_dim(parts, side, 0, keepdims=False)
        send = lax.dynamic_index_in_dim(parts, 1 - side, 0, keepdims=False)
        rel_sums = keep + trade(send, "clip", bit)
    sum_rel = rel_sums[0]

    grad_b_up = jnp.stack([bsum_a.reshape(-1, UNIT), bsum_b.reshape(-1, UNIT)], axis=1 if fast else 0).reshape(-1)
    early_vec = sum_over_win(jnp.concatenate([early[:6].reshape(-1), grad_b_up]))
    late_vec = sum_over_win(late[:4].reshape(-1))
    early_all = gather_clip(jnp.concatenate([early_vec, lifted[0].astype(f32)]))
    late_all = gather_clip(late_vec)
    d = features
    all_terms = jnp.concatenate([late_all[:, : 2 * d], early_all[:, : 4 * d]], axis=1)
    all_lifted = early_all[:, 6 * d + ff :]

    def own_block(vector):
        size = vector.shape[0] // clips
        return lax.dynamic_slice_in_dim(vector, me * size, size, 0)

    early_sum = jnp.sum(early_all[:, 4 * d : 6 * d + ff], axis=0)
    late_sum = jnp.sum(late_all[:, 2 * d :], axis=0)
    sum_bo, sum_bd, sum_bu = own_block(early_sum[:d]), own_block(early_sum[d : 2 * d]), own_block(early_sum[2 * d :])
    sum_bq, sum_bv = own_block(late_sum[:d]), own_block(late_sum[d:])
    ada_rows = d // clips
    lifted_rows = lax.dynamic_slice_in_dim(all_lifted, me * ada_rows, ada_rows, 1)
    grad_w_ada = jnp.dot(lifted_rows.T, all_terms, precision=lax.Precision.HIGHEST)
    grad_b_ada = own_block(jnp.sum(all_terms, axis=0))

    if fast:

        def rows_of(a, b):
            shape = (clips, d // clips // 2, -1)
            own, other = reduce_relative(a.reshape(shape), b.reshape(shape), clip_bits)
            return ordered(core, own, other, 0).reshape(d // clips, -1)

        def turned(a, b):
            own, other = reduce_relative(a, b, clip_bits)
            both = ordered(core, own.reshape(d // LANES, LANES // 2, UNIT), other.reshape(d // LANES, LANES // 2, UNIT), 1)
            return both.reshape(d, UNIT).T

        up_a = rows_of(up_a0, up_a1)
        down_a = turned(down_a0, down_a1)
        up_b = rows_of(up_b0, up_b1)
        down_b = turned(down_b0, down_b1)
        sum_wo = rows_of(out_g0, out_g1)
        qkv_a = rows_of(qkv_a0, qkv_a1)
        qkv_b = rows_of(qkv_b0, qkv_b1)
        rows = d // clips
        sum_wu = jnp.stack([up_a.reshape(rows, -1, UNIT), up_b.reshape(rows, -1, UNIT)], axis=2).reshape(rows, ff)
        sum_wd = jnp.concatenate([down_a, down_b], axis=0)
        sum_qkv = jnp.stack(
            [qkv_a.reshape(rows, 3, d // 2), qkv_b.reshape(rows, 3, d // 2)], axis=2
        ).reshape(rows, 3 * d)
    else:

        def share(whole_grad):
            part = lax.psum_scatter(whole_grad.astype(f32), "clip", scatter_dimension=0, tiled=True)
            return lax.psum(part, "win")

        def natural(a, b):
            return jnp.concatenate([a, b], axis=0)

        def down_natural(a, b):
            return jnp.concatenate([a, b], axis=1).transpose(0, 2, 1).reshape(-1, d)

        sum_wu = share(jnp.concatenate([natural(up_a0, up_a1), natural(up_b0, up_b1)], axis=1))
        sum_wd = share(jnp.concatenate([down_natural(down_a0, down_a1), down_natural(down_b0, down_b1)], axis=0))
        sum_wo = share(natural(out_g0, out_g1))
        qkv_a = natural(qkv_a0, qkv_a1).reshape(d, 3, d // 2)
        qkv_b = natural(qkv_b0, qkv_b1).reshape(d, 3, d // 2)
        sum_qkv = share(jnp.stack([qkv_a, qkv_b], axis=2).reshape(d, 3 * d))
    return (
        block_out,
        grad_tokens,
        sum_qkv,
        sum_bq,
        sum_bv,
        sum_wo,
        sum_bo,
        sum_wu,
        sum_bu,
        sum_wd,
        sum_bd,
        grad_w_ada,
        grad_b_ada,
        sum_rel,
    )


def solution(mesh):
    placed = (
        P("clip", "win", None, None),
        P("clip", None),
        P("clip", None),
    ) + (P(),) * 13 + (P("clip", "win", None, None),)
    return jax.shard_map(
        local,
        mesh=mesh,
        in_specs=placed,
        out_specs=(
            P("clip", "win", None, None),
            P("clip", "win", None, None),
            P("clip", None),
            P("clip"),
            P("clip"),
            P("clip", None),
            P("clip"),
            P("clip", None),
            P("clip"),
            P("clip", None),
            P("clip"),
            P("clip", None),
            P("clip"),
            P("clip", None),
        ),
        check_vma=False,
    )
```

```python
import functools
import math

import jax
import jax.numpy as jnp
from jax import lax
from jax.experimental import pallas as pl
from jax.experimental.pallas import tpu as pltpu
from jax.sharding import PartitionSpec as P

HEAD = 64
FRAMES = 5
WST = 8
PIECE = WST * WST
UNIT = 256
FF_PARTS = 4
FF_UNITS = 4
FF_BLOCKS = 2
FIRST_PAIRS = 6
LANES = 128
VMEM_LIMIT = 60 * 1024 * 1024
f32 = jnp.float32
bf16 = jnp.bfloat16
GELU_C = math.sqrt(2.0 / math.pi)
GELU_A = 0.044715


def dot_nn(a, b):
    return jnp.dot(a, b, preferred_element_type=f32)


def dot_nt(a, b):
    return lax.dot_general(a, b, (((1,), (1,)), ((), ())), preferred_element_type=f32)


def dot_tn(a, b):
    return lax.dot_general(a, b, (((0,), (0,)), ((), ())), preferred_element_type=f32)


def params():
    return pltpu.CompilerParams(vmem_limit_bytes=VMEM_LIMIT)


def cost(micros):
    return pl.CostEstimate(
        flops=int(micros * 5.0e7), bytes_accessed=int(micros * 1.0e5), transcendentals=0
    )


def pick(swap, first, second):
    return jnp.where(swap, second, first), jnp.where(swap, first, second)


def hat_of(rows):
    average = jnp.mean(rows, axis=-1, keepdims=True)
    centered = rows - average
    variance = jnp.mean(centered * centered, axis=-1, keepdims=True)
    inv_std = lax.rsqrt(variance + 1e-06)
    return centered * inv_std, inv_std


def norm_back(grad_hat, hat_rows, inv_std):
    first_mean = jnp.mean(grad_hat, axis=-1, keepdims=True)
    second_mean = jnp.mean(grad_hat * hat_rows, axis=-1, keepdims=True)
    return inv_std * (grad_hat - first_mean - hat_rows * second_mean)


def whole(shape):
    zeros = (0,) * len(shape)
    return pl.BlockSpec(shape, lambda *unused: zeros, pipeline_mode=pl.Buffered(1))


def bias_kernel(idx_ref, tab_ref, out_ref, scr_ref):
    lows = lax.broadcasted_iota(jnp.int32, (256, idx_ref.shape[1]), 0)
    tab = tab_ref[...]
    half = tab.shape[0] // 2
    heads = 16
    tiles = idx_ref.shape[1] // LANES
    win = out_ref.shape[2] // 2
    for i in range(8):
        idx = idx_ref[pl.ds(i, 1), :]
        low = idx & 255
        high = idx >> 8
        onehot = jnp.where(lows == low, 1.0, 0.0).astype(bf16)
        got = dot_nn(tab, onehot)
        got = got[:half] + got[half:]
        acc = got[:heads]
        for c in range(1, half // heads):
            acc = jnp.where(high == c, got[c * heads : (c + 1) * heads], acc)
        for t in range(tiles):
            scr_ref[t, pl.ds(i, heads, stride=8), :] = acc[:, t * LANES : (t + 1) * LANES]
    for pair in range(heads // 2):
        rows = []
        for h in range(2):
            at = (2 * pair + h) * 8
            rows.append(
                jnp.concatenate([scr_ref[t, at : at + 8, :] for t in range(tiles)], axis=1)[:, :win]
            )
        out_ref[pair] = jnp.concatenate(rows, axis=1)


def bias_gather(idx, table):
    rows, win = idx.shape
    padded = -(-win // LANES) * LANES
    buckets, heads = table.shape
    upper_f = lax.reduce_precision(table, 8, 7)
    lower = (table - upper_f).astype(bf16)

    def arrange(t):
        return t.reshape(-1, 256, heads).transpose(0, 2, 1).reshape(-1, 256)

    tab = jnp.concatenate([arrange(upper_f.astype(bf16)), arrange(lower)], axis=0)
    idx = jnp.pad(idx, ((0, 0), (0, padded - win)))
    return pl.pallas_call(
        bias_kernel,
        grid=(rows // 8,),
        in_specs=[pl.BlockSpec((8, padded), lambda i: (i, 0)), whole(tab.shape)],
        out_specs=pl.BlockSpec((heads // 2, 8, 2 * win), lambda i: (0, i, 0)),
        out_shape=jax.ShapeDtypeStruct((heads // 2, rows, 2 * win), f32),
        scratch_shapes=[pltpu.VMEM((padded // LANES, 8 * heads, LANES), f32)],
        name="bias_gather",
        compiler_params=params(),
        cost_estimate=cost(18),
    )(idx, tab)


def bucket_kernel(inv_ref, idx_ref, *refs):
    out_ref, acc_ref, scr_ref = refs[-3:]
    keep_refs = refs[: (len(refs) - 3) // 2]
    got_refs = refs[(len(refs) - 3) // 2 : -3]

    @pl.when(pl.program_id(0) == 0)
    def _():
        acc_ref[...] = jnp.zeros_like(acc_ref)

    padded = idx_ref.shape[1]
    tiles = padded // LANES
    keeps = [(r, k) for r in keep_refs for k in range(r.shape[0])]
    gots = [(r, k) for r in got_refs for k in range(r.shape[0])]
    pairs = len(keeps)
    heads = 2 * pairs
    win = keep_refs[0].shape[2] // 2
    step_rows = idx_ref.shape[0]
    lows = lax.broadcasted_iota(jnp.int32, (256, padded), 0)
    zero = jnp.zeros((step_rows, padded - win), f32)
    for pair in range(pairs):
        (keep_ref, k), (got_ref, unused) = keeps[pair], gots[pair]
        sums = keep_ref[k].astype(f32) + got_ref[k].astype(f32)
        for h in range(2):
            part = jnp.concatenate([sums[:, h * win : (h + 1) * win], zero], axis=1)
            at = (2 * pair + h) * step_rows
            for t in range(tiles):
                scr_ref[t, at : at + step_rows, :] = part[:, t * LANES : (t + 1) * LANES]
    total = acc_ref[...]
    for i in range(step_rows):
        idx = idx_ref[pl.ds(i, 1), :]
        low = idx & 255
        high = idx >> 8
        onehot = jnp.where(lows == low, 1.0, 0.0).astype(bf16)
        sums = jnp.concatenate(
            [scr_ref[t, pl.ds(i, heads, stride=step_rows), :] for t in range(tiles)], axis=1
        )
        spread = jnp.concatenate(
            [jnp.where(high == c, sums, 0.0) for c in range(acc_ref.shape[0] // heads)], axis=0
        )
        total += dot_nt(spread.astype(bf16), onehot)
    acc_ref[...] = total

    @pl.when(pl.program_id(0) == pl.num_programs(0) - 1)
    def _():
        for k in range(out_ref.shape[0]):
            out_ref[inv_ref[k]] = total[k * heads : (k + 1) * heads]


def bucket_sums(inv, idx, keeps, gots, buckets):
    rows, win = idx.shape
    padded = -(-win // LANES) * LANES
    heads = 2 * sum(k.shape[0] for k in keeps)
    step_rows = 16
    idx = jnp.pad(idx, ((0, 0), (0, padded - win)))
    out_rows = buckets // 256
    sum_specs = [
        pl.BlockSpec((k.shape[0], step_rows, 2 * win), lambda i, inv: (0, i, 0)) for k in keeps
    ]
    return pl.pallas_call(
        bucket_kernel,
        grid_spec=pltpu.PrefetchScalarGridSpec(
            num_scalar_prefetch=1,
            grid=(rows // step_rows,),
            in_specs=[pl.BlockSpec((step_rows, padded), lambda i, inv: (i, 0))] + sum_specs + sum_specs,
            out_specs=pl.BlockSpec((out_rows, heads, 256), lambda i, inv: (0, 0, 0)),
            scratch_shapes=[
                pltpu.VMEM((out_rows * heads, 256), f32),
                pltpu.VMEM((padded // LANES, step_rows * heads, LANES), f32),
            ],
        ),
        out_shape=jax.ShapeDtypeStruct((out_rows, heads, 256), f32),
        name="bucket_sums",
        compiler_params=params(),
        cost_estimate=cost(14),
    )(inv, idx, *keeps, *gots)


def qkv_kernel(src_ref, a_ref, b_ref, c_ref, d_ref, mod_ref, bias_ref, w_ref, x_ref, n_ref, o_ref):
    rows = jnp.concatenate([r[0] for r in (a_ref, b_ref, c_ref, d_ref)], axis=0)
    x_ref[...] = rows
    hat_rows, unused = hat_of(rows.astype(f32))
    normed = (hat_rows * (1.0 + mod_ref[1:2, :]) + mod_ref[0:1, :]).astype(bf16)
    n_ref[...] = normed
    features = rows.shape[1]
    for j in range(w_ref.shape[1] // 512):
        cols = slice(j * 512, (j + 1) * 512)
        got = dot_nn(normed, w_ref[:, cols]) + bias_ref[0:1, cols]
        if (j + 1) * 512 <= features:
            got = got.astype(bf16).astype(f32) * (1.0 / math.sqrt(HEAD))
        o_ref[:, cols] = got.astype(bf16)


def slot_spec(features, t):
    return pl.BlockSpec((1, PIECE, features), lambda i, src, t=t: (src[4 * i + t], 0, 0))


def qkv_call(src, pieces, mod, qkv_bias, w_qkv):
    count, unused, features = pieces.shape
    rows = count * PIECE
    wide = w_qkv.shape[1]
    block = 4 * PIECE
    return pl.pallas_call(
        qkv_kernel,
        grid_spec=pltpu.PrefetchScalarGridSpec(
            num_scalar_prefetch=1,
            grid=(count // 4,),
            in_specs=[slot_spec(features, t) for t in range(4)]
            + [whole(mod.shape), whole(qkv_bias.shape), whole(w_qkv.shape)],
            out_specs=[
                pl.BlockSpec((block, features), lambda i, src: (i, 0)),
                pl.BlockSpec((block, features), lambda i, src: (i, 0)),
                pl.BlockSpec((block, wide), lambda i, src: (i, 0)),
            ],
        ),
        out_shape=[
            jax.ShapeDtypeStruct((rows, features), bf16),
            jax.ShapeDtypeStruct((rows, features), bf16),
            jax.ShapeDtypeStruct((rows, wide), bf16),
        ],
        name="norm_qkv",
        compiler_params=params(),
        cost_estimate=cost(12),
    )(src, pieces, pieces, pieces, pieces, mod, qkv_bias, w_qkv)


def split_pair(x, left):
    zero = jnp.zeros_like(x)
    return jnp.concatenate([jnp.where(left, x, zero), jnp.where(left, zero, x)], axis=0)


def values_ones(v, left):
    one = jnp.ones_like(v)
    zero = jnp.zeros_like(v)
    marks = jnp.concatenate([jnp.where(left, one, zero), jnp.where(left, zero, one)], axis=0)
    return jnp.concatenate([split_pair(v, left), marks], axis=1)


def attn_kernel(windows, core_ref, q_ref, k_ref, v_ref, mine_ref, other_ref, o_ref, p_ref, r_ref, b_ref):
    win = q_ref.shape[0] // windows
    half = win // 2
    left = lax.broadcasted_iota(jnp.int32, (win, LANES), 1) < HEAD
    first = core_ref[0] == 0
    b_ref[:half] = jnp.where(first, mine_ref[0], other_ref[0])
    b_ref[half:] = jnp.where(first, other_ref[0], mine_ref[0])
    lowest = jnp.float32(-jnp.inf)
    whole_tiles = win // LANES * LANES
    for u in range(windows):
        rows = slice(u * win, (u + 1) * win)
        keys = split_pair(k_ref[rows], left)
        vals = values_ones(v_ref[rows], left)
        s = dot_nt(q_ref[rows], keys) + b_ref[...]
        lo = s[:, :whole_tiles]
        mid = s[:, whole_tiles : whole_tiles + LANES]
        hi = s[:, whole_tiles + LANES :]
        top_lo = jnp.where(left, mid, lowest)
        top_hi = jnp.where(left, lowest, mid)
        for t in range(whole_tiles // LANES):
            cols = slice(t * LANES, (t + 1) * LANES)
            top_lo = jnp.maximum(top_lo, lo[:, cols])
            top_hi = jnp.maximum(top_hi, hi[:, cols])
        top_lo = jnp.max(top_lo, axis=1, keepdims=True)
        top_hi = jnp.max(top_hi, axis=1, keepdims=True)
        e = jnp.concatenate(
            [
                jnp.exp(lo - top_lo),
                jnp.exp(mid - jnp.where(left, top_lo, top_hi)),
                jnp.exp(hi - top_hi),
            ],
            axis=1,
        ).astype(bf16)
        p_ref[0, u] = e
        got = dot_nn(e, vals)
        r = 1.0 / got[:, LANES:]
        r_ref[rows] = r
        o_ref[rows] = (got[:, :LANES] * r).astype(bf16)


def attn_forward(core, qkv, bias_mine, bias_other, windows):
    rows = qkv.shape[0]
    win = rows // windows
    pairs = bias_mine.shape[0]
    features = qkv.shape[1] // 3

    def col(part):
        return pl.BlockSpec((rows, LANES), lambda h, c, part=part: (0, part * pairs + h))

    half_spec = pl.BlockSpec((1, win // 2, 2 * win), lambda h, c: (h, 0, 0))
    return pl.pallas_call(
        functools.partial(attn_kernel, windows),
        grid_spec=pltpu.PrefetchScalarGridSpec(
            num_scalar_prefetch=1,
            grid=(pairs,),
            in_specs=[col(0), col(1), col(2), half_spec, half_spec],
            out_specs=[
                col(0),
                pl.BlockSpec((1, windows, win, 2 * win), lambda h, c: (h, 0, 0, 0)),
                col(0),
            ],
            scratch_shapes=[pltpu.VMEM((win, 2 * win), f32)],
        ),
        out_shape=[
            jax.ShapeDtypeStruct((rows, features), bf16),
            jax.ShapeDtypeStruct((pairs, windows, win, 2 * win), bf16),
            jax.ShapeDtypeStruct((rows, features), f32),
        ],
        name="attn_forward",
        compiler_params=params(),
        cost_estimate=cost(18),
    )(core, qkv, qkv, qkv, bias_mine, bias_other)


def fold_delta(dx, lane):
    lower_half = (lane & 32) == 0
    dx = dx + jnp.where(lower_half, pltpu.roll(dx, LANES - 32, 1), pltpu.roll(dx, 32, 1))
    upper = dx.astype(bf16)
    lower = (dx - upper.astype(f32)).astype(bf16)
    return jnp.where(lower_half, upper, lower)


def attn_back_kernel(windows, core_ref, q_ref, k_ref, v_ref, o_ref, do_ref, p_ref, r_ref, g_ref, mine_ref, other_ref):
    win = q_ref.shape[0] // windows
    lane = lax.broadcasted_iota(jnp.int32, (win, LANES), 1)
    left = lane < HEAD
    sums = None
    for u in range(windows):
        rows = slice(u * win, (u + 1) * win)
        keys = split_pair(k_ref[rows], left)
        vals = values_ones(v_ref[rows], left)
        up = (do_ref[rows].astype(f32) * r_ref[rows]).astype(bf16)
        delta = fold_delta(-(up.astype(f32) * o_ref[rows].astype(f32)), lane)
        d = dot_nt(jnp.concatenate([up, delta], axis=1), vals)
        p = p_ref[0, u]
        ds = p.astype(f32) * d
        sums = ds if sums is None else sums + ds
        low = ds.astype(bf16)
        g_ref[0, rows] = (dot_nn(low, keys) * (1.0 / math.sqrt(HEAD))).astype(bf16)
        dk = dot_tn(low, q_ref[rows])
        g_ref[1, rows] = jnp.where(left, dk[:win], dk[win:]).astype(bf16)
        dv = dot_tn(p, up)
        g_ref[2, rows] = jnp.where(left, dv[:win], dv[win:]).astype(bf16)
    half = win // 2
    first, second = sums[:half].astype(bf16), sums[half:].astype(bf16)
    mine_ref[0], other_ref[0] = pick(core_ref[0] == 1, first, second)


def attn_backward(core, qkv, attended, grad_att, probs, recips, windows, first, count):
    rows = qkv.shape[0]
    win = rows // windows
    pairs = probs.shape[0]

    def col(part):
        return pl.BlockSpec((rows, LANES), lambda h, core, part=part: (0, part * pairs + first + h))

    half_spec = pl.BlockSpec((1, win // 2, 2 * win), lambda h, core: (h, 0, 0))
    half_shape = jax.ShapeDtypeStruct((count, win // 2, 2 * win), bf16)
    return pl.pallas_call(
        functools.partial(attn_back_kernel, windows),
        grid_spec=pltpu.PrefetchScalarGridSpec(
            num_scalar_prefetch=1,
            grid=(count,),
            in_specs=[
                col(0),
                col(1),
                col(2),
                col(0),
                col(0),
                pl.BlockSpec((1, windows, win, 2 * win), lambda h, core: (first + h, 0, 0, 0)),
                col(0),
            ],
            out_specs=[
                pl.BlockSpec((3, rows, LANES), lambda h, core: (0, 0, h)),
                half_spec,
                half_spec,
            ],
        ),
        out_shape=[jax.ShapeDtypeStruct((3, rows, count * LANES), bf16), half_shape, half_shape],
        name="attn_backward",
        compiler_params=params(),
        cost_estimate=cost(3 * count),
    )(core, qkv, qkv, qkv, attended, grad_att, probs, recips)


def out_kernel(src_ref, a_ref, b_ref, c_ref, d_ref, att_ref, x_ref, mod_ref, bo_ref, w_ref, branch_ref, n_ref, gm_ref):
    branch = (dot_nn(att_ref[...], w_ref[...]) + bo_ref[...]).astype(bf16)
    branch_ref[...] = branch
    residual = x_ref[...].astype(f32) + mod_ref[2:3, :] * branch.astype(f32)
    hat_rows, unused = hat_of(residual)
    n_ref[...] = (hat_rows * (1.0 + mod_ref[4:5, :]) + mod_ref[3:4, :]).astype(bf16)
    up = jnp.concatenate([r[0] for r in (a_ref, b_ref, c_ref, d_ref)], axis=0)
    gm_ref[...] = (mod_ref[5:6, :] * up.astype(f32)).astype(bf16)


def out_call(src, pieces, attended, x_rows, mod, b_out, w_out):
    count, unused, features = pieces.shape
    rows = count * PIECE
    block = 4 * PIECE
    rows_spec = pl.BlockSpec((block, features), lambda i, src: (i, 0))
    sds = jax.ShapeDtypeStruct((rows, features), bf16)
    return pl.pallas_call(
        out_kernel,
        grid_spec=pltpu.PrefetchScalarGridSpec(
            num_scalar_prefetch=1,
            grid=(count // 4,),
            in_specs=[slot_spec(features, t) for t in range(4)]
            + [rows_spec, rows_spec, whole(mod.shape), whole(b_out.shape), whole(w_out.shape)],
            out_specs=[rows_spec, rows_spec, rows_spec],
        ),
        out_shape=[sds, sds, sds],
        name="out_norm",
        compiler_params=params(),
        cost_estimate=cost(6),
    )(src, pieces, pieces, pieces, pieces, attended, x_rows, mod, b_out, w_out)


def place_rows(inv_ref, out_ref, values):
    for k in range(out_ref.shape[0]):
        at = inv_ref[k]
        for m in range(out_ref.shape[1]):
            out_ref[at, m] = values[k * LANES : (k + 1) * LANES, m * LANES : (m + 1) * LANES]


def ff_part_kernel(count, fo_ref, co_ref, inv_ref, flag_ref, n_ref, gm_ref, *refs):
    ups = refs[:count]
    biases = refs[count : 2 * count]
    downs = refs[2 * count : 3 * count]
    act_ref, gh_ref, own_ref, other_ref, sum_ref = refs[-5:]
    step = pl.program_id(0)
    rows = n_ref.shape[0]
    block = rows // FF_BLOCKS
    wu = jnp.concatenate([r[...] for r in ups], axis=1)
    wd = jnp.concatenate([r[...] for r in downs], axis=0)
    bias = jnp.concatenate([r[0] for r in biases], axis=1)
    sums = None
    for c in range(FF_BLOCKS):
        part = slice(c * block, (c + 1) * block)
        v = dot_nn(n_ref[part], wu) + bias
        v2 = v * v
        t = jnp.tanh(v * (GELU_C + (GELU_C * GELU_A) * v2))
        h = 0.5 + 0.5 * t
        slope = h + (0.5 * v) * (1.0 - t * t) * (GELU_C + (3.0 * GELU_C * GELU_A) * v2)
        gh = (dot_nt(gm_ref[part], wd) * slope).astype(bf16)
        act_ref[0, part] = (v * h).astype(bf16)
        gh_ref[0, part] = gh
        piece = jnp.sum(gh.astype(f32), axis=0, keepdims=True)
        sums = piece if sums is None else sums + piece
    sum_ref[0] = sums
    up = dot_tn(n_ref[...], gh_ref[0]).astype(bf16)
    down = dot_tn(act_ref[0], gm_ref[...]).astype(bf16)
    half = down.shape[1] // 2
    blocks = half // LANES
    for p in range(count // 2):
        left = up[:, 2 * p * LANES : (2 * p + 1) * LANES]
        right = up[:, (2 * p + 1) * LANES : (2 * p + 2) * LANES]
        own, other = pick(flag_ref[1] == 1, left, right)
        col = co_ref[step * (count // 2) + p]
        for k in range(own_ref.shape[0]):
            at = inv_ref[k]
            own_ref[at, col] = own[k * LANES : (k + 1) * LANES]
            other_ref[at, col] = other[k * LANES : (k + 1) * LANES]
    own, other = pick(flag_ref[0] == 1, down[:, :half], down[:, half:])
    first = own_ref.shape[1] - blocks
    for k in range(count):
        for m in range(blocks):
            tile = (slice(k * LANES, (k + 1) * LANES), slice(m * LANES, (m + 1) * LANES))
            own_ref[step * count + k, first + m] = own[tile]
            other_ref[step * count + k, first + m] = other[tile]


def ff_part(j, fo, co, inv, flags, normed, grad_mixed, w_up, b_up, w_down, before):
    units = fo.shape[0]
    count = FF_UNITS
    steps = units // count
    rows, features = normed.shape

    def up(k):
        return pl.BlockSpec((features, LANES), lambda i, fo, *more: (0, fo[count * i + k]))

    def bias(k):
        return pl.BlockSpec((1, 1, LANES), lambda i, fo, *more: (fo[count * i + k], 0, 0))

    def down(k):
        return pl.BlockSpec((LANES, features), lambda i, fo, *more: (fo[count * i + k], 0))

    cols = pl.BlockSpec((1, rows, count * LANES), lambda i, *more: (j, 0, i))
    hidden = jax.ShapeDtypeStruct((FF_PARTS, rows, units * LANES), bf16)
    blocks = units // 2 + features // 2 // LANES
    grad = jax.ShapeDtypeStruct((units, blocks, LANES, LANES), bf16)
    ks = range(count)
    at = 4 + 2 + 3 * count
    return pl.pallas_call(
        functools.partial(ff_part_kernel, count),
        grid_spec=pltpu.PrefetchScalarGridSpec(
            num_scalar_prefetch=4,
            grid=(steps,),
            in_specs=[whole(normed.shape), whole(normed.shape)]
            + [up(k) for k in ks]
            + [bias(k) for k in ks]
            + [down(k) for k in ks]
            + [pl.BlockSpec(memory_space=pl.ANY)] * len(before),
            out_specs=[cols, cols, whole(grad.shape), whole(grad.shape)]
            + [pl.BlockSpec((1, 1, count * LANES), lambda i, *more: (i, 0, 0))],
        ),
        out_shape=[hidden, hidden, grad, grad, jax.ShapeDtypeStruct((steps, 1, count * LANES), f32)],
        input_output_aliases={at: 0, at + 1: 1} if before else {},
        name="ff_part",
        compiler_params=params(),
        cost_estimate=cost(20),
    )(fo, co, inv, flags, normed, grad_mixed, *[w_up] * count, *[b_up] * count, *[w_down] * count, *before)


def ff_join_kernel(parts, blocks, units, *refs):
    fo_ref, src_ref, inv_ref, flag_ref, act_ref, gh_ref = refs[:6]
    up_refs = refs[6 : 6 + units]
    down_refs = refs[6 + units : 6 + 2 * units]
    at = 6 + 2 * units
    a_ref, b_ref, c_ref, d_ref, x_ref, branch_ref, mod_ref, bd_ref, wo_ref, att_ref = refs[at : at + 10]
    gres_ref, vec_ref, do_ref, own_ref, other_ref, out_ref = refs[at + 10 : at + 16]
    mixed_ref, back_ref, stage_ref, gb_ref, sem_ref = refs[at + 16 :]
    step = pl.program_id(0)

    @pl.when(step == 0)
    def _():
        mixed_ref[...] = jnp.zeros_like(mixed_ref)
        back_ref[...] = jnp.zeros_like(back_ref)

    @pl.when(step < parts)
    def _():
        wd = jnp.concatenate([r[...] for r in down_refs], axis=0)
        wu = jnp.concatenate([r[...] for r in up_refs], axis=1)
        half = mixed_ref.shape[0] // 2
        for k in range(2):
            part = slice(k * half, (k + 1) * half)
            mixed_ref[part] += dot_nn(act_ref[0, part], wd)
            back_ref[part] += dot_nt(gh_ref[0, part], wu)

    @pl.when(jnp.logical_and(step >= parts, step < parts + blocks))
    def _():
        e = step - parts
        block = 4 * PIECE
        part = pl.ds(pl.multiple_of(e * block, block), block)
        mixed = mixed_ref[part] + bd_ref[...]
        back = back_ref[part]
        branch = branch_ref[...].astype(f32)
        gate_one = mod_ref[2:3, :]
        gate_two = mod_ref[5:6, :]
        residual = x_ref[...].astype(f32) + gate_one * branch
        hat_rows, inv_std = hat_of(residual)
        up = jnp.concatenate([r[0] for r in (a_ref, b_ref, c_ref, d_ref)], axis=0).astype(f32)
        stage_ref[part] = (residual + gate_two * mixed).astype(bf16)
        for t in range(4):
            pltpu.make_async_copy(
                stage_ref.at[pl.ds(pl.multiple_of(e * block + t * PIECE, PIECE), PIECE)],
                out_ref.at[src_ref[4 * e + t]],
                sem_ref.at[4 * e + t],
            ).start()
        gres = up + norm_back(back * (1.0 + mod_ref[4:5, :]), hat_rows, inv_std)
        gres_ref[...] = gres.astype(bf16)
        low = (gate_one * gres).astype(bf16)
        gb_ref[part] = low
        do_ref[...] = dot_nt(low, wo_ref[...]).astype(bf16)
        grad_mixed = (gate_two * up).astype(bf16).astype(f32)

        def total(values):
            return jnp.sum(values, axis=0, keepdims=True)

        pieces = jnp.concatenate(
            [
                total(gres * branch),
                total(back),
                total(back * hat_rows),
                total(up * mixed),
                total(low.astype(f32)),
                total(grad_mixed),
                jnp.zeros((2, gate_one.shape[1]), f32),
            ],
            axis=0,
        )

        @pl.when(e == 0)
        def _():
            vec_ref[...] = pieces

        @pl.when(e > 0)
        def _():
            vec_ref[...] += pieces

    @pl.when(step >= parts + blocks)
    def _():
        width = own_ref.shape[1] * LANES
        half = gb_ref.shape[1] // 2
        flag = flag_ref[0]
        for grad_ref, side in ((own_ref, flag), (other_ref, 1 - flag)):
            start = pl.multiple_of(side * half + (step - parts - blocks) * width, width)
            got = dot_tn(att_ref[...], gb_ref[:, pl.ds(start, width)])
            place_rows(inv_ref, grad_ref, got.astype(bf16))

    @pl.when(step == pl.num_programs(0) - 1)
    def _():
        for k in range(sem_ref.shape[0]):
            pltpu.make_async_copy(
                stage_ref.at[pl.ds(k * PIECE, PIECE)], out_ref.at[src_ref[k]], sem_ref.at[k]
            ).wait()


def ff_join(fo, src, inv, flags, act, gh, w_up, w_down, pieces, x_rows, branch, mod, b_down, w_out, attended):
    parts, rows, wide = act.shape
    units = wide // LANES
    features = x_rows.shape[1]
    shards = features // LANES
    block = 4 * PIECE
    blocks = rows // block
    ends = features // 2 // UNIT

    def late(i):
        return jnp.clip(i - parts, 0, blocks - 1)

    def early(i):
        return jnp.minimum(i, parts - 1)

    rows_spec = pl.BlockSpec((block, features), lambda i, *more: (late(i), 0))
    slots = [
        pl.BlockSpec((1, PIECE, features), lambda i, fo, src, *more, t=t: (src[4 * late(i) + t], 0, 0))
        for t in range(4)
    ]
    ups = [
        pl.BlockSpec((features, LANES), lambda i, fo, *more, u=u: (0, fo[early(i) * units + u]))
        for u in range(units)
    ]
    downs = [
        pl.BlockSpec((LANES, features), lambda i, fo, *more, u=u: (fo[early(i) * units + u], 0))
        for u in range(units)
    ]
    hidden = pl.BlockSpec((1, rows, wide), lambda i, *more: (early(i), 0, 0))
    grad_spec = pl.BlockSpec(
        (shards, UNIT // LANES, LANES, LANES),
        lambda i, *more: (0, jnp.maximum(i - parts - blocks, 0), 0, 0),
    )
    grad = jax.ShapeDtypeStruct((shards, features // 2 // LANES, LANES, LANES), bf16)
    rows_shape = jax.ShapeDtypeStruct((rows, features), bf16)
    return pl.pallas_call(
        functools.partial(ff_join_kernel, parts, blocks, units),
        grid_spec=pltpu.PrefetchScalarGridSpec(
            num_scalar_prefetch=4,
            grid=(parts + blocks + ends,),
            in_specs=[hidden, hidden]
            + ups
            + downs
            + slots
            + [rows_spec, rows_spec, whole(mod.shape), whole(b_down.shape)]
            + [whole(w_out.shape), whole(attended.shape)],
            out_specs=[
                rows_spec,
                pl.BlockSpec((8, features), lambda i, *more: (0, 0)),
                rows_spec,
                grad_spec,
                grad_spec,
                pl.BlockSpec(memory_space=pl.ANY),
            ],
            scratch_shapes=[
                pltpu.VMEM((rows, features), f32),
                pltpu.VMEM((rows, features), f32),
                pltpu.VMEM((rows, features), bf16),
                pltpu.VMEM((rows, features), bf16),
                pltpu.SemaphoreType.DMA((rows // PIECE,)),
            ],
        ),
        out_shape=[
            rows_shape,
            jax.ShapeDtypeStruct((8, features), f32),
            rows_shape,
            grad,
            grad,
            jax.ShapeDtypeStruct(pieces.shape, bf16),
        ],
        name="ff_join",
        compiler_params=params(),
        cost_estimate=cost(45),
    )(
        fo, src, inv, flags, act, gh, *([w_up] * units), *([w_down] * units), *([pieces] * 4),
        x_rows, branch, mod, b_down, w_out, attended,
    )


def qkv_weight_kernel(inv_ref, flag_ref, n_ref, a_ref, b_ref, g0_ref, g1_ref):
    for out_ref, ref in ((g0_ref, a_ref), (g1_ref, b_ref)):
        place_rows(inv_ref, out_ref, dot_tn(n_ref[...], ref[0]).astype(bf16))


def qkv_weight(inv, flags, normed, grads):
    rows, features = normed.shape
    parts, unused, wide = grads.shape
    half = wide // 2
    shards = features // LANES
    tiles = half // LANES
    out_spec = pl.BlockSpec((shards, tiles, LANES, LANES), lambda i, *more: (0, i, 0, 0))
    grad = jax.ShapeDtypeStruct((shards, parts * tiles, LANES, LANES), bf16)
    return pl.pallas_call(
        qkv_weight_kernel,
        grid_spec=pltpu.PrefetchScalarGridSpec(
            num_scalar_prefetch=2,
            grid=(parts,),
            in_specs=[
                whole(normed.shape),
                pl.BlockSpec((1, rows, half), lambda i, inv, flags: (i, 0, flags[0])),
                pl.BlockSpec((1, rows, half), lambda i, inv, flags: (i, 0, 1 - flags[0])),
            ],
            out_specs=[out_spec, out_spec],
        ),
        out_shape=[grad, grad],
        name="qkv_weight",
        compiler_params=params(),
        cost_estimate=cost(6),
    )(inv, flags, normed, grads, grads)


def qkv_back_kernel(src_ref, *refs):
    count = len(refs) - 8
    grads = refs[:count]
    w_ref, x_ref, gres_ref, mod_ref, out_ref, vec_ref, stage_ref, sem_ref = refs[count:]
    step = pl.program_id(0)
    block = x_ref.shape[0]
    features = x_ref.shape[1]
    back = None
    bias = []
    for part in range(3):
        joined = jnp.concatenate([g[part] for g in grads], axis=1)
        bias.append(jnp.sum(joined.astype(f32), axis=0, keepdims=True))
        got = dot_nt(joined, w_ref[:, part * features : (part + 1) * features])
        back = got if back is None else back + got
    back = back.astype(bf16).astype(f32)
    hat_rows, inv_std = hat_of(x_ref[...].astype(f32))
    grad = gres_ref[...].astype(f32) + norm_back(back * (1.0 + mod_ref[1:2, :]), hat_rows, inv_std)
    stage_ref[pl.ds(pl.multiple_of(step * block, block), block)] = grad.astype(bf16)
    for t in range(4):
        pltpu.make_async_copy(
            stage_ref.at[pl.ds(pl.multiple_of(step * block + t * PIECE, PIECE), PIECE)],
            out_ref.at[src_ref[4 * step + t]],
            sem_ref.at[4 * step + t],
        ).start()
    pieces = jnp.concatenate(
        [
            jnp.sum(back, axis=0, keepdims=True),
            jnp.sum(back * hat_rows, axis=0, keepdims=True),
            bias[0],
            bias[2],
            jnp.zeros((4, features), f32),
        ],
        axis=0,
    )

    @pl.when(step == 0)
    def _():
        vec_ref[...] = pieces

    @pl.when(step > 0)
    def _():
        vec_ref[...] += pieces

    @pl.when(step == pl.num_programs(0) - 1)
    def _():
        for k in range(sem_ref.shape[0]):
            pltpu.make_async_copy(
                stage_ref.at[pl.ds(k * PIECE, PIECE)], out_ref.at[src_ref[k]], sem_ref.at[k]
            ).wait()


def qkv_backward(src, grads, w_qkv, x_rows, gres, mod):
    rows, features = x_rows.shape
    block = 4 * PIECE
    rows_spec = pl.BlockSpec((block, features), lambda i, src: (i, 0))
    grad_specs = [pl.BlockSpec((3, block, g.shape[2]), lambda i, src: (0, i, 0)) for g in grads]
    return pl.pallas_call(
        qkv_back_kernel,
        grid_spec=pltpu.PrefetchScalarGridSpec(
            num_scalar_prefetch=1,
            grid=(rows // block,),
            in_specs=grad_specs + [whole(w_qkv.shape), rows_spec, rows_spec, whole(mod.shape)],
            out_specs=[
                pl.BlockSpec(memory_space=pl.ANY),
                pl.BlockSpec((8, features), lambda i, src: (0, 0)),
            ],
            scratch_shapes=[
                pltpu.VMEM((rows, features), bf16),
                pltpu.SemaphoreType.DMA((rows // PIECE,)),
            ],
        ),
        out_shape=[
            jax.ShapeDtypeStruct((rows // PIECE, PIECE, features), bf16),
            jax.ShapeDtypeStruct((8, features), f32),
        ],
        name="qkv_backward",
        compiler_params=params(),
        cost_estimate=cost(14),
    )(src, *grads, w_qkv, x_rows, gres, mod)


def assemble_kernel(places, counts, core_ref, *refs):
    ins = refs[: 2 * len(counts)]
    outs = refs[2 * len(counts) :]
    swap = core_ref[0] == 1
    at = 0
    for k, count in enumerate(counts):
        for m in range(count):
            pair = pick(swap, ins[2 * k][m], ins[2 * k + 1][m])
            for tile, (out, row, col) in zip(pair, places[at]):
                outs[out][row * LANES : (row + 1) * LANES, col * LANES : (col + 1) * LANES] = tile.astype(f32)
            at += 1


def assemble(core, pairs, places, shapes):
    flat = [array for pair in pairs for array in pair]
    return pl.pallas_call(
        functools.partial(assemble_kernel, places, [own.shape[0] for own, unused in pairs]),
        grid_spec=pltpu.PrefetchScalarGridSpec(
            num_scalar_prefetch=1,
            grid=(1,),
            in_specs=[whole(array.shape) for array in flat],
            out_specs=[whole(shape) for shape in shapes],
        ),
        out_shape=[jax.ShapeDtypeStruct(shape, f32) for shape in shapes],
        name="assemble",
        compiler_params=params(),
        cost_estimate=cost(5),
    )(core, *flat)


def flip(axis, bit):
    size = lax.axis_size(axis)
    return [(i, i ^ (1 << bit)) for i in range(size)]


def trade(array, axis, bit):
    return lax.ppermute(array, axis, flip(axis, bit))


def add_low(a, b):
    return (a.astype(f32) + b.astype(f32)).astype(bf16)


class Chain:
    def __init__(self, clip_bits, own, sends, stage=0):
        self.clip_bits = clip_bits
        self.own = own
        self.sends = sends
        self.stage = stage
        self.got = None

    def launch(self):
        if self.stage == 0 or self.stage == self.clip_bits + 2:
            axis, bit = "win", 0
        elif self.stage == self.clip_bits + 1:
            axis, bit = "win", 1
        else:
            axis, bit = "clip", self.stage - 1
        self.got = [trade(send, axis, bit) for send in self.sends]

    def prepare(self):
        self.stage += 1
        both = list(zip(self.own, self.got))
        if self.stage <= self.clip_bits:
            half = self.own[0].shape[0] // 2
            self.sends = [joined([add_low(o[half:], g[half:]) for o, g in both])]
            self.own = [joined([add_low(o[:half], g[:half]) for o, g in both])]
        elif self.stage == self.clip_bits + 1:
            self.own = self.sends = [joined([add_low(o, g) for o, g in both])]
        else:
            exact = [o.astype(f32) + g.astype(f32) for o, g in both]
            self.own = self.sends = [
                joined([lax.reduce_precision(e, 8, 7).astype(bf16) for e in exact])
            ]

    def finish(self):
        while self.stage < self.clip_bits + 2:
            boundary((), [self], [])
        return self.own[0][0], self.got[0][0]


class Vectors:
    def __init__(self, clip_bits, me, rows, vectors):
        self.clip_bits = clip_bits
        self.me = me
        self.rows = rows
        self.gathered = vectors
        self.stage = 0
        self.sends = [jnp.concatenate([rows, vectors])]
        self.own = None
        self.got = None

    def launch(self):
        axis, bit = ("win", self.stage) if self.stage < 2 else ("clip", self.stage - 2)
        self.got = [trade(self.sends[0], axis, bit)]

    def prepare(self):
        got = self.got[0]
        count = got.shape[0] - self.gathered.shape[0]
        if self.stage < 2:
            both = self.sends[0] + got
            self.rows, self.gathered = both[:count], both[count:]
        else:
            self.rows = self.rows[:count] + got[:count]
            upper = (self.me >> (self.stage - 2)) & 1 == 1
            self.gathered = jnp.concatenate(pick(upper, self.gathered, got[count:]))
        self.stage += 1
        if self.stage < 2:
            self.sends = [both]
        else:
            self.sends = [jnp.concatenate([self.rows[self.rows.shape[0] // 2 :], self.gathered])]

    def finish(self):
        while self.stage < self.clip_bits + 1:
            boundary((), [self], [])
        self.prepare()
        return self.rows[0], self.gathered


def joined(arrays):
    return arrays[0] if len(arrays) == 1 else jnp.concatenate(arrays, axis=1)


def unite(*chains):
    first = chains[0]
    united = Chain(first.clip_bits, None, None, first.stage)
    united.own = [o for c in chains for o in c.own]
    united.got = [g for c in chains for g in c.got]
    return united


def boundary(inputs, moved, fresh):
    got = [c.got for c in moved]
    inputs, got = lax.optimization_barrier((inputs, got))
    for c, g in zip(moved, got):
        c.got = g
        c.prepare()
    chains = moved + fresh
    inputs, sends = lax.optimization_barrier((inputs, [c.sends for c in chains]))
    for c, sent in zip(chains, sends):
        c.sends = sent
        if c.own is not None and c.stage >= c.clip_bits + 1:
            c.own = sent
        c.launch()
    return inputs


def to_quadrants(slot_rows):
    local_slots = slot_rows.shape[0]
    channels = slot_rows.shape[-1]
    arranged = slot_rows.reshape(local_slots, 2, WST, 2, WST, channels).transpose(1, 3, 0, 2, 4, 5)
    return arranged.reshape(4, local_slots, PIECE, channels)


def from_quadrants(received):
    local_slots = received.shape[1]
    channels = received.shape[-1]
    arranged = received.reshape(2, 2, local_slots, WST, WST, channels).transpose(2, 0, 3, 1, 4, 5)
    return arranged.reshape(local_slots, 4 * PIECE, channels)


def exchange(quadrants):
    return lax.all_to_all(quadrants, "win", split_axis=0, concat_axis=0, tiled=True)


def local(
    tokens,
    condition,
    slot_order,
    rel_index,
    w_qkv,
    b_query,
    b_value,
    w_out,
    b_out,
    w_up,
    b_up,
    w_down,
    b_down,
    w_ada,
    b_ada,
    rel_table,
    grad_out,
):
    features = tokens.shape[-1]
    clips = lax.axis_size("clip")
    clip_bits = clips.bit_length() - 1
    me = lax.axis_index("clip")
    core = lax.axis_index("win") & 1
    ff = w_up.shape[1]
    fast = features // clips == LANES and ff // clips == FF_PARTS * LANES

    quadrants, rel_index = lax.optimization_barrier((to_quadrants(tokens[0]), rel_index))
    pieces = exchange(quadrants).reshape(-1, PIECE, features)
    grad_quadrants = to_quadrants(grad_out[0])
    slots = pieces.shape[0]
    per_frame = slots // FRAMES
    order_row = slot_order[0]
    window_place = jnp.arange(slots, dtype=jnp.int32)
    wanted = (window_place % FRAMES) * per_frame + window_place // FRAMES
    src = jnp.sum(
        jnp.where(order_row[None, :] == wanted[:, None], window_place[None, :], 0), axis=1
    ).astype(jnp.int32)
    windows = per_frame
    win = FRAMES * PIECE

    half = win // 2
    idx_mine = lax.dynamic_slice_in_dim(rel_index, core * half, half, 0)
    bias_mine = bias_gather(idx_mine, rel_table)
    grad_quadrants, bias_mine, w_ada = lax.optimization_barrier((grad_quadrants, bias_mine, w_ada))
    grad_pieces = exchange(grad_quadrants).reshape(-1, PIECE, features)
    bias_other = trade(bias_mine, "win", 0)

    lifted = jax.nn.silu(condition.astype(f32)).astype(bf16)
    modulation = jnp.dot(lifted, w_ada, preferred_element_type=f32)[0] + b_ada
    mod = jnp.concatenate([modulation.reshape(6, features), jnp.zeros((2, features), f32)])

    qkv_bias = jnp.concatenate([b_query, jnp.zeros_like(b_query), b_value]).astype(f32)[None]
    x_rows, normed, qkv = qkv_call(src, pieces, mod, qkv_bias, w_qkv)
    core_arr = core.astype(jnp.int32)[None]
    attended, probs, recips = attn_forward(core_arr, qkv, bias_mine, bias_other, windows)
    branch, normed_two, grad_mixed = out_call(
        src, grad_pieces, attended, x_rows, mod, b_out.astype(f32)[None], w_out
    )

    shards = features // LANES
    natural = jnp.arange(shards, dtype=jnp.int32)
    if fast:
        places = jnp.zeros_like(natural)
        for bit in range(clip_bits):
            places = places | (((natural >> (clip_bits - 1 - bit)) & 1) << bit)
        order = me ^ places
        inv = jnp.zeros_like(natural)
        for bit in range(clip_bits):
            inv = inv | ((((natural ^ me) >> (clip_bits - 1 - bit)) & 1) << bit)
        per_shard = ff // clips // LANES
        fos = [order * per_shard + j for j in range(FF_PARTS)]
        co = order[::2] & (clips // 2 - 1)
        upper = me >> (clip_bits - 1)
        flags = jnp.stack([core, (upper != core).astype(jnp.int32)]).astype(jnp.int32)
    else:
        inv = natural
        per_part = ff // LANES // FF_PARTS
        fos = [jnp.arange(per_part, dtype=jnp.int32) + j * per_part for j in range(FF_PARTS)]
        co = jnp.arange(per_part // 2, dtype=jnp.int32)
        flags = jnp.zeros((2,), jnp.int32)

    def chain(own, sends):
        return Chain(clip_bits, [own], [sends]) if fast else (own, sends)

    def meet(inputs, moved, fresh=()):
        return boundary(inputs, list(moved), list(fresh)) if fast else inputs

    def merge(*chains):
        return unite(*chains) if fast else chains

    b_up_rows = b_up.astype(f32).reshape(-1, 1, LANES)
    before, up_sums, ffs = [], [], []
    steps = [((), ()), ((), (0,)), ((0,), (1,)), ((0, 1), (2,))]
    for j in range(FF_PARTS):
        moved, fresh = steps[j]
        if j:
            normed_two, grad_mixed = meet(
                (normed_two, grad_mixed), [ffs[k] for k in moved], [ffs[k] for k in fresh]
            )
        act, gh, own, other, sums = ff_part(
            j, fos[j], co, inv, flags, normed_two, grad_mixed, w_up, b_up_rows, w_down, before
        )
        before = [act, gh]
        up_sums.append(sums.reshape(-1, LANES))
        ffs.append(chain(own, other))
    act, gh = meet((act, gh), ffs[:3], [ffs[3]])
    gres, early, grad_att, out_own, out_other, out_pieces = ff_join(
        jnp.concatenate(fos), src, inv, flags, act, gh, w_up, w_down, grad_pieces, x_rows, branch, mod,
        b_down.astype(f32)[None], w_out, attended,
    )
    local_slots = tokens.shape[1]
    piece_shape = (-1, local_slots, PIECE, features)
    out_pieces = exchange(out_pieces.reshape(piece_shape))
    wos = chain(out_own, out_other)
    grad_att = meet(grad_att, ffs[1:], [wos])
    pairs = probs.shape[0]
    grads_a, mine_a, others_a = attn_backward(core_arr, qkv, attended, grad_att, probs, recips, windows, 0, FIRST_PAIRS)
    grads_a = meet(grads_a, [ffs[2], ffs[3], wos])
    qa_own, qa_other = qkv_weight(inv, flags, normed, grads_a)
    qas = chain(qa_own, qa_other)
    front = merge(*ffs[:3])
    grad_att, unused, out_pieces = meet((grad_att, qa_own, out_pieces), [front, ffs[3], wos], [qas])
    others_a = trade(others_a, "win", 0)
    grads_b, mine_b, others_b = attn_backward(
        core_arr, qkv, attended, grad_att, probs, recips, windows, FIRST_PAIRS, pairs - FIRST_PAIRS
    )
    grads_b = meet(grads_b, [qas, wos])
    qb_own, qb_other = qkv_weight(inv, flags, normed, grads_b)
    qbs = chain(qb_own, qb_other)

    rear = merge(ffs[3], wos)
    gres_late, unused, others_a, others_b = meet((gres, qb_own, others_a, others_b), [front, rear], [qbs])
    others_b = trade(others_b, "win", 0)
    token_pieces, late = qkv_backward(src, (grads_a, grads_b), w_qkv, x_rows, gres_late, mod)
    token_pieces = exchange(token_pieces.reshape(piece_shape))
    late, others_b = meet((late, others_b), [qbs, qas, rear])
    rel_sums = bucket_sums(inv, idx_mine, [mine_a, mine_b], [others_a, others_b], rel_table.shape[0])

    if fast:
        here = natural[:, None] == order[None, :]
        up_sums = [jnp.sum(jnp.where(here[:, :, None], u[None], 0.0), axis=1) for u in up_sums]
    grad_b_up = jnp.stack(up_sums, axis=1 if fast else 0)
    d = features
    tile_rows = d // LANES
    lifted_row = lifted[0].astype(f32).reshape(1, tile_rows, LANES)
    early_rows = early[:6].reshape(6, tile_rows, LANES)
    late_rows = late[:4].reshape(4, tile_rows, LANES)
    vectors = jnp.concatenate(
        [early_rows, lifted_row, jnp.zeros_like(lifted_row), grad_b_up.reshape(-1, tile_rows, LANES), late_rows]
    )
    buckets = rel_table.shape[0]
    heads = rel_sums.shape[1]
    rel_rows = buckets // clips
    if fast:
        own_rows = rel_rows * heads // LANES
        chain_v = Vectors(
            clip_bits, me, rel_sums.reshape(shards, own_rows, LANES), vectors.reshape(-1, own_rows, LANES)
        )
        boundary(rel_sums, [qbs, qas], [chain_v])
        boundary((), [qbs, chain_v], [])
        last = merge(qas, qbs)
        token_pieces = boundary(token_pieces, [last, chain_v], [])
        boundary((), [last, chain_v], [])
        rel, vectors_all = chain_v.finish()
        sum_rel = rel.reshape(heads, rel_rows).T
        vectors_all = vectors_all.reshape(clips, -1, d)
    else:
        vectors_all = lax.psum(lax.all_gather(vectors.reshape(-1, d), "clip", axis=0), "win")
        rel = lax.psum(rel_sums.transpose(0, 2, 1).reshape(buckets, heads), "win")
        sum_rel = lax.psum_scatter(rel, "clip", scatter_dimension=0, tiled=True)
    late_all = vectors_all[:, -4:].reshape(clips, 4 * d)
    early_all = vectors_all[:, :-4]
    all_lifted = early_all[:, 6] * (1.0 / lax.axis_size("win"))
    all_terms = jnp.concatenate([late_all[:, : 2 * d], early_all[:, :4].reshape(clips, 4 * d)], axis=1)

    def own_block(vector):
        size = vector.shape[0] // clips
        return lax.dynamic_slice_in_dim(vector, me * size, size, 0)

    early_sum = jnp.sum(jnp.concatenate([early_all[:, 4:6], early_all[:, 8:]], axis=1), axis=0).reshape(-1)
    late_sum = jnp.sum(late_all[:, 2 * d :], axis=0)
    sum_bo, sum_bd, sum_bu = own_block(early_sum[:d]), own_block(early_sum[d : 2 * d]), own_block(early_sum[2 * d :])
    sum_bq, sum_bv = own_block(late_sum[:d]), own_block(late_sum[d:])
    ada_rows = d // clips
    lifted_rows = lax.dynamic_slice_in_dim(all_lifted, me * ada_rows, ada_rows, 1)
    grad_w_ada = jnp.dot(lifted_rows.T, all_terms, precision=lax.Precision.HIGHEST)
    grad_b_ada = own_block(jnp.sum(all_terms, axis=0))

    rows = d // clips
    block_out = from_quadrants(out_pieces).reshape(tokens.shape)
    if fast:
        side = shards // 2
        places = []
        for j in range(FF_PARTS):
            places += [[(0, 0, (c * side + m) * FF_PARTS + j) for c in range(2)] for m in range(side)]
            places += [[(1, j, c * side + m) for c in range(2)] for m in range(side)]
        places += [[(2, 0, c * side + m) for c in range(2)] for m in range(side)]
        sum_wu, sum_wd, sum_wo = assemble(
            core_arr, [front.finish(), rear.finish()], places, [(rows, ff), (ff // clips, d), (rows, d)]
        )
        places, first = [], 0
        for count in (FIRST_PAIRS // 2, (pairs - FIRST_PAIRS) // 2):
            for part in range(3):
                places += [
                    [(0, 0, part * shards + first + c * count + m) for c in range(2)] for m in range(count)
                ]
            first += 2 * count
        (sum_qkv,) = assemble(core_arr, [last.finish()], places, [(rows, 3 * d)])
    else:

        def share(whole_grad):
            part = lax.psum_scatter(whole_grad.astype(f32), "clip", scatter_dimension=0, tiled=True)
            return lax.psum(part, "win")

        def flat_rows(blocks):
            return blocks.transpose(0, 2, 1, 3).reshape(d, -1, LANES)

        halves = len(ffs[0][0][0]) // 2
        ups = [jnp.stack([flat_rows(g[:, :halves]) for g in f], axis=2).reshape(d, -1) for f in ffs]
        sum_wu = share(jnp.concatenate(ups, axis=1))
        downs = [jnp.concatenate([flat_rows(g[:, halves:]).reshape(d, -1) for g in f], axis=1) for f in ffs]
        sum_wd = share(jnp.concatenate(downs, axis=0))
        sum_wo = share(jnp.concatenate([flat_rows(g).reshape(d, -1) for g in wos], axis=1))
        parts = [
            jnp.concatenate([flat_rows(g).reshape(d, 3, -1) for g in q], axis=2) for q in (qas, qbs)
        ]
        sum_qkv = share(jnp.concatenate(parts, axis=2).reshape(d, 3 * d))
    grad_tokens = from_quadrants(token_pieces).reshape(tokens.shape)
    return (
        block_out,
        grad_tokens,
        sum_qkv,
        sum_bq,
        sum_bv,
        sum_wo,
        sum_bo,
        sum_wu,
        sum_bu,
        sum_wd,
        sum_bd,
        grad_w_ada,
        grad_b_ada,
        sum_rel,
    )


def solution(mesh):
    placed = (
        P("clip", "win", None, None),
        P("clip", None),
        P("clip", None),
    ) + (P(),) * 13 + (P("clip", "win", None, None),)
    return jax.shard_map(
        local,
        mesh=mesh,
        in_specs=placed,
        out_specs=(
            P("clip", "win", None, None),
            P("clip", "win", None, None),
            P("clip", None),
            P("clip"),
            P("clip"),
            P("clip", None),
            P("clip"),
            P("clip", None),
            P("clip"),
            P("clip", None),
            P("clip"),
            P("clip", None),
            P("clip"),
            P("clip", None),
        ),
        check_vma=False,
    )
```

```python
import functools
import math

import jax
import jax.numpy as jnp
from jax import lax
from jax.experimental import pallas as pl
from jax.experimental.pallas import tpu as pltpu
from jax.sharding import PartitionSpec as P

HEAD = 64
FRAMES = 5
WST = 8
PIECE = WST * WST
UNIT = 256
FF_PARTS = 4
FF_UNITS = 4
FF_BLOCKS = 2
FIRST_PAIRS = 6
LANES = 128
VMEM_LIMIT = 60 * 1024 * 1024
f32 = jnp.float32
bf16 = jnp.bfloat16
GELU_C = math.sqrt(2.0 / math.pi)
GELU_A = 0.044715


def dot_nn(a, b):
    return jnp.dot(a, b, preferred_element_type=f32)


def dot_nt(a, b):
    return lax.dot_general(a, b, (((1,), (1,)), ((), ())), preferred_element_type=f32)


def dot_tn(a, b):
    return lax.dot_general(a, b, (((0,), (0,)), ((), ())), preferred_element_type=f32)


def params():
    return pltpu.CompilerParams(vmem_limit_bytes=VMEM_LIMIT)


def cost(micros):
    return pl.CostEstimate(
        flops=int(micros * 1.0e9), bytes_accessed=int(micros * 2.0e6), transcendentals=0
    )


def pick(swap, first, second):
    return jnp.where(swap, second, first), jnp.where(swap, first, second)


def hat_of(rows):
    average = jnp.mean(rows, axis=-1, keepdims=True)
    centered = rows - average
    variance = jnp.mean(centered * centered, axis=-1, keepdims=True)
    inv_std = lax.rsqrt(variance + 1e-06)
    return centered * inv_std, inv_std


def norm_back(grad_hat, hat_rows, inv_std):
    first_mean = jnp.mean(grad_hat, axis=-1, keepdims=True)
    second_mean = jnp.mean(grad_hat * hat_rows, axis=-1, keepdims=True)
    return inv_std * (grad_hat - first_mean - hat_rows * second_mean)


def whole(shape):
    zeros = (0,) * len(shape)
    return pl.BlockSpec(shape, lambda *unused: zeros, pipeline_mode=pl.Buffered(1))


def bias_kernel(idx_ref, tab_ref, out_ref, scr_ref):
    lows = lax.broadcasted_iota(jnp.int32, (256, idx_ref.shape[1]), 0)
    tab = tab_ref[...]
    half = tab.shape[0] // 2
    heads = 16
    tiles = idx_ref.shape[1] // LANES
    win = out_ref.shape[2] // 2
    for i in range(8):
        idx = idx_ref[pl.ds(i, 1), :]
        low = idx & 255
        high = idx >> 8
        onehot = jnp.where(lows == low, 1.0, 0.0).astype(bf16)
        got = dot_nn(tab, onehot)
        got = got[:half] + got[half:]
        acc = got[:heads]
        for c in range(1, half // heads):
            acc = jnp.where(high == c, got[c * heads : (c + 1) * heads], acc)
        for t in range(tiles):
            scr_ref[t, pl.ds(i, heads, stride=8), :] = acc[:, t * LANES : (t + 1) * LANES]
    for pair in range(heads // 2):
        rows = []
        for h in range(2):
            at = (2 * pair + h) * 8
            rows.append(
                jnp.concatenate([scr_ref[t, at : at + 8, :] for t in range(tiles)], axis=1)[:, :win]
            )
        out_ref[pair] = jnp.concatenate(rows, axis=1)


def bias_gather(idx, table):
    rows, win = idx.shape
    padded = -(-win // LANES) * LANES
    buckets, heads = table.shape
    upper_f = lax.reduce_precision(table, 8, 7)
    lower = (table - upper_f).astype(bf16)

    def arrange(t):
        return t.reshape(-1, 256, heads).transpose(0, 2, 1).reshape(-1, 256)

    tab = jnp.concatenate([arrange(upper_f.astype(bf16)), arrange(lower)], axis=0)
    idx = jnp.pad(idx, ((0, 0), (0, padded - win)))
    return pl.pallas_call(
        bias_kernel,
        grid=(rows // 8,),
        in_specs=[pl.BlockSpec((8, padded), lambda i: (i, 0)), whole(tab.shape)],
        out_specs=pl.BlockSpec((heads // 2, 8, 2 * win), lambda i: (0, i, 0)),
        out_shape=jax.ShapeDtypeStruct((heads // 2, rows, 2 * win), f32),
        scratch_shapes=[pltpu.VMEM((padded // LANES, 8 * heads, LANES), f32)],
        name="bias_gather",
        compiler_params=params(),
        cost_estimate=cost(0.9),
    )(idx, tab)


def bucket_kernel(idx_ref, *refs):
    out_ref, acc_ref, scr_ref = refs[-3:]
    keep_refs = refs[: (len(refs) - 3) // 2]
    got_refs = refs[(len(refs) - 3) // 2 : -3]

    @pl.when(pl.program_id(0) == 0)
    def _():
        acc_ref[...] = jnp.zeros_like(acc_ref)

    padded = idx_ref.shape[1]
    tiles = padded // LANES
    keeps = [(r, k) for r in keep_refs for k in range(r.shape[0])]
    gots = [(r, k) for r in got_refs for k in range(r.shape[0])]
    pairs = len(keeps)
    heads = 2 * pairs
    win = keep_refs[0].shape[2] // 2
    step_rows = idx_ref.shape[0]
    lows = lax.broadcasted_iota(jnp.int32, (256, padded), 0)
    zero = jnp.zeros((step_rows, padded - win), f32)
    for pair in range(pairs):
        (keep_ref, k), (got_ref, unused) = keeps[pair], gots[pair]
        sums = keep_ref[k].astype(f32) + got_ref[k].astype(f32)
        for h in range(2):
            part = jnp.concatenate([sums[:, h * win : (h + 1) * win], zero], axis=1)
            at = (2 * pair + h) * step_rows
            for t in range(tiles):
                scr_ref[t, at : at + step_rows, :] = part[:, t * LANES : (t + 1) * LANES]
    total = acc_ref[...]
    for i in range(step_rows):
        idx = idx_ref[pl.ds(i, 1), :]
        low = idx & 255
        high = idx >> 8
        onehot = jnp.where(lows == low, 1.0, 0.0).astype(bf16)
        sums = jnp.concatenate(
            [scr_ref[t, pl.ds(i, heads, stride=step_rows), :] for t in range(tiles)], axis=1
        )
        spread = jnp.concatenate(
            [jnp.where(high == c, sums, 0.0) for c in range(acc_ref.shape[0] // heads)], axis=0
        )
        total += dot_nt(spread.astype(bf16), onehot)
    acc_ref[...] = total

    @pl.when(pl.program_id(0) == pl.num_programs(0) - 1)
    def _():
        for k in range(out_ref.shape[0]):
            for t in range(2):
                out_ref[k, t * heads : (t + 1) * heads] = total[
                    k * heads : (k + 1) * heads, t * LANES : (t + 1) * LANES
                ]


def bucket_sums(idx, keeps, gots, buckets):
    rows, win = idx.shape
    padded = -(-win // LANES) * LANES
    heads = 2 * sum(k.shape[0] for k in keeps)
    step_rows = 16
    idx = jnp.pad(idx, ((0, 0), (0, padded - win)))
    out_rows = buckets // 256
    sum_specs = [pl.BlockSpec((k.shape[0], step_rows, 2 * win), lambda i: (0, i, 0)) for k in keeps]
    out_shape = jax.ShapeDtypeStruct((out_rows, 2 * heads, LANES), f32)
    return pl.pallas_call(
        bucket_kernel,
        grid=(rows // step_rows,),
        in_specs=[pl.BlockSpec((step_rows, padded), lambda i: (i, 0))] + sum_specs + sum_specs,
        out_specs=pl.BlockSpec(out_shape.shape, lambda i: (0, 0, 0)),
        out_shape=out_shape,
        scratch_shapes=[
            pltpu.VMEM((out_rows * heads, 256), f32),
            pltpu.VMEM((padded // LANES, step_rows * heads, LANES), f32),
        ],
        name="bucket_sums",
        compiler_params=params(),
        cost_estimate=cost(14),
    )(idx, *keeps, *gots)


def qkv_kernel(src_ref, a_ref, b_ref, c_ref, d_ref, mod_ref, bias_ref, w_ref, x_ref, n_ref, o_ref):
    rows = jnp.concatenate([r[0] for r in (a_ref, b_ref, c_ref, d_ref)], axis=0)
    x_ref[...] = rows
    hat_rows, unused = hat_of(rows.astype(f32))
    normed = (hat_rows * (1.0 + mod_ref[1:2, :]) + mod_ref[0:1, :]).astype(bf16)
    n_ref[...] = normed
    features = rows.shape[1]
    for j in range(w_ref.shape[1] // 512):
        cols = slice(j * 512, (j + 1) * 512)
        got = dot_nn(normed, w_ref[:, cols]) + bias_ref[0:1, cols]
        if (j + 1) * 512 <= features:
            got = got.astype(bf16).astype(f32) * (1.0 / math.sqrt(HEAD))
        o_ref[:, cols] = got.astype(bf16)


def slot_spec(features, t):
    return pl.BlockSpec((1, PIECE, features), lambda i, src, t=t: (src[4 * i + t], 0, 0))


def qkv_call(src, pieces, mod, qkv_bias, w_qkv):
    count, unused, features = pieces.shape
    rows = count * PIECE
    wide = w_qkv.shape[1]
    block = 4 * PIECE
    return pl.pallas_call(
        qkv_kernel,
        grid_spec=pltpu.PrefetchScalarGridSpec(
            num_scalar_prefetch=1,
            grid=(count // 4,),
            in_specs=[slot_spec(features, t) for t in range(4)]
            + [whole(mod.shape), whole(qkv_bias.shape), whole(w_qkv.shape)],
            out_specs=[
                pl.BlockSpec((block, features), lambda i, src: (i, 0)),
                pl.BlockSpec((block, features), lambda i, src: (i, 0)),
                pl.BlockSpec((block, wide), lambda i, src: (i, 0)),
            ],
        ),
        out_shape=[
            jax.ShapeDtypeStruct((rows, features), bf16),
            jax.ShapeDtypeStruct((rows, features), bf16),
            jax.ShapeDtypeStruct((rows, wide), bf16),
        ],
        name="norm_qkv",
        compiler_params=params(),
        cost_estimate=cost(0.6),
    )(src, pieces, pieces, pieces, pieces, mod, qkv_bias, w_qkv)


def split_pair(x, left):
    zero = jnp.zeros_like(x)
    return jnp.concatenate([jnp.where(left, x, zero), jnp.where(left, zero, x)], axis=0)


def values_ones(v, left):
    one = jnp.ones_like(v)
    zero = jnp.zeros_like(v)
    marks = jnp.concatenate([jnp.where(left, one, zero), jnp.where(left, zero, one)], axis=0)
    return jnp.concatenate([split_pair(v, left), marks], axis=1)


def attn_kernel(windows, core_ref, q_ref, k_ref, v_ref, mine_ref, other_ref, o_ref, p_ref, r_ref, b_ref):
    win = q_ref.shape[0] // windows
    half = win // 2
    left = lax.broadcasted_iota(jnp.int32, (win, LANES), 1) < HEAD
    first = core_ref[0] == 0
    b_ref[:half] = jnp.where(first, mine_ref[0], other_ref[0])
    b_ref[half:] = jnp.where(first, other_ref[0], mine_ref[0])
    lowest = jnp.float32(-jnp.inf)
    whole_tiles = win // LANES * LANES
    for u in range(windows):
        rows = slice(u * win, (u + 1) * win)
        keys = split_pair(k_ref[rows], left)
        vals = values_ones(v_ref[rows], left)
        s = dot_nt(q_ref[rows], keys) + b_ref[...]
        lo = s[:, :whole_tiles]
        mid = s[:, whole_tiles : whole_tiles + LANES]
        hi = s[:, whole_tiles + LANES :]
        top_lo = jnp.where(left, mid, lowest)
        top_hi = jnp.where(left, lowest, mid)
        for t in range(whole_tiles // LANES):
            cols = slice(t * LANES, (t + 1) * LANES)
            top_lo = jnp.maximum(top_lo, lo[:, cols])
            top_hi = jnp.maximum(top_hi, hi[:, cols])
        top_lo = jnp.max(top_lo, axis=1, keepdims=True)
        top_hi = jnp.max(top_hi, axis=1, keepdims=True)
        e = jnp.concatenate(
            [
                jnp.exp(lo - top_lo),
                jnp.exp(mid - jnp.where(left, top_lo, top_hi)),
                jnp.exp(hi - top_hi),
            ],
            axis=1,
        ).astype(bf16)
        p_ref[0, u] = e
        got = dot_nn(e, vals)
        r = 1.0 / got[:, LANES:]
        r_ref[rows] = r
        o_ref[rows] = (got[:, :LANES] * r).astype(bf16)


def attn_forward(core, qkv, bias_mine, bias_other, windows):
    rows = qkv.shape[0]
    win = rows // windows
    pairs = bias_mine.shape[0]
    features = qkv.shape[1] // 3

    def col(part):
        return pl.BlockSpec((rows, LANES), lambda h, c, part=part: (0, part * pairs + h))

    half_spec = pl.BlockSpec((1, win // 2, 2 * win), lambda h, c: (h, 0, 0))
    return pl.pallas_call(
        functools.partial(attn_kernel, windows),
        grid_spec=pltpu.PrefetchScalarGridSpec(
            num_scalar_prefetch=1,
            grid=(pairs,),
            in_specs=[col(0), col(1), col(2), half_spec, half_spec],
            out_specs=[
                col(0),
                pl.BlockSpec((1, windows, win, 2 * win), lambda h, c: (h, 0, 0, 0)),
                col(0),
            ],
            scratch_shapes=[pltpu.VMEM((win, 2 * win), f32)],
        ),
        out_shape=[
            jax.ShapeDtypeStruct((rows, features), bf16),
            jax.ShapeDtypeStruct((pairs, windows, win, 2 * win), bf16),
            jax.ShapeDtypeStruct((rows, features), f32),
        ],
        name="attn_forward",
        compiler_params=params(),
        cost_estimate=cost(0.9),
    )(core, qkv, qkv, qkv, bias_mine, bias_other)


def fold_delta(dx, lane):
    lower_half = (lane & 32) == 0
    dx = dx + jnp.where(lower_half, pltpu.roll(dx, LANES - 32, 1), pltpu.roll(dx, 32, 1))
    upper = dx.astype(bf16)
    lower = (dx - upper.astype(f32)).astype(bf16)
    return jnp.where(lower_half, upper, lower)


def attn_back_kernel(windows, core_ref, q_ref, k_ref, v_ref, o_ref, do_ref, p_ref, r_ref, g_ref, mine_ref, other_ref):
    win = q_ref.shape[0] // windows
    lane = lax.broadcasted_iota(jnp.int32, (win, LANES), 1)
    left = lane < HEAD
    sums = None
    for u in range(windows):
        rows = slice(u * win, (u + 1) * win)
        keys = split_pair(k_ref[rows], left)
        vals = values_ones(v_ref[rows], left)
        up = (do_ref[rows].astype(f32) * r_ref[rows]).astype(bf16)
        delta = fold_delta(-(up.astype(f32) * o_ref[rows].astype(f32)), lane)
        d = dot_nt(jnp.concatenate([up, delta], axis=1), vals)
        p = p_ref[0, u]
        ds = p.astype(f32) * d
        sums = ds if sums is None else sums + ds
        low = ds.astype(bf16)
        g_ref[0, rows] = (dot_nn(low, keys) * (1.0 / math.sqrt(HEAD))).astype(bf16)
        dk = dot_tn(low, q_ref[rows])
        g_ref[1, rows] = jnp.where(left, dk[:win], dk[win:]).astype(bf16)
        dv = dot_tn(p, up)
        g_ref[2, rows] = jnp.where(left, dv[:win], dv[win:]).astype(bf16)
    half = win // 2
    first, second = sums[:half].astype(bf16), sums[half:].astype(bf16)
    mine_ref[0], other_ref[0] = pick(core_ref[0] == 1, first, second)


def attn_backward(core, qkv, attended, grad_att, probs, recips, windows, first, count):
    rows = qkv.shape[0]
    win = rows // windows
    pairs = probs.shape[0]

    def col(part):
        return pl.BlockSpec((rows, LANES), lambda h, core, part=part: (0, part * pairs + first + h))

    half_spec = pl.BlockSpec((1, win // 2, 2 * win), lambda h, core: (h, 0, 0))
    half_shape = jax.ShapeDtypeStruct((count, win // 2, 2 * win), bf16)
    return pl.pallas_call(
        functools.partial(attn_back_kernel, windows),
        grid_spec=pltpu.PrefetchScalarGridSpec(
            num_scalar_prefetch=1,
            grid=(count,),
            in_specs=[
                col(0),
                col(1),
                col(2),
                col(0),
                col(0),
                pl.BlockSpec((1, windows, win, 2 * win), lambda h, core: (first + h, 0, 0, 0)),
                col(0),
            ],
            out_specs=[
                pl.BlockSpec((3, rows, LANES), lambda h, core: (0, 0, h)),
                half_spec,
                half_spec,
            ],
        ),
        out_shape=[jax.ShapeDtypeStruct((3, rows, count * LANES), bf16), half_shape, half_shape],
        name="attn_backward",
        compiler_params=params(),
        cost_estimate=cost(3 * count),
    )(core, qkv, qkv, qkv, attended, grad_att, probs, recips)


def out_kernel(src_ref, a_ref, b_ref, c_ref, d_ref, att_ref, x_ref, mod_ref, bo_ref, w_ref, branch_ref, n_ref, gm_ref):
    branch = (dot_nn(att_ref[...], w_ref[...]) + bo_ref[...]).astype(bf16)
    branch_ref[...] = branch
    residual = x_ref[...].astype(f32) + mod_ref[2:3, :] * branch.astype(f32)
    hat_rows, unused = hat_of(residual)
    n_ref[...] = (hat_rows * (1.0 + mod_ref[4:5, :]) + mod_ref[3:4, :]).astype(bf16)
    up = jnp.concatenate([r[0] for r in (a_ref, b_ref, c_ref, d_ref)], axis=0)
    gm_ref[...] = (mod_ref[5:6, :] * up.astype(f32)).astype(bf16)


def out_call(src, pieces, attended, x_rows, mod, b_out, w_out):
    count, unused, features = pieces.shape
    rows = count * PIECE
    block = 4 * PIECE
    rows_spec = pl.BlockSpec((block, features), lambda i, src: (i, 0))
    sds = jax.ShapeDtypeStruct((rows, features), bf16)
    return pl.pallas_call(
        out_kernel,
        grid_spec=pltpu.PrefetchScalarGridSpec(
            num_scalar_prefetch=1,
            grid=(count // 4,),
            in_specs=[slot_spec(features, t) for t in range(4)]
            + [rows_spec, rows_spec, whole(mod.shape), whole(b_out.shape), whole(w_out.shape)],
            out_specs=[rows_spec, rows_spec, rows_spec],
        ),
        out_shape=[sds, sds, sds],
        name="out_norm",
        compiler_params=params(),
        cost_estimate=cost(0.3),
    )(src, pieces, pieces, pieces, pieces, attended, x_rows, mod, b_out, w_out)


def place_rows(inv_ref, out_ref, values):
    for k in range(out_ref.shape[0]):
        at = inv_ref[k]
        for m in range(out_ref.shape[1]):
            out_ref[at, m] = values[k * LANES : (k + 1) * LANES, m * LANES : (m + 1) * LANES]


def ff_part_kernel(count, fo_ref, co_ref, inv_ref, flag_ref, n_ref, gm_ref, *refs):
    ups = refs[:count]
    biases = refs[count : 2 * count]
    downs = refs[2 * count : 3 * count]
    act_ref, gh_ref, own_ref, other_ref, sum_ref = refs[-5:]
    step = pl.program_id(0)
    rows = n_ref.shape[0]
    block = rows // FF_BLOCKS
    wu = jnp.concatenate([r[...] for r in ups], axis=1)
    wd = jnp.concatenate([r[...] for r in downs], axis=0)
    bias = jnp.concatenate([r[0] for r in biases], axis=1)
    sums = None
    for c in range(FF_BLOCKS):
        part = slice(c * block, (c + 1) * block)
        v = dot_nn(n_ref[part], wu) + bias
        v2 = v * v
        t = jnp.tanh(v * (GELU_C + (GELU_C * GELU_A) * v2))
        h = 0.5 + 0.5 * t
        slope = h + (0.5 * v) * (1.0 - t * t) * (GELU_C + (3.0 * GELU_C * GELU_A) * v2)
        gh = (dot_nt(gm_ref[part], wd) * slope).astype(bf16)
        act_ref[0, part] = (v * h).astype(bf16)
        gh_ref[0, part] = gh
        piece = jnp.sum(gh.astype(f32), axis=0, keepdims=True)
        sums = piece if sums is None else sums + piece
    sum_ref[0] = sums
    up = dot_tn(n_ref[...], gh_ref[0]).astype(bf16)
    down = dot_tn(act_ref[0], gm_ref[...]).astype(bf16)
    half = down.shape[1] // 2
    blocks = half // LANES
    for p in range(count // 2):
        left = up[:, 2 * p * LANES : (2 * p + 1) * LANES]
        right = up[:, (2 * p + 1) * LANES : (2 * p + 2) * LANES]
        own, other = pick(flag_ref[1] == 1, left, right)
        col = co_ref[step * (count // 2) + p]
        for k in range(own_ref.shape[0]):
            at = inv_ref[k]
            own_ref[at, col] = own[k * LANES : (k + 1) * LANES]
            other_ref[at, col] = other[k * LANES : (k + 1) * LANES]
    own, other = pick(flag_ref[0] == 1, down[:, :half], down[:, half:])
    first = own_ref.shape[1] - blocks
    for k in range(count):
        for m in range(blocks):
            tile = (slice(k * LANES, (k + 1) * LANES), slice(m * LANES, (m + 1) * LANES))
            own_ref[step * count + k, first + m] = own[tile]
            other_ref[step * count + k, first + m] = other[tile]


def ff_part(j, fo, co, inv, flags, normed, grad_mixed, w_up, b_up, w_down, before):
    units = fo.shape[0]
    count = FF_UNITS
    steps = units // count
    rows, features = normed.shape

    def up(k):
        return pl.BlockSpec((features, LANES), lambda i, fo, *more: (0, fo[count * i + k]))

    def bias(k):
        return pl.BlockSpec((1, 1, LANES), lambda i, fo, *more: (fo[count * i + k], 0, 0))

    def down(k):
        return pl.BlockSpec((LANES, features), lambda i, fo, *more: (fo[count * i + k], 0))

    cols = pl.BlockSpec((1, rows, count * LANES), lambda i, *more: (j, 0, i))
    hidden = jax.ShapeDtypeStruct((FF_PARTS, rows, units * LANES), bf16)
    blocks = units // 2 + features // 2 // LANES
    grad = jax.ShapeDtypeStruct((units, blocks, LANES, LANES), bf16)
    ks = range(count)
    at = 4 + 2 + 3 * count
    return pl.pallas_call(
        functools.partial(ff_part_kernel, count),
        grid_spec=pltpu.PrefetchScalarGridSpec(
            num_scalar_prefetch=4,
            grid=(steps,),
            in_specs=[whole(normed.shape), whole(normed.shape)]
            + [up(k) for k in ks]
            + [bias(k) for k in ks]
            + [down(k) for k in ks]
            + [pl.BlockSpec(memory_space=pl.ANY)] * len(before),
            out_specs=[cols, cols, whole(grad.shape), whole(grad.shape)]
            + [pl.BlockSpec((1, 1, count * LANES), lambda i, *more: (i, 0, 0))],
        ),
        out_shape=[hidden, hidden, grad, grad, jax.ShapeDtypeStruct((steps, 1, count * LANES), f32)],
        input_output_aliases={at: 0, at + 1: 1} if before else {},
        name="ff_part",
        compiler_params=params(),
        cost_estimate=cost(20),
    )(fo, co, inv, flags, normed, grad_mixed, *[w_up] * count, *[b_up] * count, *[w_down] * count, *before)


def ff_join_kernel(units, fo_ref, act_ref, gh_ref, *refs):
    up_refs = refs[:units]
    down_refs = refs[units : 2 * units]
    mixed_ref, back_ref = refs[2 * units :]

    @pl.when(pl.program_id(0) == 0)
    def _():
        mixed_ref[...] = jnp.zeros_like(mixed_ref)
        back_ref[...] = jnp.zeros_like(back_ref)

    wd = jnp.concatenate([r[...] for r in down_refs], axis=0)
    wu = jnp.concatenate([r[...] for r in up_refs], axis=1)
    half = mixed_ref.shape[0] // 2
    for k in range(2):
        part = slice(k * half, (k + 1) * half)
        mixed_ref[part] += dot_nn(act_ref[0, part], wd)
        back_ref[part] += dot_nt(gh_ref[0, part], wu)


def ff_join(fo, act, gh, w_up, w_down):
    parts, rows, wide = act.shape
    units = wide // LANES
    features = w_up.shape[0]
    ups = [
        pl.BlockSpec((features, LANES), lambda i, fo, u=u: (0, fo[i * units + u])) for u in range(units)
    ]
    downs = [
        pl.BlockSpec((LANES, features), lambda i, fo, u=u: (fo[i * units + u], 0)) for u in range(units)
    ]
    hidden = pl.BlockSpec((1, rows, wide), lambda i, fo: (i, 0, 0))
    sums = jax.ShapeDtypeStruct((rows, features), f32)
    return pl.pallas_call(
        functools.partial(ff_join_kernel, units),
        grid_spec=pltpu.PrefetchScalarGridSpec(
            num_scalar_prefetch=1,
            grid=(parts,),
            in_specs=[hidden, hidden] + ups + downs,
            out_specs=[whole(sums.shape), whole(sums.shape)],
        ),
        out_shape=[sums, sums],
        name="ff_join",
        compiler_params=params(),
        cost_estimate=cost(28),
    )(fo, act, gh, *([w_up] * units), *([w_down] * units))


def ff_rows_kernel(blocks, src_ref, inv_ref, flag_ref, mixed_ref, back_ref, *refs):
    a_ref, b_ref, c_ref, d_ref, x_ref, branch_ref, mod_ref, bd_ref, wo_ref, att_ref = refs[:10]
    gres_ref, vec_ref, do_ref, own_ref, other_ref, out_ref = refs[10:16]
    stage_ref, gb_ref, sem_ref = refs[16:]
    step = pl.program_id(0)

    @pl.when(step < blocks)
    def _():
        e = step
        block = 4 * PIECE
        part = pl.ds(pl.multiple_of(e * block, block), block)
        mixed = mixed_ref[...] + bd_ref[...]
        back = back_ref[...]
        branch = branch_ref[...].astype(f32)
        gate_one = mod_ref[2:3, :]
        gate_two = mod_ref[5:6, :]
        residual = x_ref[...].astype(f32) + gate_one * branch
        hat_rows, inv_std = hat_of(residual)
        up = jnp.concatenate([r[0] for r in (a_ref, b_ref, c_ref, d_ref)], axis=0).astype(f32)
        stage_ref[part] = (residual + gate_two * mixed).astype(bf16)
        for t in range(4):
            pltpu.make_async_copy(
                stage_ref.at[pl.ds(pl.multiple_of(e * block + t * PIECE, PIECE), PIECE)],
                out_ref.at[src_ref[4 * e + t]],
                sem_ref.at[4 * e + t],
            ).start()
        gres = up + norm_back(back * (1.0 + mod_ref[4:5, :]), hat_rows, inv_std)
        gres_ref[...] = gres.astype(bf16)
        low = (gate_one * gres).astype(bf16)
        gb_ref[part] = low
        do_ref[...] = dot_nt(low, wo_ref[...]).astype(bf16)
        grad_mixed = (gate_two * up).astype(bf16).astype(f32)

        def total(values):
            return jnp.sum(values, axis=0, keepdims=True)

        pieces = jnp.concatenate(
            [
                total(gres * branch),
                total(back),
                total(back * hat_rows),
                total(up * mixed),
                total(low.astype(f32)),
                total(grad_mixed),
                jnp.zeros((2, gate_one.shape[1]), f32),
            ],
            axis=0,
        )

        @pl.when(e == 0)
        def _():
            vec_ref[...] = pieces

        @pl.when(e > 0)
        def _():
            vec_ref[...] += pieces

    @pl.when(step >= blocks)
    def _():
        width = own_ref.shape[1] * LANES
        half = gb_ref.shape[1] // 2
        flag = flag_ref[0]
        for grad_ref, side in ((own_ref, flag), (other_ref, 1 - flag)):
            start = pl.multiple_of(side * half + (step - blocks) * width, width)
            got = dot_tn(att_ref[...], gb_ref[:, pl.ds(start, width)])
            place_rows(inv_ref, grad_ref, got.astype(bf16))

    @pl.when(step == pl.num_programs(0) - 1)
    def _():
        for k in range(sem_ref.shape[0]):
            pltpu.make_async_copy(
                stage_ref.at[pl.ds(k * PIECE, PIECE)], out_ref.at[src_ref[k]], sem_ref.at[k]
            ).wait()


def ff_rows(src, inv, flags, mixed, back, pieces, x_rows, branch, mod, b_down, w_out, attended):
    rows, features = x_rows.shape
    shards = features // LANES
    block = 4 * PIECE
    blocks = rows // block
    ends = features // 2 // UNIT

    def at(i):
        return jnp.minimum(i, blocks - 1)

    rows_spec = pl.BlockSpec((block, features), lambda i, *more: (at(i), 0))
    slots = [
        pl.BlockSpec((1, PIECE, features), lambda i, src, *more, t=t: (src[4 * at(i) + t], 0, 0))
        for t in range(4)
    ]
    grad_spec = pl.BlockSpec(
        (shards, UNIT // LANES, LANES, LANES), lambda i, *more: (0, jnp.maximum(i - blocks, 0), 0, 0)
    )
    grad = jax.ShapeDtypeStruct((shards, features // 2 // LANES, LANES, LANES), bf16)
    rows_shape = jax.ShapeDtypeStruct((rows, features), bf16)
    return pl.pallas_call(
        functools.partial(ff_rows_kernel, blocks),
        grid_spec=pltpu.PrefetchScalarGridSpec(
            num_scalar_prefetch=3,
            grid=(blocks + ends,),
            in_specs=[rows_spec, rows_spec]
            + slots
            + [rows_spec, rows_spec, whole(mod.shape), whole(b_down.shape)]
            + [whole(w_out.shape), whole(attended.shape)],
            out_specs=[
                rows_spec,
                pl.BlockSpec((8, features), lambda i, *more: (0, 0)),
                rows_spec,
                grad_spec,
                grad_spec,
                pl.BlockSpec(memory_space=pl.ANY),
            ],
            scratch_shapes=[
                pltpu.VMEM((rows, features), bf16),
                pltpu.VMEM((rows, features), bf16),
                pltpu.SemaphoreType.DMA((rows // PIECE,)),
            ],
        ),
        out_shape=[
            rows_shape,
            jax.ShapeDtypeStruct((8, features), f32),
            rows_shape,
            grad,
            grad,
            jax.ShapeDtypeStruct(pieces.shape, bf16),
        ],
        name="ff_rows",
        compiler_params=params(),
        cost_estimate=cost(22),
    )(src, inv, flags, mixed, back, *([pieces] * 4), x_rows, branch, mod, b_down, w_out, attended)


def qkv_weight_kernel(inv_ref, flag_ref, n_ref, a_ref, b_ref, g0_ref, g1_ref):
    for out_ref, ref in ((g0_ref, a_ref), (g1_ref, b_ref)):
        place_rows(inv_ref, out_ref, dot_tn(n_ref[...], ref[0]).astype(bf16))


def qkv_weight(inv, flags, normed, grads):
    rows, features = normed.shape
    parts, unused, wide = grads.shape
    half = wide // 2
    shards = features // LANES
    tiles = half // LANES
    out_spec = pl.BlockSpec((shards, tiles, LANES, LANES), lambda i, *more: (0, i, 0, 0))
    grad = jax.ShapeDtypeStruct((shards, parts * tiles, LANES, LANES), bf16)
    return pl.pallas_call(
        qkv_weight_kernel,
        grid_spec=pltpu.PrefetchScalarGridSpec(
            num_scalar_prefetch=2,
            grid=(parts,),
            in_specs=[
                whole(normed.shape),
                pl.BlockSpec((1, rows, half), lambda i, inv, flags: (i, 0, flags[0])),
                pl.BlockSpec((1, rows, half), lambda i, inv, flags: (i, 0, 1 - flags[0])),
            ],
            out_specs=[out_spec, out_spec],
        ),
        out_shape=[grad, grad],
        name="qkv_weight",
        compiler_params=params(),
        cost_estimate=cost(6),
    )(inv, flags, normed, grads, grads)


def qkv_back_kernel(src_ref, *refs):
    count = len(refs) - 8
    grads = refs[:count]
    w_ref, x_ref, gres_ref, mod_ref, out_ref, vec_ref, stage_ref, sem_ref = refs[count:]
    step = pl.program_id(0)
    block = x_ref.shape[0]
    features = x_ref.shape[1]
    back = None
    bias = []
    for part in range(3):
        joined = jnp.concatenate([g[part] for g in grads], axis=1)
        bias.append(jnp.sum(joined.astype(f32), axis=0, keepdims=True))
        got = dot_nt(joined, w_ref[:, part * features : (part + 1) * features])
        back = got if back is None else back + got
    back = back.astype(bf16).astype(f32)
    hat_rows, inv_std = hat_of(x_ref[...].astype(f32))
    grad = gres_ref[...].astype(f32) + norm_back(back * (1.0 + mod_ref[1:2, :]), hat_rows, inv_std)
    stage_ref[pl.ds(pl.multiple_of(step * block, block), block)] = grad.astype(bf16)
    for t in range(4):
        pltpu.make_async_copy(
            stage_ref.at[pl.ds(pl.multiple_of(step * block + t * PIECE, PIECE), PIECE)],
            out_ref.at[src_ref[4 * step + t]],
            sem_ref.at[4 * step + t],
        ).start()
    pieces = jnp.concatenate(
        [
            jnp.sum(back, axis=0, keepdims=True),
            jnp.sum(back * hat_rows, axis=0, keepdims=True),
            bias[0],
            bias[2],
            jnp.zeros((4, features), f32),
        ],
        axis=0,
    )

    @pl.when(step == 0)
    def _():
        vec_ref[...] = pieces

    @pl.when(step > 0)
    def _():
        vec_ref[...] += pieces

    @pl.when(step == pl.num_programs(0) - 1)
    def _():
        for k in range(sem_ref.shape[0]):
            pltpu.make_async_copy(
                stage_ref.at[pl.ds(k * PIECE, PIECE)], out_ref.at[src_ref[k]], sem_ref.at[k]
            ).wait()


def qkv_backward(src, grads, w_qkv, x_rows, gres, mod):
    rows, features = x_rows.shape
    block = 4 * PIECE
    rows_spec = pl.BlockSpec((block, features), lambda i, src: (i, 0))
    grad_specs = [pl.BlockSpec((3, block, g.shape[2]), lambda i, src: (0, i, 0)) for g in grads]
    return pl.pallas_call(
        qkv_back_kernel,
        grid_spec=pltpu.PrefetchScalarGridSpec(
            num_scalar_prefetch=1,
            grid=(rows // block,),
            in_specs=grad_specs + [whole(w_qkv.shape), rows_spec, rows_spec, whole(mod.shape)],
            out_specs=[
                pl.BlockSpec(memory_space=pl.ANY),
                pl.BlockSpec((8, features), lambda i, src: (0, 0)),
            ],
            scratch_shapes=[
                pltpu.VMEM((rows, features), bf16),
                pltpu.SemaphoreType.DMA((rows // PIECE,)),
            ],
        ),
        out_shape=[
            jax.ShapeDtypeStruct((rows // PIECE, PIECE, features), bf16),
            jax.ShapeDtypeStruct((8, features), f32),
        ],
        name="qkv_backward",
        compiler_params=params(),
        cost_estimate=cost(14),
    )(src, *grads, w_qkv, x_rows, gres, mod)


def assemble_kernel(places, counts, core_ref, *refs):
    ins = refs[: 2 * len(counts)]
    outs = refs[2 * len(counts) :]
    swap = core_ref[0] == 1
    at = 0
    for k, count in enumerate(counts):
        for m in range(count):
            pair = pick(swap, ins[2 * k][m], ins[2 * k + 1][m])
            for tile, (out, row, col) in zip(pair, places[at]):
                outs[out][row * LANES : (row + 1) * LANES, col * LANES : (col + 1) * LANES] = tile.astype(f32)
            at += 1


def assemble(core, pairs, places, shapes):
    flat = [array for pair in pairs for array in pair]
    return pl.pallas_call(
        functools.partial(assemble_kernel, places, [own.shape[0] for own, unused in pairs]),
        grid_spec=pltpu.PrefetchScalarGridSpec(
            num_scalar_prefetch=1,
            grid=(1,),
            in_specs=[whole(array.shape) for array in flat],
            out_specs=[whole(shape) for shape in shapes],
        ),
        out_shape=[jax.ShapeDtypeStruct(shape, f32) for shape in shapes],
        name="assemble",
        compiler_params=params(),
        cost_estimate=cost(5),
    )(core, *flat)


def flip(axis, bit):
    size = lax.axis_size(axis)
    return [(i, i ^ (1 << bit)) for i in range(size)]


def trade(array, axis, bit):
    return lax.ppermute(array, axis, flip(axis, bit))


def add_low(a, b):
    return (a.astype(f32) + b.astype(f32)).astype(bf16)


class Chain:
    def __init__(self, clip_bits, own, sends, stage=0):
        self.clip_bits = clip_bits
        self.own = own
        self.sends = sends
        self.stage = stage
        self.got = None

    def launch(self):
        if self.stage == 0 or self.stage == self.clip_bits + 2:
            axis, bit = "win", 0
        elif self.stage == self.clip_bits + 1:
            axis, bit = "win", 1
        else:
            axis, bit = "clip", self.stage - 1
        self.got = [trade(send, axis, bit) for send in self.sends]

    def prepare(self):
        self.stage += 1
        both = list(zip(self.own, self.got))
        if self.stage <= self.clip_bits:
            half = self.own[0].shape[0] // 2
            self.sends = [joined([add_low(o[half:], g[half:]) for o, g in both])]
            self.own = [joined([add_low(o[:half], g[:half]) for o, g in both])]
        elif self.stage == self.clip_bits + 1:
            self.own = self.sends = [joined([add_low(o, g) for o, g in both])]
        else:
            exact = [o.astype(f32) + g.astype(f32) for o, g in both]
            self.own = self.sends = [
                joined([lax.reduce_precision(e, 8, 7).astype(bf16) for e in exact])
            ]

    def finish(self):
        while self.stage < self.clip_bits + 2:
            boundary((), [self], [])
        return self.own[0][0], self.got[0][0]


def joined(arrays):
    return arrays[0] if len(arrays) == 1 else jnp.concatenate(arrays, axis=1)


def unite(*chains):
    first = chains[0]
    united = Chain(first.clip_bits, None, None, first.stage)
    united.own = [o for c in chains for o in c.own]
    united.got = [g for c in chains for g in c.got]
    return united


def boundary(inputs, moved, fresh, held=()):
    waited = moved + list(held)
    got = [c.got for c in waited]
    inputs, got = lax.optimization_barrier((inputs, got))
    for c, g in zip(waited, got):
        c.got = g
    for c in moved:
        c.prepare()
    chains = moved + fresh
    inputs, sends = lax.optimization_barrier((inputs, [c.sends for c in chains]))
    for c, sent in zip(chains, sends):
        c.sends = sent
        if c.own is not None and c.stage >= c.clip_bits + 1:
            c.own = sent
        c.launch()
    return inputs


def to_quadrants(slot_rows):
    local_slots = slot_rows.shape[0]
    channels = slot_rows.shape[-1]
    arranged = slot_rows.reshape(local_slots, 2, WST, 2, WST, channels).transpose(1, 3, 0, 2, 4, 5)
    return arranged.reshape(4, local_slots, PIECE, channels)


def from_quadrants(received):
    local_slots = received.shape[1]
    channels = received.shape[-1]
    arranged = received.reshape(2, 2, local_slots, WST, WST, channels).transpose(2, 0, 3, 1, 4, 5)
    return arranged.reshape(local_slots, 4 * PIECE, channels)


def exchange(quadrants):
    return lax.all_to_all(quadrants, "win", split_axis=0, concat_axis=0, tiled=True)


def local(
    tokens,
    condition,
    slot_order,
    rel_index,
    w_qkv,
    b_query,
    b_value,
    w_out,
    b_out,
    w_up,
    b_up,
    w_down,
    b_down,
    w_ada,
    b_ada,
    rel_table,
    grad_out,
):
    features = tokens.shape[-1]
    clips = lax.axis_size("clip")
    clip_bits = clips.bit_length() - 1
    me = lax.axis_index("clip")
    core = lax.axis_index("win") & 1
    ff = w_up.shape[1]
    fast = features // clips == LANES and ff // clips == FF_PARTS * LANES

    quadrants, rel_index = lax.optimization_barrier((to_quadrants(tokens[0]), rel_index))
    pieces = exchange(quadrants).reshape(-1, PIECE, features)
    grad_quadrants = to_quadrants(grad_out[0])
    slots = pieces.shape[0]
    per_frame = slots // FRAMES
    order_row = slot_order[0]
    window_place = jnp.arange(slots, dtype=jnp.int32)
    wanted = (window_place % FRAMES) * per_frame + window_place // FRAMES
    src = jnp.sum(
        jnp.where(order_row[None, :] == wanted[:, None], window_place[None, :], 0), axis=1
    ).astype(jnp.int32)
    windows = per_frame
    win = FRAMES * PIECE

    half = win // 2
    idx_mine = lax.dynamic_slice_in_dim(rel_index, core * half, half, 0)
    bias_mine = bias_gather(idx_mine, rel_table)
    lifted = jax.nn.silu(condition.astype(f32)).astype(bf16)
    modulation = jnp.dot(lifted, w_ada, preferred_element_type=f32)[0] + b_ada
    mod = jnp.concatenate([modulation.reshape(6, features), jnp.zeros((2, features), f32)])

    grad_quadrants, bias_mine, mod = lax.optimization_barrier((grad_quadrants, bias_mine, mod))
    grad_pieces = exchange(grad_quadrants).reshape(-1, PIECE, features)
    bias_other = trade(bias_mine, "win", 0)

    qkv_bias = jnp.concatenate([b_query, jnp.zeros_like(b_query), b_value]).astype(f32)[None]
    x_rows, normed, qkv = qkv_call(src, pieces, mod, qkv_bias, w_qkv)
    core_arr = core.astype(jnp.int32)[None]
    attended, probs, recips = attn_forward(core_arr, qkv, bias_mine, bias_other, windows)
    branch, normed_two, grad_mixed = out_call(
        src, grad_pieces, attended, x_rows, mod, b_out.astype(f32)[None], w_out
    )

    shards = features // LANES
    natural = jnp.arange(shards, dtype=jnp.int32)
    if fast:
        places = jnp.zeros_like(natural)
        for bit in range(clip_bits):
            places = places | (((natural >> (clip_bits - 1 - bit)) & 1) << bit)
        order = me ^ places
        inv = jnp.zeros_like(natural)
        for bit in range(clip_bits):
            inv = inv | ((((natural ^ me) >> (clip_bits - 1 - bit)) & 1) << bit)
        per_shard = ff // clips // LANES
        fos = [order * per_shard + j for j in range(FF_PARTS)]
        co = order[::2] & (clips // 2 - 1)
        upper = me >> (clip_bits - 1)
        flags = jnp.stack([core, (upper != core).astype(jnp.int32)]).astype(jnp.int32)
    else:
        inv = natural
        per_part = ff // LANES // FF_PARTS
        fos = [jnp.arange(per_part, dtype=jnp.int32) + j * per_part for j in range(FF_PARTS)]
        co = jnp.arange(per_part // 2, dtype=jnp.int32)
        flags = jnp.zeros((2,), jnp.int32)

    def chain(own, sends):
        return Chain(clip_bits, [own], [sends]) if fast else (own, sends)

    def meet(inputs, moved, fresh=(), held=()):
        return boundary(inputs, list(moved), list(fresh), list(held)) if fast else inputs

    def merge(*chains):
        return unite(*chains) if fast else chains

    b_up_rows = b_up.astype(f32).reshape(-1, 1, LANES)
    before, up_sums, ffs = [], [], []
    steps = [((), ()), ((), (0,)), ((0,), (1,)), ((0, 1), (2,))]
    for j in range(FF_PARTS):
        moved, fresh = steps[j]
        if j:
            normed_two, grad_mixed = meet(
                (normed_two, grad_mixed), [ffs[k] for k in moved], [ffs[k] for k in fresh]
            )
        act, gh, own, other, sums = ff_part(
            j, fos[j], co, inv, flags, normed_two, grad_mixed, w_up, b_up_rows, w_down, before
        )
        before = [act, gh]
        up_sums.append(sums.reshape(-1, LANES))
        ffs.append(chain(own, other))
    act, gh = meet((act, gh), ffs[:3], [ffs[3]])
    mixed, back = ff_join(jnp.concatenate(fos), act, gh, w_up, w_down)
    mixed, back = meet((mixed, back), ffs[1:], held=ffs[:1])
    gres, early, grad_att, out_own, out_other, out_pieces = ff_rows(
        src, inv, flags, mixed, back, grad_pieces, x_rows, branch, mod, b_down.astype(f32)[None], w_out, attended
    )
    local_slots = tokens.shape[1]
    piece_shape = (-1, local_slots, PIECE, features)
    wos = chain(out_own, out_other)
    grad_att, out_pieces = meet((grad_att, out_pieces), ffs[2:], [wos], held=ffs[1:2])
    out_pieces = exchange(out_pieces.reshape(piece_shape))
    pairs = probs.shape[0]
    grads_a, mine_a, others_a = attn_backward(core_arr, qkv, attended, grad_att, probs, recips, windows, 0, FIRST_PAIRS)
    grads_a = meet(grads_a, [ffs[3], wos], held=ffs[2:3])
    qa_own, qa_other = qkv_weight(inv, flags, normed, grads_a)
    qas = chain(qa_own, qa_other)
    front = merge(*ffs[:3])
    grad_att, unused, out_pieces = meet((grad_att, qa_own, out_pieces), [wos, front], [qas], held=ffs[3:])
    others_a = trade(others_a, "win", 0)
    grads_b, mine_b, others_b = attn_backward(
        core_arr, qkv, attended, grad_att, probs, recips, windows, FIRST_PAIRS, pairs - FIRST_PAIRS
    )
    grads_b, others_a, others_b = meet((grads_b, others_a, others_b), [qas, wos])
    others_b = trade(others_b, "win", 0)
    qb_own, qb_other = qkv_weight(inv, flags, normed, grads_b)
    qbs = chain(qb_own, qb_other)

    rear = merge(ffs[3], wos)
    others_a, others_b, unused = meet((others_a, others_b, qb_own), [rear, front], [qbs])
    rel_sums = bucket_sums(idx_mine, [mine_a, mine_b], [others_a, others_b], rel_table.shape[0])

    if fast:
        here = natural[:, None] == order[None, :]
        up_sums = [jnp.sum(jnp.where(here[:, :, None], u[None], 0.0), axis=1) for u in up_sums]
    grad_b_up = jnp.stack(up_sums, axis=1 if fast else 0)
    d = features
    tile_rows = d // LANES
    wins = lax.axis_size("win")
    buckets, heads = rel_table.shape

    def to_all(to_each, by_clip):
        parts = [jnp.broadcast_to(v[None], (clips,) + v.shape) for v in to_each] + by_clip
        packed = jnp.concatenate(parts, axis=1).astype(bf16)
        packed = jnp.broadcast_to(packed[:, None], (clips, wins) + packed.shape[1:])
        packed = packed.reshape((clips * wins,) + packed.shape[2:])
        return lax.all_to_all(packed, ("clip", "win"), split_axis=0, concat_axis=0, tiled=True)

    def from_all(received):
        return jnp.sum(received.astype(f32).reshape((clips, wins) + received.shape[1:]), axis=1)

    if fast:
        early_vec = to_all(
            [early[:4].reshape(-1, LANES), lifted[0].astype(f32).reshape(-1, LANES)],
            [
                early[4].reshape(clips, 1, LANES),
                early[5].reshape(clips, 1, LANES),
                grad_b_up.reshape(clips, -1, LANES),
                rel_sums,
            ],
        )
    gres_late, unused = meet((gres, rel_sums), [rear, qas, qbs])
    home = lax.axis_index("win") if fast else 0
    src_back = (((src // local_slots) ^ home) * local_slots + src % local_slots).astype(jnp.int32)
    token_pieces, late = qkv_backward(src_back, (grads_a, grads_b), w_qkv, x_rows, gres_late, mod)
    token_pieces = token_pieces.reshape(piece_shape)
    if fast:
        token_parts = [token_pieces[k] for k in range(4)]
        token_parts, late, early_vec, out_pieces = meet(
            (token_parts, late, early_vec, out_pieces), [qbs, qas], held=[front, rear]
        )
        moves = [[(i, i ^ k) for i in range(wins)] for k in range(4)]
        far = [lax.ppermute(token_parts[k], "win", moves[k]) for k in (2, 3)]
        near = lax.ppermute(token_parts[1], "win", moves[1])
        late_vec = to_all(
            [late[:2].reshape(-1, LANES)],
            [late[2].reshape(clips, 1, LANES), late[3].reshape(clips, 1, LANES)],
        )
        near = boundary(near, [qbs], [])
        last = merge(qas, qbs)
        far, late_vec = boundary((far, late_vec), [last], [])
        (late_vec,) = boundary((late_vec,), [last], [])
        token_pieces = jnp.stack([token_parts[0], near] + far).reshape((2, 2) + token_parts[0].shape)
        for axis, bit in ((0, 1), (1, 0)):
            swapped = (home >> bit) & 1 == 1
            token_pieces = jnp.where(swapped, jnp.flip(token_pieces, axis), token_pieces)
        token_pieces = token_pieces.reshape(piece_shape)
        early_rows, late_rows = from_all(early_vec), from_all(late_vec)
        n = 4 * tile_rows
        early_terms = early_rows[:, :n].reshape(clips, 4 * d)
        late_terms = late_rows[:, : 2 * tile_rows].reshape(clips, 2 * d)
        all_lifted = early_rows[:, n : n + tile_rows].reshape(clips, d) * (1.0 / wins)
        n += tile_rows
        own = jnp.sum(early_rows[:, n:], axis=0)
        sum_bo, sum_bd, sum_bu = own[0], own[1], own[2 : 2 + ff // clips // LANES].reshape(-1)
        rel = own[2 + ff // clips // LANES :].reshape(2, heads, LANES)
        sum_rel = rel.transpose(0, 2, 1).reshape(buckets // clips, heads)
        own = jnp.sum(late_rows[:, 2 * tile_rows :], axis=0)
        sum_bq, sum_bv = own[0], own[1]
    else:
        token_pieces = exchange(token_pieces)

        def all_clips(rows):
            return lax.psum(lax.all_gather(rows.reshape(-1), "clip", axis=0), "win")

        def own_sum(vector):
            return lax.psum(lax.psum_scatter(vector, "clip", scatter_dimension=0, tiled=True), "win")

        early_terms, late_terms = all_clips(early[:4]), all_clips(late[:2])
        all_lifted = lax.all_gather(lifted[0].astype(f32), "clip", axis=0)
        sum_bo, sum_bd, sum_bu = own_sum(early[4]), own_sum(early[5]), own_sum(grad_b_up.reshape(-1))
        sum_bq, sum_bv = own_sum(late[2]), own_sum(late[3])
        rel = rel_sums.reshape(-1, 2, heads, LANES).transpose(0, 1, 3, 2).reshape(buckets, heads)
        sum_rel = own_sum(rel)
    all_terms = jnp.concatenate([late_terms, early_terms], axis=1)

    def own_block(vector):
        size = vector.shape[0] // clips
        return lax.dynamic_slice_in_dim(vector, me * size, size, 0)

    ada_rows = d // clips
    lifted_rows = lax.dynamic_slice_in_dim(all_lifted, me * ada_rows, ada_rows, 1)
    grad_w_ada = jnp.dot(lifted_rows.T, all_terms, precision=lax.Precision.HIGHEST)
    grad_b_ada = own_block(jnp.sum(all_terms, axis=0))

    rows = d // clips
    block_out = from_quadrants(out_pieces).reshape(tokens.shape)
    if fast:
        side = shards // 2
        places = []
        for j in range(FF_PARTS):
            places += [[(0, 0, (c * side + m) * FF_PARTS + j) for c in range(2)] for m in range(side)]
            places += [[(1, j, c * side + m) for c in range(2)] for m in range(side)]
        places += [[(2, 0, c * side + m) for c in range(2)] for m in range(side)]
        sum_wu, sum_wd, sum_wo = assemble(
            core_arr, [front.finish(), rear.finish()], places, [(rows, ff), (ff // clips, d), (rows, d)]
        )
        places, first = [], 0
        for count in (FIRST_PAIRS // 2, (pairs - FIRST_PAIRS) // 2):
            for part in range(3):
                places += [
                    [(0, 0, part * shards + first + c * count + m) for c in range(2)] for m in range(count)
                ]
            first += 2 * count
        (sum_qkv,) = assemble(core_arr, [last.finish()], places, [(rows, 3 * d)])
    else:

        def share(whole_grad):
            part = lax.psum_scatter(whole_grad.astype(f32), "clip", scatter_dimension=0, tiled=True)
            return lax.psum(part, "win")

        def flat_rows(blocks):
            return blocks.transpose(0, 2, 1, 3).reshape(d, -1, LANES)

        halves = len(ffs[0][0][0]) // 2
        ups = [jnp.stack([flat_rows(g[:, :halves]) for g in f], axis=2).reshape(d, -1) for f in ffs]
        sum_wu = share(jnp.concatenate(ups, axis=1))
        downs = [jnp.concatenate([flat_rows(g[:, halves:]).reshape(d, -1) for g in f], axis=1) for f in ffs]
        sum_wd = share(jnp.concatenate(downs, axis=0))
        sum_wo = share(jnp.concatenate([flat_rows(g).reshape(d, -1) for g in wos], axis=1))
        parts = [
            jnp.concatenate([flat_rows(g).reshape(d, 3, -1) for g in q], axis=2) for q in (qas, qbs)
        ]
        sum_qkv = share(jnp.concatenate(parts, axis=2).reshape(d, 3 * d))
    grad_tokens = from_quadrants(token_pieces).reshape(tokens.shape)
    return (
        block_out,
        grad_tokens,
        sum_qkv,
        sum_bq,
        sum_bv,
        sum_wo,
        sum_bo,
        sum_wu,
        sum_bu,
        sum_wd,
        sum_bd,
        grad_w_ada,
        grad_b_ada,
        sum_rel,
    )


def solution(mesh):
    placed = (
        P("clip", "win", None, None),
        P("clip", None),
        P("clip", None),
    ) + (P(),) * 13 + (P("clip", "win", None, None),)
    return jax.shard_map(
        local,
        mesh=mesh,
        in_specs=placed,
        out_specs=(
            P("clip", "win", None, None),
            P("clip", "win", None, None),
            P("clip", None),
            P("clip"),
            P("clip"),
            P("clip", None),
            P("clip"),
            P("clip", None),
            P("clip"),
            P("clip", None),
            P("clip"),
            P("clip", None),
            P("clip"),
            P("clip", None),
        ),
        check_vma=False,
    )
```

```python
import functools
import math

import jax
import jax.numpy as jnp
from jax import lax
from jax.experimental import pallas as pl
from jax.experimental.pallas import tpu as pltpu
from jax.sharding import PartitionSpec as P

HEAD = 64
FRAMES = 5
WST = 8
PIECE = WST * WST
UNIT = 256
FF_PARTS = 4
FF_UNITS = 4
FF_BLOCKS = 2
FIRST_PAIRS = 6
LANES = 128
VMEM_LIMIT = 60 * 1024 * 1024
f32 = jnp.float32
bf16 = jnp.bfloat16
GELU_C = math.sqrt(2.0 / math.pi)
GELU_A = 0.044715


def dot_nn(a, b):
    return jnp.dot(a, b, preferred_element_type=f32)


def dot_nt(a, b):
    return lax.dot_general(a, b, (((1,), (1,)), ((), ())), preferred_element_type=f32)


def dot_tn(a, b):
    return lax.dot_general(a, b, (((0,), (0,)), ((), ())), preferred_element_type=f32)


def params():
    return pltpu.CompilerParams(vmem_limit_bytes=VMEM_LIMIT)


def cost(micros):
    return pl.CostEstimate(
        flops=int(micros * 1.0e9), bytes_accessed=int(micros * 2.0e6), transcendentals=0
    )


def pick(swap, first, second):
    return jnp.where(swap, second, first), jnp.where(swap, first, second)


def hat_of(rows):
    average = jnp.mean(rows, axis=-1, keepdims=True)
    centered = rows - average
    variance = jnp.mean(centered * centered, axis=-1, keepdims=True)
    inv_std = lax.rsqrt(variance + 1e-06)
    return centered * inv_std, inv_std


def norm_back(grad_hat, hat_rows, inv_std):
    first_mean = jnp.mean(grad_hat, axis=-1, keepdims=True)
    second_mean = jnp.mean(grad_hat * hat_rows, axis=-1, keepdims=True)
    return inv_std * (grad_hat - first_mean - hat_rows * second_mean)


def whole(shape):
    zeros = (0,) * len(shape)
    return pl.BlockSpec(shape, lambda *unused: zeros, pipeline_mode=pl.Buffered(1))


def bias_kernel(idx_ref, tab_ref, out_ref, scr_ref):
    lows = lax.broadcasted_iota(jnp.int32, (256, idx_ref.shape[1]), 0)
    tab = tab_ref[...]
    half = tab.shape[0] // 2
    heads = 16
    tiles = idx_ref.shape[1] // LANES
    win = out_ref.shape[2] // 2
    for i in range(8):
        idx = idx_ref[pl.ds(i, 1), :]
        low = idx & 255
        high = idx >> 8
        onehot = jnp.where(lows == low, 1.0, 0.0).astype(bf16)
        got = dot_nn(tab, onehot)
        got = got[:half] + got[half:]
        acc = got[:heads]
        for c in range(1, half // heads):
            acc = jnp.where(high == c, got[c * heads : (c + 1) * heads], acc)
        for t in range(tiles):
            scr_ref[t, pl.ds(i, heads, stride=8), :] = acc[:, t * LANES : (t + 1) * LANES]
    for pair in range(heads // 2):
        rows = []
        for h in range(2):
            at = (2 * pair + h) * 8
            rows.append(
                jnp.concatenate([scr_ref[t, at : at + 8, :] for t in range(tiles)], axis=1)[:, :win]
            )
        out_ref[pair] = jnp.concatenate(rows, axis=1)


def bias_gather(idx, table):
    rows, win = idx.shape
    padded = -(-win // LANES) * LANES
    buckets, heads = table.shape
    upper_f = lax.reduce_precision(table, 8, 7)
    lower = (table - upper_f).astype(bf16)

    def arrange(t):
        return t.reshape(-1, 256, heads).transpose(0, 2, 1).reshape(-1, 256)

    tab = jnp.concatenate([arrange(upper_f.astype(bf16)), arrange(lower)], axis=0)
    idx = jnp.pad(idx, ((0, 0), (0, padded - win)))
    return pl.pallas_call(
        bias_kernel,
        grid=(rows // 8,),
        in_specs=[pl.BlockSpec((8, padded), lambda i: (i, 0)), whole(tab.shape)],
        out_specs=pl.BlockSpec((heads // 2, 8, 2 * win), lambda i: (0, i, 0)),
        out_shape=jax.ShapeDtypeStruct((heads // 2, rows, 2 * win), f32),
        scratch_shapes=[pltpu.VMEM((padded // LANES, 8 * heads, LANES), f32)],
        name="bias_gather",
        compiler_params=params(),
        cost_estimate=cost(0.9),
    )(idx, tab)


def bucket_kernel(idx_ref, *refs):
    out_ref, acc_ref, scr_ref = refs[-3:]
    keep_refs = refs[: (len(refs) - 3) // 2]
    got_refs = refs[(len(refs) - 3) // 2 : -3]

    @pl.when(pl.program_id(0) == 0)
    def _():
        acc_ref[...] = jnp.zeros_like(acc_ref)

    padded = idx_ref.shape[1]
    tiles = padded // LANES
    keeps = [(r, k) for r in keep_refs for k in range(r.shape[0])]
    gots = [(r, k) for r in got_refs for k in range(r.shape[0])]
    pairs = len(keeps)
    heads = 2 * pairs
    win = keep_refs[0].shape[2] // 2
    step_rows = idx_ref.shape[0]
    lows = lax.broadcasted_iota(jnp.int32, (256, padded), 0)
    zero = jnp.zeros((step_rows, padded - win), f32)
    for pair in range(pairs):
        (keep_ref, k), (got_ref, unused) = keeps[pair], gots[pair]
        sums = keep_ref[k].astype(f32) + got_ref[k].astype(f32)
        for h in range(2):
            part = jnp.concatenate([sums[:, h * win : (h + 1) * win], zero], axis=1)
            at = (2 * pair + h) * step_rows
            for t in range(tiles):
                scr_ref[t, at : at + step_rows, :] = part[:, t * LANES : (t + 1) * LANES]
    total = acc_ref[...]
    for i in range(step_rows):
        idx = idx_ref[pl.ds(i, 1), :]
        low = idx & 255
        high = idx >> 8
        onehot = jnp.where(lows == low, 1.0, 0.0).astype(bf16)
        sums = jnp.concatenate(
            [scr_ref[t, pl.ds(i, heads, stride=step_rows), :] for t in range(tiles)], axis=1
        )
        spread = jnp.concatenate(
            [jnp.where(high == c, sums, 0.0) for c in range(acc_ref.shape[0] // heads)], axis=0
        )
        total += dot_nt(spread.astype(bf16), onehot)
    acc_ref[...] = total

    @pl.when(pl.program_id(0) == pl.num_programs(0) - 1)
    def _():
        for k in range(out_ref.shape[0]):
            for t in range(2):
                out_ref[k, t * heads : (t + 1) * heads] = total[
                    k * heads : (k + 1) * heads, t * LANES : (t + 1) * LANES
                ]


def bucket_sums(idx, keeps, gots, buckets):
    rows, win = idx.shape
    padded = -(-win // LANES) * LANES
    heads = 2 * sum(k.shape[0] for k in keeps)
    step_rows = 16
    idx = jnp.pad(idx, ((0, 0), (0, padded - win)))
    out_rows = buckets // 256
    sum_specs = [pl.BlockSpec((k.shape[0], step_rows, 2 * win), lambda i: (0, i, 0)) for k in keeps]
    out_shape = jax.ShapeDtypeStruct((out_rows, 2 * heads, LANES), f32)
    return pl.pallas_call(
        bucket_kernel,
        grid=(rows // step_rows,),
        in_specs=[pl.BlockSpec((step_rows, padded), lambda i: (i, 0))] + sum_specs + sum_specs,
        out_specs=pl.BlockSpec(out_shape.shape, lambda i: (0, 0, 0)),
        out_shape=out_shape,
        scratch_shapes=[
            pltpu.VMEM((out_rows * heads, 256), f32),
            pltpu.VMEM((padded // LANES, step_rows * heads, LANES), f32),
        ],
        name="bucket_sums",
        compiler_params=params(),
        cost_estimate=cost(4),
    )(idx, *keeps, *gots)


def qkv_kernel(src_ref, a_ref, b_ref, c_ref, d_ref, mod_ref, bias_ref, w_ref, x_ref, n_ref, o_ref):
    rows = jnp.concatenate([r[0] for r in (a_ref, b_ref, c_ref, d_ref)], axis=0)
    x_ref[...] = rows
    hat_rows, unused = hat_of(rows.astype(f32))
    normed = (hat_rows * (1.0 + mod_ref[1:2, :]) + mod_ref[0:1, :]).astype(bf16)
    n_ref[...] = normed
    features = rows.shape[1]
    for j in range(w_ref.shape[1] // 512):
        cols = slice(j * 512, (j + 1) * 512)
        got = dot_nn(normed, w_ref[:, cols]) + bias_ref[0:1, cols]
        if (j + 1) * 512 <= features:
            got = got.astype(bf16).astype(f32) * (1.0 / math.sqrt(HEAD))
        o_ref[:, cols] = got.astype(bf16)


def slot_spec(features, t):
    return pl.BlockSpec((1, PIECE, features), lambda i, src, t=t: (src[4 * i + t], 0, 0))


def qkv_call(src, pieces, mod, qkv_bias, w_qkv):
    count, unused, features = pieces.shape
    rows = count * PIECE
    wide = w_qkv.shape[1]
    block = 4 * PIECE
    return pl.pallas_call(
        qkv_kernel,
        grid_spec=pltpu.PrefetchScalarGridSpec(
            num_scalar_prefetch=1,
            grid=(count // 4,),
            in_specs=[slot_spec(features, t) for t in range(4)]
            + [whole(mod.shape), whole(qkv_bias.shape), whole(w_qkv.shape)],
            out_specs=[
                pl.BlockSpec((block, features), lambda i, src: (i, 0)),
                pl.BlockSpec((block, features), lambda i, src: (i, 0)),
                pl.BlockSpec((block, wide), lambda i, src: (i, 0)),
            ],
        ),
        out_shape=[
            jax.ShapeDtypeStruct((rows, features), bf16),
            jax.ShapeDtypeStruct((rows, features), bf16),
            jax.ShapeDtypeStruct((rows, wide), bf16),
        ],
        name="norm_qkv",
        compiler_params=params(),
        cost_estimate=cost(0.6),
    )(src, pieces, pieces, pieces, pieces, mod, qkv_bias, w_qkv)


def split_pair(x, left):
    zero = jnp.zeros_like(x)
    return jnp.concatenate([jnp.where(left, x, zero), jnp.where(left, zero, x)], axis=0)


def values_ones(v, left):
    one = jnp.ones_like(v)
    zero = jnp.zeros_like(v)
    marks = jnp.concatenate([jnp.where(left, one, zero), jnp.where(left, zero, one)], axis=0)
    return jnp.concatenate([split_pair(v, left), marks], axis=1)


def attn_kernel(windows, core_ref, q_ref, k_ref, v_ref, mine_ref, other_ref, o_ref, p_ref, r_ref, b_ref):
    win = q_ref.shape[0] // windows
    half = win // 2
    left = lax.broadcasted_iota(jnp.int32, (win, LANES), 1) < HEAD
    first = core_ref[0] == 0
    b_ref[:half] = jnp.where(first, mine_ref[0], other_ref[0])
    b_ref[half:] = jnp.where(first, other_ref[0], mine_ref[0])
    lowest = jnp.float32(-jnp.inf)
    whole_tiles = win // LANES * LANES
    for u in range(windows):
        rows = slice(u * win, (u + 1) * win)
        keys = split_pair(k_ref[rows], left)
        vals = values_ones(v_ref[rows], left)
        s = dot_nt(q_ref[rows], keys) + b_ref[...]
        lo = s[:, :whole_tiles]
        mid = s[:, whole_tiles : whole_tiles + LANES]
        hi = s[:, whole_tiles + LANES :]
        top_lo = jnp.where(left, mid, lowest)
        top_hi = jnp.where(left, lowest, mid)
        for t in range(whole_tiles // LANES):
            cols = slice(t * LANES, (t + 1) * LANES)
            top_lo = jnp.maximum(top_lo, lo[:, cols])
            top_hi = jnp.maximum(top_hi, hi[:, cols])
        top_lo = jnp.max(top_lo, axis=1, keepdims=True)
        top_hi = jnp.max(top_hi, axis=1, keepdims=True)
        e = jnp.concatenate(
            [
                jnp.exp(lo - top_lo),
                jnp.exp(mid - jnp.where(left, top_lo, top_hi)),
                jnp.exp(hi - top_hi),
            ],
            axis=1,
        ).astype(bf16)
        p_ref[0, u] = e
        got = dot_nn(e, vals)
        r = 1.0 / got[:, LANES:]
        r_ref[rows] = r
        o_ref[rows] = (got[:, :LANES] * r).astype(bf16)


def attn_forward(core, qkv, bias_mine, bias_other, windows):
    rows = qkv.shape[0]
    win = rows // windows
    pairs = bias_mine.shape[0]
    features = qkv.shape[1] // 3

    def col(part):
        return pl.BlockSpec((rows, LANES), lambda h, c, part=part: (0, part * pairs + h))

    half_spec = pl.BlockSpec((1, win // 2, 2 * win), lambda h, c: (h, 0, 0))
    return pl.pallas_call(
        functools.partial(attn_kernel, windows),
        grid_spec=pltpu.PrefetchScalarGridSpec(
            num_scalar_prefetch=1,
            grid=(pairs,),
            in_specs=[col(0), col(1), col(2), half_spec, half_spec],
            out_specs=[
                col(0),
                pl.BlockSpec((1, windows, win, 2 * win), lambda h, c: (h, 0, 0, 0)),
                col(0),
            ],
            scratch_shapes=[pltpu.VMEM((win, 2 * win), f32)],
        ),
        out_shape=[
            jax.ShapeDtypeStruct((rows, features), bf16),
            jax.ShapeDtypeStruct((pairs, windows, win, 2 * win), bf16),
            jax.ShapeDtypeStruct((rows, features), f32),
        ],
        name="attn_forward",
        compiler_params=params(),
        cost_estimate=cost(0.9),
    )(core, qkv, qkv, qkv, bias_mine, bias_other)


def fold_delta(dx, lane):
    lower_half = (lane & 32) == 0
    dx = dx + jnp.where(lower_half, pltpu.roll(dx, LANES - 32, 1), pltpu.roll(dx, 32, 1))
    upper = dx.astype(bf16)
    lower = (dx - upper.astype(f32)).astype(bf16)
    return jnp.where(lower_half, upper, lower)


def attn_back_kernel(windows, core_ref, q_ref, k_ref, v_ref, o_ref, do_ref, p_ref, r_ref, g_ref, mine_ref, other_ref):
    win = q_ref.shape[0] // windows
    lane = lax.broadcasted_iota(jnp.int32, (win, LANES), 1)
    left = lane < HEAD
    sums = None
    for u in range(windows):
        rows = slice(u * win, (u + 1) * win)
        keys = split_pair(k_ref[rows], left)
        vals = values_ones(v_ref[rows], left)
        up = (do_ref[rows].astype(f32) * r_ref[rows]).astype(bf16)
        delta = fold_delta(-(up.astype(f32) * o_ref[rows].astype(f32)), lane)
        d = dot_nt(jnp.concatenate([up, delta], axis=1), vals)
        p = p_ref[0, u]
        ds = p.astype(f32) * d
        sums = ds if sums is None else sums + ds
        low = ds.astype(bf16)
        g_ref[0, rows] = (dot_nn(low, keys) * (1.0 / math.sqrt(HEAD))).astype(bf16)
        dk = dot_tn(low, q_ref[rows])
        g_ref[1, rows] = jnp.where(left, dk[:win], dk[win:]).astype(bf16)
        dv = dot_tn(p, up)
        g_ref[2, rows] = jnp.where(left, dv[:win], dv[win:]).astype(bf16)
    half = win // 2
    first, second = sums[:half].astype(bf16), sums[half:].astype(bf16)
    mine_ref[0], other_ref[0] = pick(core_ref[0] == 1, first, second)


def attn_backward(core, qkv, attended, grad_att, probs, recips, windows, first, count):
    rows = qkv.shape[0]
    win = rows // windows
    pairs = probs.shape[0]

    def col(part):
        return pl.BlockSpec((rows, LANES), lambda h, core, part=part: (0, part * pairs + first + h))

    half_spec = pl.BlockSpec((1, win // 2, 2 * win), lambda h, core: (h, 0, 0))
    half_shape = jax.ShapeDtypeStruct((count, win // 2, 2 * win), bf16)
    return pl.pallas_call(
        functools.partial(attn_back_kernel, windows),
        grid_spec=pltpu.PrefetchScalarGridSpec(
            num_scalar_prefetch=1,
            grid=(count,),
            in_specs=[
                col(0),
                col(1),
                col(2),
                col(0),
                col(0),
                pl.BlockSpec((1, windows, win, 2 * win), lambda h, core: (first + h, 0, 0, 0)),
                col(0),
            ],
            out_specs=[
                pl.BlockSpec((3, rows, LANES), lambda h, core: (0, 0, h)),
                half_spec,
                half_spec,
            ],
        ),
        out_shape=[jax.ShapeDtypeStruct((3, rows, count * LANES), bf16), half_shape, half_shape],
        name="attn_backward",
        compiler_params=params(),
        cost_estimate=cost(3 * count),
    )(core, qkv, qkv, qkv, attended, grad_att, probs, recips)


def out_kernel(src_ref, a_ref, b_ref, c_ref, d_ref, att_ref, x_ref, mod_ref, bo_ref, w_ref, branch_ref, n_ref, gm_ref):
    branch = (dot_nn(att_ref[...], w_ref[...]) + bo_ref[...]).astype(bf16)
    branch_ref[...] = branch
    residual = x_ref[...].astype(f32) + mod_ref[2:3, :] * branch.astype(f32)
    hat_rows, unused = hat_of(residual)
    n_ref[...] = (hat_rows * (1.0 + mod_ref[4:5, :]) + mod_ref[3:4, :]).astype(bf16)
    up = jnp.concatenate([r[0] for r in (a_ref, b_ref, c_ref, d_ref)], axis=0)
    gm_ref[...] = (mod_ref[5:6, :] * up.astype(f32)).astype(bf16)


def out_call(src, pieces, attended, x_rows, mod, b_out, w_out):
    count, unused, features = pieces.shape
    rows = count * PIECE
    block = 4 * PIECE
    rows_spec = pl.BlockSpec((block, features), lambda i, src: (i, 0))
    sds = jax.ShapeDtypeStruct((rows, features), bf16)
    return pl.pallas_call(
        out_kernel,
        grid_spec=pltpu.PrefetchScalarGridSpec(
            num_scalar_prefetch=1,
            grid=(count // 4,),
            in_specs=[slot_spec(features, t) for t in range(4)]
            + [rows_spec, rows_spec, whole(mod.shape), whole(b_out.shape), whole(w_out.shape)],
            out_specs=[rows_spec, rows_spec, rows_spec],
        ),
        out_shape=[sds, sds, sds],
        name="out_norm",
        compiler_params=params(),
        cost_estimate=cost(0.3),
    )(src, pieces, pieces, pieces, pieces, attended, x_rows, mod, b_out, w_out)


def place_rows(inv_ref, out_ref, values):
    for k in range(out_ref.shape[0]):
        at = inv_ref[k]
        for m in range(out_ref.shape[1]):
            out_ref[at, m] = values[k * LANES : (k + 1) * LANES, m * LANES : (m + 1) * LANES]


def ff_part_kernel(count, fo_ref, co_ref, inv_ref, flag_ref, n_ref, gm_ref, *refs):
    ups = refs[:count]
    biases = refs[count : 2 * count]
    downs = refs[2 * count : 3 * count]
    act_ref, gh_ref, own_ref, other_ref, sum_ref = refs[-5:]
    step = pl.program_id(0)
    rows = n_ref.shape[0]
    block = rows // FF_BLOCKS
    wu = jnp.concatenate([r[...] for r in ups], axis=1)
    wd = jnp.concatenate([r[...] for r in downs], axis=0)
    bias = jnp.concatenate([r[0] for r in biases], axis=1)
    sums = None
    for c in range(FF_BLOCKS):
        part = slice(c * block, (c + 1) * block)
        v = dot_nn(n_ref[part], wu) + bias
        v2 = v * v
        t = jnp.tanh(v * (GELU_C + (GELU_C * GELU_A) * v2))
        h = 0.5 + 0.5 * t
        slope = h + (0.5 * v) * (1.0 - t * t) * (GELU_C + (3.0 * GELU_C * GELU_A) * v2)
        gh = (dot_nt(gm_ref[part], wd) * slope).astype(bf16)
        act_ref[0, part] = (v * h).astype(bf16)
        gh_ref[0, part] = gh
        piece = jnp.sum(gh.astype(f32), axis=0, keepdims=True)
        sums = piece if sums is None else sums + piece
    sum_ref[0] = sums
    up = dot_tn(n_ref[...], gh_ref[0]).astype(bf16)
    down = dot_tn(act_ref[0], gm_ref[...]).astype(bf16)
    half = down.shape[1] // 2
    blocks = half // LANES
    for p in range(count // 2):
        left = up[:, 2 * p * LANES : (2 * p + 1) * LANES]
        right = up[:, (2 * p + 1) * LANES : (2 * p + 2) * LANES]
        own, other = pick(flag_ref[1] == 1, left, right)
        col = co_ref[step * (count // 2) + p]
        for k in range(own_ref.shape[0]):
            at = inv_ref[k]
            own_ref[at, col] = own[k * LANES : (k + 1) * LANES]
            other_ref[at, col] = other[k * LANES : (k + 1) * LANES]
    own, other = pick(flag_ref[0] == 1, down[:, :half], down[:, half:])
    first = own_ref.shape[1] - blocks
    for k in range(count):
        for m in range(blocks):
            tile = (slice(k * LANES, (k + 1) * LANES), slice(m * LANES, (m + 1) * LANES))
            own_ref[step * count + k, first + m] = own[tile]
            other_ref[step * count + k, first + m] = other[tile]


def ff_part(j, fo, co, inv, flags, normed, grad_mixed, w_up, b_up, w_down, before):
    units = fo.shape[0]
    count = FF_UNITS
    steps = units // count
    rows, features = normed.shape

    def up(k):
        return pl.BlockSpec((features, LANES), lambda i, fo, *more: (0, fo[count * i + k]))

    def bias(k):
        return pl.BlockSpec((1, 1, LANES), lambda i, fo, *more: (fo[count * i + k], 0, 0))

    def down(k):
        return pl.BlockSpec((LANES, features), lambda i, fo, *more: (fo[count * i + k], 0))

    cols = pl.BlockSpec((1, rows, count * LANES), lambda i, *more: (j, 0, i))
    hidden = jax.ShapeDtypeStruct((FF_PARTS, rows, units * LANES), bf16)
    blocks = units // 2 + features // 2 // LANES
    grad = jax.ShapeDtypeStruct((units, blocks, LANES, LANES), bf16)
    ks = range(count)
    at = 4 + 2 + 3 * count
    return pl.pallas_call(
        functools.partial(ff_part_kernel, count),
        grid_spec=pltpu.PrefetchScalarGridSpec(
            num_scalar_prefetch=4,
            grid=(steps,),
            in_specs=[whole(normed.shape), whole(normed.shape)]
            + [up(k) for k in ks]
            + [bias(k) for k in ks]
            + [down(k) for k in ks]
            + [pl.BlockSpec(memory_space=pl.ANY)] * len(before),
            out_specs=[cols, cols, whole(grad.shape), whole(grad.shape)]
            + [pl.BlockSpec((1, 1, count * LANES), lambda i, *more: (i, 0, 0))],
        ),
        out_shape=[hidden, hidden, grad, grad, jax.ShapeDtypeStruct((steps, 1, count * LANES), f32)],
        input_output_aliases={at: 0, at + 1: 1} if before else {},
        name="ff_part",
        compiler_params=params(),
        cost_estimate=cost(20),
    )(fo, co, inv, flags, normed, grad_mixed, *[w_up] * count, *[b_up] * count, *[w_down] * count, *before)


def ff_join_kernel(units, fo_ref, act_ref, gh_ref, *refs):
    up_refs = refs[:units]
    down_refs = refs[units : 2 * units]
    mixed_ref, back_ref = refs[2 * units :]

    @pl.when(pl.program_id(0) == 0)
    def _():
        mixed_ref[...] = jnp.zeros_like(mixed_ref)
        back_ref[...] = jnp.zeros_like(back_ref)

    wd = jnp.concatenate([r[...] for r in down_refs], axis=0)
    wu = jnp.concatenate([r[...] for r in up_refs], axis=1)
    half = mixed_ref.shape[0] // 2
    for k in range(2):
        part = slice(k * half, (k + 1) * half)
        mixed_ref[part] += dot_nn(act_ref[0, part], wd)
        back_ref[part] += dot_nt(gh_ref[0, part], wu)


def ff_join(fo, act, gh, w_up, w_down):
    parts, rows, wide = act.shape
    units = wide // LANES
    features = w_up.shape[0]
    ups = [
        pl.BlockSpec((features, LANES), lambda i, fo, u=u: (0, fo[i * units + u])) for u in range(units)
    ]
    downs = [
        pl.BlockSpec((LANES, features), lambda i, fo, u=u: (fo[i * units + u], 0)) for u in range(units)
    ]
    hidden = pl.BlockSpec((1, rows, wide), lambda i, fo: (i, 0, 0))
    sums = jax.ShapeDtypeStruct((rows, features), f32)
    return pl.pallas_call(
        functools.partial(ff_join_kernel, units),
        grid_spec=pltpu.PrefetchScalarGridSpec(
            num_scalar_prefetch=1,
            grid=(parts,),
            in_specs=[hidden, hidden] + ups + downs,
            out_specs=[whole(sums.shape), whole(sums.shape)],
        ),
        out_shape=[sums, sums],
        name="ff_join",
        compiler_params=params(),
        cost_estimate=cost(28),
    )(fo, act, gh, *([w_up] * units), *([w_down] * units))


def ff_rows_kernel(blocks, src_ref, inv_ref, flag_ref, mixed_ref, back_ref, *refs):
    a_ref, b_ref, c_ref, d_ref, x_ref, branch_ref, mod_ref, bd_ref, wo_ref, att_ref = refs[:10]
    gres_ref, vec_ref, do_ref, own_ref, other_ref, out_ref = refs[10:16]
    stage_ref, gb_ref, sem_ref = refs[16:]
    step = pl.program_id(0)

    @pl.when(step < blocks)
    def _():
        e = step
        block = 4 * PIECE
        part = pl.ds(pl.multiple_of(e * block, block), block)
        mixed = mixed_ref[...] + bd_ref[...]
        back = back_ref[...]
        branch = branch_ref[...].astype(f32)
        gate_one = mod_ref[2:3, :]
        gate_two = mod_ref[5:6, :]
        residual = x_ref[...].astype(f32) + gate_one * branch
        hat_rows, inv_std = hat_of(residual)
        up = jnp.concatenate([r[0] for r in (a_ref, b_ref, c_ref, d_ref)], axis=0).astype(f32)
        stage_ref[part] = (residual + gate_two * mixed).astype(bf16)
        for t in range(4):
            pltpu.make_async_copy(
                stage_ref.at[pl.ds(pl.multiple_of(e * block + t * PIECE, PIECE), PIECE)],
                out_ref.at[src_ref[4 * e + t]],
                sem_ref.at[4 * e + t],
            ).start()
        gres = up + norm_back(back * (1.0 + mod_ref[4:5, :]), hat_rows, inv_std)
        gres_ref[...] = gres.astype(bf16)
        low = (gate_one * gres).astype(bf16)
        gb_ref[part] = low
        do_ref[...] = dot_nt(low, wo_ref[...]).astype(bf16)
        grad_mixed = (gate_two * up).astype(bf16).astype(f32)

        def total(values):
            return jnp.sum(values, axis=0, keepdims=True)

        pieces = jnp.concatenate(
            [
                total(gres * branch),
                total(back),
                total(back * hat_rows),
                total(up * mixed),
                total(low.astype(f32)),
                total(grad_mixed),
                jnp.zeros((2, gate_one.shape[1]), f32),
            ],
            axis=0,
        )

        @pl.when(e == 0)
        def _():
            vec_ref[...] = pieces

        @pl.when(e > 0)
        def _():
            vec_ref[...] += pieces

    @pl.when(step >= blocks)
    def _():
        width = own_ref.shape[1] * LANES
        half = gb_ref.shape[1] // 2
        flag = flag_ref[0]
        for grad_ref, side in ((own_ref, flag), (other_ref, 1 - flag)):
            start = pl.multiple_of(side * half + (step - blocks) * width, width)
            got = dot_tn(att_ref[...], gb_ref[:, pl.ds(start, width)])
            place_rows(inv_ref, grad_ref, got.astype(bf16))

    @pl.when(step == pl.num_programs(0) - 1)
    def _():
        for k in range(sem_ref.shape[0]):
            pltpu.make_async_copy(
                stage_ref.at[pl.ds(k * PIECE, PIECE)], out_ref.at[src_ref[k]], sem_ref.at[k]
            ).wait()


def ff_rows(src, inv, flags, mixed, back, pieces, x_rows, branch, mod, b_down, w_out, attended):
    rows, features = x_rows.shape
    shards = features // LANES
    block = 4 * PIECE
    blocks = rows // block
    ends = features // 2 // UNIT

    def at(i):
        return jnp.minimum(i, blocks - 1)

    rows_spec = pl.BlockSpec((block, features), lambda i, *more: (at(i), 0))
    slots = [
        pl.BlockSpec((1, PIECE, features), lambda i, src, *more, t=t: (src[4 * at(i) + t], 0, 0))
        for t in range(4)
    ]
    grad_spec = pl.BlockSpec(
        (shards, UNIT // LANES, LANES, LANES), lambda i, *more: (0, jnp.maximum(i - blocks, 0), 0, 0)
    )
    grad = jax.ShapeDtypeStruct((shards, features // 2 // LANES, LANES, LANES), bf16)
    rows_shape = jax.ShapeDtypeStruct((rows, features), bf16)
    return pl.pallas_call(
        functools.partial(ff_rows_kernel, blocks),
        grid_spec=pltpu.PrefetchScalarGridSpec(
            num_scalar_prefetch=3,
            grid=(blocks + ends,),
            in_specs=[rows_spec, rows_spec]
            + slots
            + [rows_spec, rows_spec, whole(mod.shape), whole(b_down.shape)]
            + [whole(w_out.shape), whole(attended.shape)],
            out_specs=[
                rows_spec,
                pl.BlockSpec((8, features), lambda i, *more: (0, 0)),
                rows_spec,
                grad_spec,
                grad_spec,
                pl.BlockSpec(memory_space=pl.ANY),
            ],
            scratch_shapes=[
                pltpu.VMEM((rows, features), bf16),
                pltpu.VMEM((rows, features), bf16),
                pltpu.SemaphoreType.DMA((rows // PIECE,)),
            ],
        ),
        out_shape=[
            rows_shape,
            jax.ShapeDtypeStruct((8, features), f32),
            rows_shape,
            grad,
            grad,
            jax.ShapeDtypeStruct(pieces.shape, bf16),
        ],
        name="ff_rows",
        compiler_params=params(),
        cost_estimate=cost(22),
    )(src, inv, flags, mixed, back, *([pieces] * 4), x_rows, branch, mod, b_down, w_out, attended)


def qkv_weight_kernel(inv_ref, flag_ref, n_ref, grad_ref, g0_ref, g1_ref):
    got = dot_tn(n_ref[...], grad_ref[0]).astype(bf16)
    half = got.shape[1] // 2
    own, other = pick(flag_ref[0] == 1, got[:, :half], got[:, half:])
    place_rows(inv_ref, g0_ref, own)
    place_rows(inv_ref, g1_ref, other)


def qkv_weight(inv, flags, normed, grads):
    rows, features = normed.shape
    parts, unused, wide = grads.shape
    shards = features // LANES
    tiles = wide // 2 // LANES
    out_spec = pl.BlockSpec((shards, tiles, LANES, LANES), lambda i, *more: (0, i, 0, 0))
    grad = jax.ShapeDtypeStruct((shards, parts * tiles, LANES, LANES), bf16)
    return pl.pallas_call(
        qkv_weight_kernel,
        grid_spec=pltpu.PrefetchScalarGridSpec(
            num_scalar_prefetch=2,
            grid=(parts,),
            in_specs=[
                whole(normed.shape),
                pl.BlockSpec((1, rows, wide), lambda i, *more: (i, 0, 0)),
            ],
            out_specs=[out_spec, out_spec],
        ),
        out_shape=[grad, grad],
        name="qkv_weight",
        compiler_params=params(),
        cost_estimate=cost(6),
    )(inv, flags, normed, grads)


def qkv_back_kernel(src_ref, *refs):
    count = len(refs) - 11
    grads = refs[:count]
    w_ref, x_ref, gres_ref, mod_ref = refs[count : count + 4]
    out_refs = refs[count + 4 : count + 8]
    vec_ref, stage_ref, sem_ref = refs[count + 8 :]
    per = out_refs[0].shape[0]
    step = pl.program_id(0)
    block = x_ref.shape[0]
    features = x_ref.shape[1]
    back = None
    bias = []
    for part in range(3):
        joined = jnp.concatenate([g[part] for g in grads], axis=1)
        bias.append(jnp.sum(joined.astype(f32), axis=0, keepdims=True))
        got = dot_nt(joined, w_ref[:, part * features : (part + 1) * features])
        back = got if back is None else back + got
    back = back.astype(bf16).astype(f32)
    hat_rows, inv_std = hat_of(x_ref[...].astype(f32))
    grad = gres_ref[...].astype(f32) + norm_back(back * (1.0 + mod_ref[1:2, :]), hat_rows, inv_std)
    stage_ref[pl.ds(pl.multiple_of(step * block, block), block)] = grad.astype(bf16)
    for t in range(4):
        slot = src_ref[4 * step + t]
        for k in range(4):

            @pl.when(slot // per == k)
            def _(k=k, t=t, slot=slot):
                pltpu.make_async_copy(
                    stage_ref.at[pl.ds(pl.multiple_of(step * block + t * PIECE, PIECE), PIECE)],
                    out_refs[k].at[slot - k * per],
                    sem_ref.at[4 * step + t],
                ).start()
    pieces = jnp.concatenate(
        [
            jnp.sum(back, axis=0, keepdims=True),
            jnp.sum(back * hat_rows, axis=0, keepdims=True),
            bias[0],
            bias[2],
            jnp.zeros((4, features), f32),
        ],
        axis=0,
    )

    @pl.when(step == 0)
    def _():
        vec_ref[...] = pieces

    @pl.when(step > 0)
    def _():
        vec_ref[...] += pieces

    @pl.when(step == pl.num_programs(0) - 1)
    def _():
        for k in range(sem_ref.shape[0]):
            pltpu.make_async_copy(
                stage_ref.at[pl.ds(k * PIECE, PIECE)], out_refs[0].at[0], sem_ref.at[k]
            ).wait()


def qkv_backward(src, grads, w_qkv, x_rows, gres, mod):
    rows, features = x_rows.shape
    block = 4 * PIECE
    rows_spec = pl.BlockSpec((block, features), lambda i, src: (i, 0))
    grad_specs = [pl.BlockSpec((3, block, g.shape[2]), lambda i, src: (0, i, 0)) for g in grads]
    return pl.pallas_call(
        qkv_back_kernel,
        grid_spec=pltpu.PrefetchScalarGridSpec(
            num_scalar_prefetch=1,
            grid=(rows // block,),
            in_specs=grad_specs + [whole(w_qkv.shape), rows_spec, rows_spec, whole(mod.shape)],
            out_specs=[
                *[pl.BlockSpec(memory_space=pl.ANY)] * 4,
                pl.BlockSpec((8, features), lambda i, src: (0, 0)),
            ],
            scratch_shapes=[
                pltpu.VMEM((rows, features), bf16),
                pltpu.SemaphoreType.DMA((rows // PIECE,)),
            ],
        ),
        out_shape=[
            *[jax.ShapeDtypeStruct((rows // PIECE // 4, PIECE, features), bf16)] * 4,
            jax.ShapeDtypeStruct((8, features), f32),
        ],
        name="qkv_backward",
        compiler_params=params(),
        cost_estimate=cost(14),
    )(src, *grads, w_qkv, x_rows, gres, mod)


def assemble_kernel(places, counts, core_ref, *refs):
    ins = refs[: 2 * len(counts)]
    outs = refs[2 * len(counts) :]
    swap = core_ref[0] == 1
    at = 0
    for k, count in enumerate(counts):
        for m in range(count):
            pair = pick(swap, ins[2 * k][m], ins[2 * k + 1][m])
            for tile, (out, row, col) in zip(pair, places[at]):
                outs[out][row * LANES : (row + 1) * LANES, col * LANES : (col + 1) * LANES] = tile.astype(f32)
            at += 1


def assemble(core, pairs, places, shapes):
    flat = [array for pair in pairs for array in pair]
    return pl.pallas_call(
        functools.partial(assemble_kernel, places, [own.shape[0] for own, unused in pairs]),
        grid_spec=pltpu.PrefetchScalarGridSpec(
            num_scalar_prefetch=1,
            grid=(1,),
            in_specs=[whole(array.shape) for array in flat],
            out_specs=[whole(shape) for shape in shapes],
        ),
        out_shape=[jax.ShapeDtypeStruct(shape, f32) for shape in shapes],
        name="assemble",
        compiler_params=params(),
        cost_estimate=cost(5),
    )(core, *flat)


def flip(axis, bit):
    size = lax.axis_size(axis)
    return [(i, i ^ (1 << bit)) for i in range(size)]


def trade(array, axis, bit):
    return lax.ppermute(array, axis, flip(axis, bit))


def add_kernel(plans, *refs):
    ins = refs[: 2 * sum(count for count, unused in plans)]
    outs = refs[len(ins) :]
    at = out_at = 0
    for count, halve in plans:
        col = 0
        for k in range(count):
            own_ref, got_ref = ins[at], ins[at + 1]
            at += 2
            n, m = own_ref.shape[:2]
            total = (own_ref[...].astype(f32) + got_ref[...].astype(f32)).astype(bf16)
            if halve:
                outs[out_at][:, col : col + m] = total[: n // 2]
                outs[out_at + 1][:, col : col + m] = total[n // 2 :]
            else:
                outs[out_at][:, col : col + m] = total
            col += m
        out_at += 2 if halve else 1


def add_all(groups):
    steps = 2
    plans, ins, specs, out_shapes, out_specs = [], [], [], [], []

    def spec(shape):
        return pl.BlockSpec(shape[:2] + (shape[2] // steps, shape[3]), lambda i: (0, 0, i, 0))

    for pairs, halve in groups:
        plans.append((len(pairs), halve))
        for own, got in pairs:
            ins += [own, got]
            specs += [spec(own.shape)] * 2
        n, unused, rows, cols = pairs[0][0].shape
        m = sum(own.shape[1] for own, unused in pairs)
        shape = (n // 2 if halve else n, m, rows, cols)
        out_shapes += [jax.ShapeDtypeStruct(shape, bf16)] * (2 if halve else 1)
        out_specs += [spec(shape)] * (2 if halve else 1)
    return pl.pallas_call(
        functools.partial(add_kernel, plans),
        grid=(steps,),
        in_specs=specs,
        out_specs=out_specs,
        out_shape=out_shapes,
        name="add_all",
        compiler_params=params(),
        cost_estimate=cost(2),
    )(*ins)


def prepare(chains):
    groups = []
    for c in chains:
        c.stage += 1
        groups.append((list(zip(c.own, c.got)), c.stage <= c.clip_bits))
    sums = list(add_all(groups))
    for c, (unused, halve) in zip(chains, groups):
        c.own = [sums.pop(0)]
        c.sends = [sums.pop(0)] if halve else c.own


class Chain:
    def __init__(self, clip_bits, own, sends, stage=0):
        self.clip_bits = clip_bits
        self.own = own
        self.sends = sends
        self.stage = stage
        self.got = None

    def launch(self):
        if self.stage == 0 or self.stage == self.clip_bits + 2:
            axis, bit = "win", 0
        elif self.stage == self.clip_bits + 1:
            axis, bit = "win", 1
        else:
            axis, bit = "clip", self.stage - 1
        self.got = [trade(send, axis, bit) for send in self.sends]

    def finish(self):
        while self.stage < self.clip_bits + 2:
            boundary((), [self], [])
        return self.own[0][0], self.got[0][0]


def unite(*chains):
    first = chains[0]
    united = Chain(first.clip_bits, None, None, first.stage)
    united.own = [o for c in chains for o in c.own]
    united.got = [g for c in chains for g in c.got]
    return united


def boundary(inputs, moved, fresh, held=()):
    waited = moved + list(held)
    got = [c.got for c in waited]
    inputs, got = lax.optimization_barrier((inputs, got))
    for c, g in zip(waited, got):
        c.got = g
    if moved:
        prepare(moved)
    chains = moved + fresh
    inputs, sends = lax.optimization_barrier((inputs, [c.sends for c in chains]))
    for c, sent in zip(chains, sends):
        c.sends = sent
        if c.stage >= c.clip_bits + 1:
            c.own = sent
        c.launch()
    return inputs


def to_quadrants(slot_rows):
    local_slots = slot_rows.shape[0]
    channels = slot_rows.shape[-1]
    arranged = slot_rows.reshape(local_slots, 2, WST, 2, WST, channels).transpose(1, 3, 0, 2, 4, 5)
    return arranged.reshape(4, local_slots, PIECE, channels)


def from_quadrants(received):
    local_slots = received.shape[1]
    channels = received.shape[-1]
    arranged = received.reshape(2, 2, local_slots, WST, WST, channels).transpose(2, 0, 3, 1, 4, 5)
    return arranged.reshape(local_slots, 4 * PIECE, channels)


def exchange(quadrants):
    return lax.all_to_all(quadrants, "win", split_axis=0, concat_axis=0, tiled=True)


def local(
    tokens,
    condition,
    slot_order,
    rel_index,
    w_qkv,
    b_query,
    b_value,
    w_out,
    b_out,
    w_up,
    b_up,
    w_down,
    b_down,
    w_ada,
    b_ada,
    rel_table,
    grad_out,
):
    features = tokens.shape[-1]
    clips = lax.axis_size("clip")
    clip_bits = clips.bit_length() - 1
    me = lax.axis_index("clip")
    core = lax.axis_index("win") & 1
    ff = w_up.shape[1]
    fast = features // clips == LANES and ff // clips == FF_PARTS * LANES

    quadrants, rel_index = lax.optimization_barrier((to_quadrants(tokens[0]), rel_index))
    pieces = exchange(quadrants).reshape(-1, PIECE, features)
    grad_quadrants = to_quadrants(grad_out[0])
    slots = pieces.shape[0]
    per_frame = slots // FRAMES
    order_row = slot_order[0]
    window_place = jnp.arange(slots, dtype=jnp.int32)
    wanted = (window_place % FRAMES) * per_frame + window_place // FRAMES
    src = jnp.sum(
        jnp.where(order_row[None, :] == wanted[:, None], window_place[None, :], 0), axis=1
    ).astype(jnp.int32)
    windows = per_frame
    win = FRAMES * PIECE

    half = win // 2
    idx_mine = lax.dynamic_slice_in_dim(rel_index, core * half, half, 0)
    bias_mine = bias_gather(idx_mine, rel_table)
    lifted = jax.nn.silu(condition.astype(f32)).astype(bf16)
    modulation = jnp.dot(lifted, w_ada, preferred_element_type=f32)[0] + b_ada
    mod = jnp.concatenate([modulation.reshape(6, features), jnp.zeros((2, features), f32)])

    grad_quadrants, bias_mine, mod = lax.optimization_barrier((grad_quadrants, bias_mine, mod))
    grad_pieces = exchange(grad_quadrants).reshape(-1, PIECE, features)
    bias_other = trade(bias_mine, "win", 0)

    qkv_bias = jnp.concatenate([b_query, jnp.zeros_like(b_query), b_value]).astype(f32)[None]
    x_rows, normed, qkv = qkv_call(src, pieces, mod, qkv_bias, w_qkv)
    core_arr = core.astype(jnp.int32)[None]
    attended, probs, recips = attn_forward(core_arr, qkv, bias_mine, bias_other, windows)
    branch, normed_two, grad_mixed = out_call(
        src, grad_pieces, attended, x_rows, mod, b_out.astype(f32)[None], w_out
    )

    shards = features // LANES
    natural = jnp.arange(shards, dtype=jnp.int32)
    if fast:
        places = jnp.zeros_like(natural)
        for bit in range(clip_bits):
            places = places | (((natural >> (clip_bits - 1 - bit)) & 1) << bit)
        order = me ^ places
        inv = jnp.zeros_like(natural)
        for bit in range(clip_bits):
            inv = inv | ((((natural ^ me) >> (clip_bits - 1 - bit)) & 1) << bit)
        per_shard = ff // clips // LANES
        fos = [order * per_shard + j for j in range(FF_PARTS)]
        co = order[::2] & (clips // 2 - 1)
        upper = me >> (clip_bits - 1)
        flags = jnp.stack([core, (upper != core).astype(jnp.int32)]).astype(jnp.int32)
    else:
        inv = natural
        per_part = ff // LANES // FF_PARTS
        fos = [jnp.arange(per_part, dtype=jnp.int32) + j * per_part for j in range(FF_PARTS)]
        co = jnp.arange(per_part // 2, dtype=jnp.int32)
        flags = jnp.zeros((2,), jnp.int32)

    def chain(own, sends):
        return Chain(clip_bits, [own], [sends]) if fast else (own, sends)

    def meet(inputs, moved, fresh=(), held=()):
        return boundary(inputs, list(moved), list(fresh), list(held)) if fast else inputs

    def merge(*chains):
        return unite(*chains) if fast else chains

    b_up_rows = b_up.astype(f32).reshape(-1, 1, LANES)
    before, up_sums, ffs = [], [], []
    steps = [((), ()), ((), (0,)), ((0,), (1,)), ((0, 1), (2,))]
    for j in range(FF_PARTS):
        moved, fresh = steps[j]
        if j:
            normed_two, grad_mixed = meet(
                (normed_two, grad_mixed), [ffs[k] for k in moved], [ffs[k] for k in fresh]
            )
        act, gh, own, other, sums = ff_part(
            j, fos[j], co, inv, flags, normed_two, grad_mixed, w_up, b_up_rows, w_down, before
        )
        before = [act, gh]
        up_sums.append(sums.reshape(-1, LANES))
        ffs.append(chain(own, other))
    act, gh = meet((act, gh), ffs[:3], [ffs[3]])
    mixed, back = ff_join(jnp.concatenate(fos), act, gh, w_up, w_down)
    mixed, back = meet((mixed, back), ffs[1:], held=ffs[:1])
    gres, early, grad_att, out_own, out_other, out_pieces = ff_rows(
        src, inv, flags, mixed, back, grad_pieces, x_rows, branch, mod, b_down.astype(f32)[None], w_out, attended
    )
    local_slots = tokens.shape[1]
    piece_shape = (-1, local_slots, PIECE, features)
    wos = chain(out_own, out_other)
    grad_att, out_pieces = meet((grad_att, out_pieces), ffs[2:], [wos], held=ffs[1:2])
    out_pieces = exchange(out_pieces.reshape(piece_shape))
    pairs = probs.shape[0]
    grads_a, mine_a, others_a = attn_backward(core_arr, qkv, attended, grad_att, probs, recips, windows, 0, FIRST_PAIRS)
    grads_a = meet(grads_a, [ffs[3], wos], held=ffs[2:3])
    qa_own, qa_other = qkv_weight(inv, flags, normed, grads_a)
    qas = chain(qa_own, qa_other)
    front = merge(*ffs[:3])
    grad_att, unused, out_pieces = meet((grad_att, qa_own, out_pieces), [wos, front], [qas], held=ffs[3:])
    others_a = trade(others_a, "win", 0)
    grads_b, mine_b, others_b = attn_backward(
        core_arr, qkv, attended, grad_att, probs, recips, windows, FIRST_PAIRS, pairs - FIRST_PAIRS
    )
    grads_b, others_a, others_b = meet((grads_b, others_a, others_b), [qas, wos])
    others_b = trade(others_b, "win", 0)
    qb_own, qb_other = qkv_weight(inv, flags, normed, grads_b)
    qbs = chain(qb_own, qb_other)

    rear = merge(ffs[3], wos)
    others_a, others_b, unused = meet((others_a, others_b, qb_own), [rear, front], [qbs])
    rel_sums = bucket_sums(idx_mine, [mine_a, mine_b], [others_a, others_b], rel_table.shape[0])

    d = features
    tile_rows = d // LANES
    wins = lax.axis_size("win")
    buckets, heads = rel_table.shape
    gres_late, unused = meet((gres, rel_sums), [rear, qas, qbs])
    home = lax.axis_index("win") if fast else 0
    src_back = (((src // local_slots) ^ home) * local_slots + src % local_slots).astype(jnp.int32)
    *token_parts, late = qkv_backward(src_back, (grads_a, grads_b), w_qkv, x_rows, gres_late, mod)
    if fast:
        token_parts, late, early, up_sums, rel_sums, out_pieces = meet(
            (token_parts, late, early, up_sums, rel_sums, out_pieces), [qbs, qas], held=[front, rear]
        )
        moves = [[(i, i ^ k) for i in range(wins)] for k in range(4)]
        far = [lax.ppermute(token_parts[k], "win", moves[k]) for k in (2, 3)]
        near = lax.ppermute(token_parts[1], "win", moves[1])
        near, late, early, up_sums, rel_sums = boundary((near, late, early, up_sums, rel_sums), [qbs], [])
        here = natural[:, None] == order[None, :]
        up_sums = [jnp.sum(jnp.where(here[:, :, None], u[None], 0.0), axis=1) for u in up_sums]
    grad_b_up = jnp.stack(up_sums, axis=1 if fast else 0)
    if fast:
        to_each = [early[:4].reshape(-1, LANES), late[:2].reshape(-1, LANES), lifted[0].astype(f32).reshape(-1, LANES)]
        by_clip = [v.reshape(clips, 1, LANES) for v in (early[4], early[5], late[2], late[3])]
        by_clip += [grad_b_up.reshape(clips, -1, LANES), rel_sums]
        parts = [jnp.broadcast_to(v[None], (clips,) + v.shape) for v in to_each] + by_clip
        packed = jnp.concatenate(parts, axis=1).astype(bf16)
        packed = jnp.broadcast_to(packed[:, None], (clips, wins) + packed.shape[1:])
        packed = packed.reshape((clips * wins,) + packed.shape[2:])
        vectors = lax.all_to_all(packed, ("clip", "win"), split_axis=0, concat_axis=0, tiled=True)
        last = merge(qas, qbs)
        far = boundary(far, [last], [])
        (vectors,) = boundary((vectors,), [last], [])
        token_pieces = jnp.stack([token_parts[0], near] + far).reshape((2, 2) + token_parts[0].shape)
        for axis, bit in ((0, 1), (1, 0)):
            swapped = (home >> bit) & 1 == 1
            token_pieces = jnp.where(swapped, jnp.flip(token_pieces, axis), token_pieces)
        token_pieces = token_pieces.reshape(piece_shape)
        rows_of = jnp.sum(vectors.astype(f32).reshape((clips, wins) + vectors.shape[1:]), axis=1)
        early_terms = rows_of[:, : 4 * tile_rows].reshape(clips, 4 * d)
        late_terms = rows_of[:, 4 * tile_rows : 6 * tile_rows].reshape(clips, 2 * d)
        all_lifted = rows_of[:, 6 * tile_rows : 7 * tile_rows].reshape(clips, d) * (1.0 / wins)
        own = jnp.sum(rows_of[:, 7 * tile_rows :], axis=0)
        sum_bo, sum_bd, sum_bq, sum_bv = own[0], own[1], own[2], own[3]
        at = 4 + ff // clips // LANES
        sum_bu = own[4:at].reshape(-1)
        sum_rel = own[at:].reshape(2, heads, LANES).transpose(0, 2, 1).reshape(buckets // clips, heads)
    else:
        token_pieces = exchange(jnp.stack(token_parts))

        def all_clips(rows):
            return lax.psum(lax.all_gather(rows.reshape(-1), "clip", axis=0), "win")

        def own_sum(vector):
            return lax.psum(lax.psum_scatter(vector, "clip", scatter_dimension=0, tiled=True), "win")

        early_terms, late_terms = all_clips(early[:4]), all_clips(late[:2])
        all_lifted = lax.all_gather(lifted[0].astype(f32), "clip", axis=0)
        sum_bo, sum_bd, sum_bu = own_sum(early[4]), own_sum(early[5]), own_sum(grad_b_up.reshape(-1))
        sum_bq, sum_bv = own_sum(late[2]), own_sum(late[3])
        rel = rel_sums.reshape(-1, 2, heads, LANES).transpose(0, 1, 3, 2).reshape(buckets, heads)
        sum_rel = own_sum(rel)
    all_terms = jnp.concatenate([late_terms, early_terms], axis=1)

    def own_block(vector):
        size = vector.shape[0] // clips
        return lax.dynamic_slice_in_dim(vector, me * size, size, 0)

    ada_rows = d // clips
    lifted_rows = lax.dynamic_slice_in_dim(all_lifted, me * ada_rows, ada_rows, 1)
    grad_w_ada = jnp.dot(lifted_rows.T, all_terms, precision=lax.Precision.HIGHEST)
    grad_b_ada = own_block(jnp.sum(all_terms, axis=0))

    rows = d // clips
    block_out = from_quadrants(out_pieces).reshape(tokens.shape)
    if fast:
        side = shards // 2
        places = []
        for j in range(FF_PARTS):
            places += [[(0, 0, (c * side + m) * FF_PARTS + j) for c in range(2)] for m in range(side)]
            places += [[(1, j, c * side + m) for c in range(2)] for m in range(side)]
        places += [[(2, 0, c * side + m) for c in range(2)] for m in range(side)]
        sum_wu, sum_wd, sum_wo = assemble(
            core_arr, [front.finish(), rear.finish()], places, [(rows, ff), (ff // clips, d), (rows, d)]
        )
        places, first = [], 0
        for count in (FIRST_PAIRS // 2, (pairs - FIRST_PAIRS) // 2):
            for part in range(3):
                places += [
                    [(0, 0, part * shards + first + c * count + m) for c in range(2)] for m in range(count)
                ]
            first += 2 * count
        (sum_qkv,) = assemble(core_arr, [last.finish()], places, [(rows, 3 * d)])
    else:

        def share(whole_grad):
            part = lax.psum_scatter(whole_grad.astype(f32), "clip", scatter_dimension=0, tiled=True)
            return lax.psum(part, "win")

        def flat_rows(blocks):
            return blocks.transpose(0, 2, 1, 3).reshape(d, -1, LANES)

        halves = len(ffs[0][0][0]) // 2
        ups = [jnp.stack([flat_rows(g[:, :halves]) for g in f], axis=2).reshape(d, -1) for f in ffs]
        sum_wu = share(jnp.concatenate(ups, axis=1))
        downs = [jnp.concatenate([flat_rows(g[:, halves:]).reshape(d, -1) for g in f], axis=1) for f in ffs]
        sum_wd = share(jnp.concatenate(downs, axis=0))
        sum_wo = share(jnp.concatenate([flat_rows(g).reshape(d, -1) for g in wos], axis=1))
        parts = [
            jnp.concatenate([flat_rows(g).reshape(d, 3, -1) for g in q], axis=2) for q in (qas, qbs)
        ]
        sum_qkv = share(jnp.concatenate(parts, axis=2).reshape(d, 3 * d))
    grad_tokens = from_quadrants(token_pieces).reshape(tokens.shape)
    return (
        block_out,
        grad_tokens,
        sum_qkv,
        sum_bq,
        sum_bv,
        sum_wo,
        sum_bo,
        sum_wu,
        sum_bu,
        sum_wd,
        sum_bd,
        grad_w_ada,
        grad_b_ada,
        sum_rel,
    )


def solution(mesh):
    placed = (
        P("clip", "win", None, None),
        P("clip", None),
        P("clip", None),
    ) + (P(),) * 13 + (P("clip", "win", None, None),)
    return jax.shard_map(
        local,
        mesh=mesh,
        in_specs=placed,
        out_specs=(
            P("clip", "win", None, None),
            P("clip", "win", None, None),
            P("clip", None),
            P("clip"),
            P("clip"),
            P("clip", None),
            P("clip"),
            P("clip", None),
            P("clip"),
            P("clip", None),
            P("clip"),
            P("clip", None),
            P("clip"),
            P("clip", None),
        ),
        check_vma=False,
    )
```

```python
import functools
import math

import jax
import jax.numpy as jnp
from jax import lax
from jax.experimental import pallas as pl
from jax.experimental.pallas import tpu as pltpu
from jax.sharding import PartitionSpec as P

HEAD = 64
FRAMES = 5
WST = 8
PIECE = WST * WST
UNIT = 256
FF_PARTS = 4
FF_UNITS = 4
FF_BLOCKS = 2
FIRST_PAIRS = 6
LANES = 128
VMEM_LIMIT = 60 * 1024 * 1024
f32 = jnp.float32
bf16 = jnp.bfloat16
GELU_C = math.sqrt(2.0 / math.pi)
GELU_A = 0.044715


def dot_nn(a, b):
    return jnp.dot(a, b, preferred_element_type=f32)


def dot_nt(a, b):
    return lax.dot_general(a, b, (((1,), (1,)), ((), ())), preferred_element_type=f32)


def dot_tn(a, b):
    return lax.dot_general(a, b, (((0,), (0,)), ((), ())), preferred_element_type=f32)


def params():
    return pltpu.CompilerParams(vmem_limit_bytes=VMEM_LIMIT)


def cost(micros):
    return pl.CostEstimate(
        flops=int(micros * 1.0e9), bytes_accessed=int(micros * 2.0e6), transcendentals=0
    )


def pick(swap, first, second):
    return jnp.where(swap, second, first), jnp.where(swap, first, second)


def hat_of(rows):
    average = jnp.mean(rows, axis=-1, keepdims=True)
    centered = rows - average
    variance = jnp.mean(centered * centered, axis=-1, keepdims=True)
    inv_std = lax.rsqrt(variance + 1e-06)
    return centered * inv_std, inv_std


def norm_back(grad_hat, hat_rows, inv_std):
    first_mean = jnp.mean(grad_hat, axis=-1, keepdims=True)
    second_mean = jnp.mean(grad_hat * hat_rows, axis=-1, keepdims=True)
    return inv_std * (grad_hat - first_mean - hat_rows * second_mean)


def whole(shape):
    zeros = (0,) * len(shape)
    return pl.BlockSpec(shape, lambda *unused: zeros, pipeline_mode=pl.Buffered(1))


def bias_kernel(idx_ref, tab_ref, out_ref, scr_ref):
    lows = lax.broadcasted_iota(jnp.int32, (256, idx_ref.shape[1]), 0)
    tab = tab_ref[...]
    half = tab.shape[0] // 2
    heads = 16
    tiles = idx_ref.shape[1] // LANES
    win = out_ref.shape[2] // 2
    for i in range(8):
        idx = idx_ref[pl.ds(i, 1), :]
        low = idx & 255
        high = idx >> 8
        onehot = jnp.where(lows == low, 1.0, 0.0).astype(bf16)
        got = dot_nn(tab, onehot)
        got = got[:half] + got[half:]
        acc = got[:heads]
        for c in range(1, half // heads):
            acc = jnp.where(high == c, got[c * heads : (c + 1) * heads], acc)
        for t in range(tiles):
            scr_ref[t, pl.ds(i, heads, stride=8), :] = acc[:, t * LANES : (t + 1) * LANES]
    for pair in range(heads // 2):
        rows = []
        for h in range(2):
            at = (2 * pair + h) * 8
            rows.append(
                jnp.concatenate([scr_ref[t, at : at + 8, :] for t in range(tiles)], axis=1)[:, :win]
            )
        out_ref[pair] = jnp.concatenate(rows, axis=1)


def bias_gather(idx, table):
    rows, win = idx.shape
    padded = -(-win // LANES) * LANES
    buckets, heads = table.shape
    upper_f = lax.reduce_precision(table, 8, 7)
    lower = (table - upper_f).astype(bf16)

    def arrange(t):
        return t.reshape(-1, 256, heads).transpose(0, 2, 1).reshape(-1, 256)

    tab = jnp.concatenate([arrange(upper_f.astype(bf16)), arrange(lower)], axis=0)
    idx = jnp.pad(idx, ((0, 0), (0, padded - win)))
    return pl.pallas_call(
        bias_kernel,
        grid=(rows // 8,),
        in_specs=[pl.BlockSpec((8, padded), lambda i: (i, 0)), whole(tab.shape)],
        out_specs=pl.BlockSpec((heads // 2, 8, 2 * win), lambda i: (0, i, 0)),
        out_shape=jax.ShapeDtypeStruct((heads // 2, rows, 2 * win), f32),
        scratch_shapes=[pltpu.VMEM((padded // LANES, 8 * heads, LANES), f32)],
        name="bias_gather",
        compiler_params=params(),
        cost_estimate=cost(0.9),
    )(idx, tab)


def bucket_kernel(idx_ref, *refs):
    out_ref, acc_ref, scr_ref = refs[-3:]
    keep_refs = refs[: (len(refs) - 3) // 2]
    got_refs = refs[(len(refs) - 3) // 2 : -3]

    @pl.when(pl.program_id(0) == 0)
    def _():
        acc_ref[...] = jnp.zeros_like(acc_ref)

    padded = idx_ref.shape[1]
    tiles = padded // LANES
    keeps = [(r, k) for r in keep_refs for k in range(r.shape[0])]
    gots = [(r, k) for r in got_refs for k in range(r.shape[0])]
    pairs = len(keeps)
    heads = 2 * pairs
    win = keep_refs[0].shape[2] // 2
    step_rows = idx_ref.shape[0]
    lows = lax.broadcasted_iota(jnp.int32, (256, padded), 0)
    zero = jnp.zeros((step_rows, padded - win), f32)
    for pair in range(pairs):
        (keep_ref, k), (got_ref, unused) = keeps[pair], gots[pair]
        sums = keep_ref[k].astype(f32) + got_ref[k].astype(f32)
        for h in range(2):
            part = jnp.concatenate([sums[:, h * win : (h + 1) * win], zero], axis=1)
            at = (2 * pair + h) * step_rows
            for t in range(tiles):
                scr_ref[t, at : at + step_rows, :] = part[:, t * LANES : (t + 1) * LANES]
    total = acc_ref[...]
    for i in range(step_rows):
        idx = idx_ref[pl.ds(i, 1), :]
        low = idx & 255
        high = idx >> 8
        onehot = jnp.where(lows == low, 1.0, 0.0).astype(bf16)
        sums = jnp.concatenate(
            [scr_ref[t, pl.ds(i, heads, stride=step_rows), :] for t in range(tiles)], axis=1
        )
        spread = jnp.concatenate(
            [jnp.where(high == c, sums, 0.0) for c in range(acc_ref.shape[0] // heads)], axis=0
        )
        total += dot_nt(spread.astype(bf16), onehot)
    acc_ref[...] = total

    @pl.when(pl.program_id(0) == pl.num_programs(0) - 1)
    def _():
        for k in range(out_ref.shape[0]):
            for t in range(2):
                out_ref[k, t * heads : (t + 1) * heads] = total[
                    k * heads : (k + 1) * heads, t * LANES : (t + 1) * LANES
                ]


def bucket_sums(idx, keeps, gots, buckets):
    rows, win = idx.shape
    padded = -(-win // LANES) * LANES
    heads = 2 * sum(k.shape[0] for k in keeps)
    step_rows = 16
    idx = jnp.pad(idx, ((0, 0), (0, padded - win)))
    out_rows = buckets // 256
    sum_specs = [pl.BlockSpec((k.shape[0], step_rows, 2 * win), lambda i: (0, i, 0)) for k in keeps]
    out_shape = jax.ShapeDtypeStruct((out_rows, 2 * heads, LANES), f32)
    return pl.pallas_call(
        bucket_kernel,
        grid=(rows // step_rows,),
        in_specs=[pl.BlockSpec((step_rows, padded), lambda i: (i, 0))] + sum_specs + sum_specs,
        out_specs=pl.BlockSpec(out_shape.shape, lambda i: (0, 0, 0)),
        out_shape=out_shape,
        scratch_shapes=[
            pltpu.VMEM((out_rows * heads, 256), f32),
            pltpu.VMEM((padded // LANES, step_rows * heads, LANES), f32),
        ],
        name="bucket_sums",
        compiler_params=params(),
        cost_estimate=cost(4),
    )(idx, *keeps, *gots)


def qkv_kernel(src_ref, a_ref, b_ref, c_ref, d_ref, mod_ref, bias_ref, w_ref, x_ref, n_ref, o_ref):
    rows = jnp.concatenate([r[0] for r in (a_ref, b_ref, c_ref, d_ref)], axis=0)
    x_ref[...] = rows
    hat_rows, unused = hat_of(rows.astype(f32))
    normed = (hat_rows * (1.0 + mod_ref[1:2, :]) + mod_ref[0:1, :]).astype(bf16)
    n_ref[...] = normed
    features = rows.shape[1]
    for j in range(w_ref.shape[1] // 512):
        cols = slice(j * 512, (j + 1) * 512)
        got = dot_nn(normed, w_ref[:, cols]) + bias_ref[0:1, cols]
        if (j + 1) * 512 <= features:
            got = got.astype(bf16).astype(f32) * (1.0 / math.sqrt(HEAD))
        o_ref[:, cols] = got.astype(bf16)


def slot_spec(features, t):
    return pl.BlockSpec((1, PIECE, features), lambda i, src, t=t: (src[4 * i + t], 0, 0))


def qkv_call(src, pieces, mod, qkv_bias, w_qkv):
    count, unused, features = pieces.shape
    rows = count * PIECE
    wide = w_qkv.shape[1]
    block = 4 * PIECE
    return pl.pallas_call(
        qkv_kernel,
        grid_spec=pltpu.PrefetchScalarGridSpec(
            num_scalar_prefetch=1,
            grid=(count // 4,),
            in_specs=[slot_spec(features, t) for t in range(4)]
            + [whole(mod.shape), whole(qkv_bias.shape), whole(w_qkv.shape)],
            out_specs=[
                pl.BlockSpec((block, features), lambda i, src: (i, 0)),
                pl.BlockSpec((block, features), lambda i, src: (i, 0)),
                pl.BlockSpec((block, wide), lambda i, src: (i, 0)),
            ],
        ),
        out_shape=[
            jax.ShapeDtypeStruct((rows, features), bf16),
            jax.ShapeDtypeStruct((rows, features), bf16),
            jax.ShapeDtypeStruct((rows, wide), bf16),
        ],
        name="norm_qkv",
        compiler_params=params(),
        cost_estimate=cost(0.6),
    )(src, pieces, pieces, pieces, pieces, mod, qkv_bias, w_qkv)


def split_pair(x, left):
    zero = jnp.zeros_like(x)
    return jnp.concatenate([jnp.where(left, x, zero), jnp.where(left, zero, x)], axis=0)


def values_ones(v, left):
    one = jnp.ones_like(v)
    zero = jnp.zeros_like(v)
    marks = jnp.concatenate([jnp.where(left, one, zero), jnp.where(left, zero, one)], axis=0)
    return jnp.concatenate([split_pair(v, left), marks], axis=1)


def attn_kernel(windows, core_ref, q_ref, k_ref, v_ref, mine_ref, other_ref, o_ref, p_ref, r_ref, b_ref):
    win = q_ref.shape[0] // windows
    half = win // 2
    left = lax.broadcasted_iota(jnp.int32, (win, LANES), 1) < HEAD
    first = core_ref[0] == 0
    b_ref[:half] = jnp.where(first, mine_ref[0], other_ref[0])
    b_ref[half:] = jnp.where(first, other_ref[0], mine_ref[0])
    lowest = jnp.float32(-jnp.inf)
    whole_tiles = win // LANES * LANES
    for u in range(windows):
        rows = slice(u * win, (u + 1) * win)
        keys = split_pair(k_ref[rows], left)
        vals = values_ones(v_ref[rows], left)
        s = dot_nt(q_ref[rows], keys) + b_ref[...]
        lo = s[:, :whole_tiles]
        mid = s[:, whole_tiles : whole_tiles + LANES]
        hi = s[:, whole_tiles + LANES :]
        top_lo = jnp.where(left, mid, lowest)
        top_hi = jnp.where(left, lowest, mid)
        for t in range(whole_tiles // LANES):
            cols = slice(t * LANES, (t + 1) * LANES)
            top_lo = jnp.maximum(top_lo, lo[:, cols])
            top_hi = jnp.maximum(top_hi, hi[:, cols])
        top_lo = jnp.max(top_lo, axis=1, keepdims=True)
        top_hi = jnp.max(top_hi, axis=1, keepdims=True)
        e = jnp.concatenate(
            [
                jnp.exp(lo - top_lo),
                jnp.exp(mid - jnp.where(left, top_lo, top_hi)),
                jnp.exp(hi - top_hi),
            ],
            axis=1,
        ).astype(bf16)
        p_ref[0, u] = e
        got = dot_nn(e, vals)
        r = 1.0 / got[:, LANES:]
        r_ref[rows] = r
        o_ref[rows] = (got[:, :LANES] * r).astype(bf16)


def attn_forward(core, qkv, bias_mine, bias_other, windows):
    rows = qkv.shape[0]
    win = rows // windows
    pairs = bias_mine.shape[0]
    features = qkv.shape[1] // 3

    def col(part):
        return pl.BlockSpec((rows, LANES), lambda h, c, part=part: (0, part * pairs + h))

    half_spec = pl.BlockSpec((1, win // 2, 2 * win), lambda h, c: (h, 0, 0))
    return pl.pallas_call(
        functools.partial(attn_kernel, windows),
        grid_spec=pltpu.PrefetchScalarGridSpec(
            num_scalar_prefetch=1,
            grid=(pairs,),
            in_specs=[col(0), col(1), col(2), half_spec, half_spec],
            out_specs=[
                col(0),
                pl.BlockSpec((1, windows, win, 2 * win), lambda h, c: (h, 0, 0, 0)),
                col(0),
            ],
            scratch_shapes=[pltpu.VMEM((win, 2 * win), f32)],
        ),
        out_shape=[
            jax.ShapeDtypeStruct((rows, features), bf16),
            jax.ShapeDtypeStruct((pairs, windows, win, 2 * win), bf16),
            jax.ShapeDtypeStruct((rows, features), f32),
        ],
        name="attn_forward",
        compiler_params=params(),
        cost_estimate=cost(0.9),
    )(core, qkv, qkv, qkv, bias_mine, bias_other)


def fold_delta(dx, lane):
    lower_half = (lane & 32) == 0
    dx = dx + jnp.where(lower_half, pltpu.roll(dx, LANES - 32, 1), pltpu.roll(dx, 32, 1))
    upper = dx.astype(bf16)
    lower = (dx - upper.astype(f32)).astype(bf16)
    return jnp.where(lower_half, upper, lower)


def attn_back_kernel(windows, core_ref, q_ref, k_ref, v_ref, o_ref, do_ref, p_ref, r_ref, g_ref, mine_ref, other_ref):
    win = q_ref.shape[0] // windows
    lane = lax.broadcasted_iota(jnp.int32, (win, LANES), 1)
    left = lane < HEAD
    sums = None
    for u in range(windows):
        rows = slice(u * win, (u + 1) * win)
        keys = split_pair(k_ref[rows], left)
        vals = values_ones(v_ref[rows], left)
        up = (do_ref[rows].astype(f32) * r_ref[rows]).astype(bf16)
        delta = fold_delta(-(up.astype(f32) * o_ref[rows].astype(f32)), lane)
        d = dot_nt(jnp.concatenate([up, delta], axis=1), vals)
        p = p_ref[0, u]
        ds = p.astype(f32) * d
        sums = ds if sums is None else sums + ds
        low = ds.astype(bf16)
        g_ref[0, rows] = (dot_nn(low, keys) * (1.0 / math.sqrt(HEAD))).astype(bf16)
        dk = dot_tn(low, q_ref[rows])
        g_ref[1, rows] = jnp.where(left, dk[:win], dk[win:]).astype(bf16)
        dv = dot_tn(p, up)
        g_ref[2, rows] = jnp.where(left, dv[:win], dv[win:]).astype(bf16)
    half = win // 2
    first, second = sums[:half].astype(bf16), sums[half:].astype(bf16)
    mine_ref[0], other_ref[0] = pick(core_ref[0] == 1, first, second)


def attn_backward(core, qkv, attended, grad_att, probs, recips, windows, first, count):
    rows = qkv.shape[0]
    win = rows // windows
    pairs = probs.shape[0]

    def col(part):
        return pl.BlockSpec((rows, LANES), lambda h, core, part=part: (0, part * pairs + first + h))

    half_spec = pl.BlockSpec((1, win // 2, 2 * win), lambda h, core: (h, 0, 0))
    half_shape = jax.ShapeDtypeStruct((count, win // 2, 2 * win), bf16)
    return pl.pallas_call(
        functools.partial(attn_back_kernel, windows),
        grid_spec=pltpu.PrefetchScalarGridSpec(
            num_scalar_prefetch=1,
            grid=(count,),
            in_specs=[
                col(0),
                col(1),
                col(2),
                col(0),
                col(0),
                pl.BlockSpec((1, windows, win, 2 * win), lambda h, core: (first + h, 0, 0, 0)),
                col(0),
            ],
            out_specs=[
                pl.BlockSpec((3, rows, LANES), lambda h, core: (0, 0, h)),
                half_spec,
                half_spec,
            ],
        ),
        out_shape=[jax.ShapeDtypeStruct((3, rows, count * LANES), bf16), half_shape, half_shape],
        name="attn_backward",
        compiler_params=params(),
        cost_estimate=cost(3 * count),
    )(core, qkv, qkv, qkv, attended, grad_att, probs, recips)


def out_kernel(src_ref, a_ref, b_ref, c_ref, d_ref, att_ref, x_ref, mod_ref, bo_ref, w_ref, branch_ref, n_ref, gm_ref):
    branch = (dot_nn(att_ref[...], w_ref[...]) + bo_ref[...]).astype(bf16)
    branch_ref[...] = branch
    residual = x_ref[...].astype(f32) + mod_ref[2:3, :] * branch.astype(f32)
    hat_rows, unused = hat_of(residual)
    n_ref[...] = (hat_rows * (1.0 + mod_ref[4:5, :]) + mod_ref[3:4, :]).astype(bf16)
    up = jnp.concatenate([r[0] for r in (a_ref, b_ref, c_ref, d_ref)], axis=0)
    gm_ref[...] = (mod_ref[5:6, :] * up.astype(f32)).astype(bf16)


def out_call(src, pieces, attended, x_rows, mod, b_out, w_out):
    count, unused, features = pieces.shape
    rows = count * PIECE
    block = 4 * PIECE
    rows_spec = pl.BlockSpec((block, features), lambda i, src: (i, 0))
    sds = jax.ShapeDtypeStruct((rows, features), bf16)
    return pl.pallas_call(
        out_kernel,
        grid_spec=pltpu.PrefetchScalarGridSpec(
            num_scalar_prefetch=1,
            grid=(count // 4,),
            in_specs=[slot_spec(features, t) for t in range(4)]
            + [rows_spec, rows_spec, whole(mod.shape), whole(b_out.shape), whole(w_out.shape)],
            out_specs=[rows_spec, rows_spec, rows_spec],
        ),
        out_shape=[sds, sds, sds],
        name="out_norm",
        compiler_params=params(),
        cost_estimate=cost(0.3),
    )(src, pieces, pieces, pieces, pieces, attended, x_rows, mod, b_out, w_out)


def place_rows(inv_ref, out_ref, values):
    for k in range(out_ref.shape[0]):
        at = inv_ref[k]
        for m in range(out_ref.shape[1]):
            out_ref[at, m] = values[k * LANES : (k + 1) * LANES, m * LANES : (m + 1) * LANES]


def ff_part_kernel(count, fo_ref, co_ref, inv_ref, flag_ref, n_ref, gm_ref, *refs):
    ups = refs[:count]
    biases = refs[count : 2 * count]
    downs = refs[2 * count : 3 * count]
    act_ref, gh_ref, own_ref, other_ref, sum_ref = refs[-5:]
    step = pl.program_id(0)
    rows = n_ref.shape[0]
    block = rows // FF_BLOCKS
    wu = jnp.concatenate([r[...] for r in ups], axis=1)
    wd = jnp.concatenate([r[...] for r in downs], axis=0)
    bias = jnp.concatenate([r[0] for r in biases], axis=1)
    sums = None
    for c in range(FF_BLOCKS):
        part = slice(c * block, (c + 1) * block)
        v = dot_nn(n_ref[part], wu) + bias
        v2 = v * v
        t = jnp.tanh(v * (GELU_C + (GELU_C * GELU_A) * v2))
        h = 0.5 + 0.5 * t
        slope = h + (0.5 * v) * (1.0 - t * t) * (GELU_C + (3.0 * GELU_C * GELU_A) * v2)
        gh = (dot_nt(gm_ref[part], wd) * slope).astype(bf16)
        act_ref[0, part] = (v * h).astype(bf16)
        gh_ref[0, part] = gh
        piece = jnp.sum(gh.astype(f32), axis=0, keepdims=True)
        sums = piece if sums is None else sums + piece
    sum_ref[0] = sums
    up = dot_tn(n_ref[...], gh_ref[0]).astype(bf16)
    down = dot_tn(act_ref[0], gm_ref[...]).astype(bf16)
    half = down.shape[1] // 2
    blocks = half // LANES
    for p in range(count // 2):
        left = up[:, 2 * p * LANES : (2 * p + 1) * LANES]
        right = up[:, (2 * p + 1) * LANES : (2 * p + 2) * LANES]
        own, other = pick(flag_ref[1] == 1, left, right)
        col = co_ref[step * (count // 2) + p]
        for k in range(own_ref.shape[0]):
            at = inv_ref[k]
            own_ref[at, col] = own[k * LANES : (k + 1) * LANES]
            other_ref[at, col] = other[k * LANES : (k + 1) * LANES]
    own, other = pick(flag_ref[0] == 1, down[:, :half], down[:, half:])
    first = own_ref.shape[1] - blocks
    for k in range(count):
        for m in range(blocks):
            tile = (slice(k * LANES, (k + 1) * LANES), slice(m * LANES, (m + 1) * LANES))
            own_ref[step * count + k, first + m] = own[tile]
            other_ref[step * count + k, first + m] = other[tile]


def ff_part(j, fo, co, inv, flags, normed, grad_mixed, w_up, b_up, w_down, before):
    units = fo.shape[0]
    count = FF_UNITS
    steps = units // count
    rows, features = normed.shape

    def up(k):
        return pl.BlockSpec((features, LANES), lambda i, fo, *more: (0, fo[count * i + k]))

    def bias(k):
        return pl.BlockSpec((1, 1, LANES), lambda i, fo, *more: (fo[count * i + k], 0, 0))

    def down(k):
        return pl.BlockSpec((LANES, features), lambda i, fo, *more: (fo[count * i + k], 0))

    cols = pl.BlockSpec((1, rows, count * LANES), lambda i, *more: (j, 0, i))
    hidden = jax.ShapeDtypeStruct((FF_PARTS, rows, units * LANES), bf16)
    blocks = units // 2 + features // 2 // LANES
    grad = jax.ShapeDtypeStruct((units, blocks, LANES, LANES), bf16)
    ks = range(count)
    at = 4 + 2 + 3 * count
    return pl.pallas_call(
        functools.partial(ff_part_kernel, count),
        grid_spec=pltpu.PrefetchScalarGridSpec(
            num_scalar_prefetch=4,
            grid=(steps,),
            in_specs=[whole(normed.shape), whole(normed.shape)]
            + [up(k) for k in ks]
            + [bias(k) for k in ks]
            + [down(k) for k in ks]
            + [pl.BlockSpec(memory_space=pl.ANY)] * len(before),
            out_specs=[cols, cols, whole(grad.shape), whole(grad.shape)]
            + [pl.BlockSpec((1, 1, count * LANES), lambda i, *more: (i, 0, 0))],
        ),
        out_shape=[hidden, hidden, grad, grad, jax.ShapeDtypeStruct((steps, 1, count * LANES), f32)],
        input_output_aliases={at: 0, at + 1: 1} if before else {},
        name="ff_part",
        compiler_params=params(),
        cost_estimate=cost(20),
    )(fo, co, inv, flags, normed, grad_mixed, *[w_up] * count, *[b_up] * count, *[w_down] * count, *before)


def ff_join_kernel(units, parts, fo_ref, act_ref, gh_ref, *refs):
    up_refs = refs[:units]
    down_refs = refs[units : 2 * units]
    mixed_ref, back_ref, mixed_sum, back_sum = refs[2 * units :]
    step = pl.program_id(0)
    half = mixed_ref.shape[0] // 2

    def each(put):
        wd = jnp.concatenate([r[...] for r in down_refs], axis=0)
        wu = jnp.concatenate([r[...] for r in up_refs], axis=1)
        for k in range(2):
            part = slice(k * half, (k + 1) * half)
            put(part, mixed_ref, mixed_sum, dot_nn(act_ref[0, part], wd))
            put(part, back_ref, back_sum, dot_nt(gh_ref[0, part], wu))

    def first(part, out_ref, sum_ref, got):
        sum_ref[part] = got

    def middle(part, out_ref, sum_ref, got):
        sum_ref[part] += got

    def last(part, out_ref, sum_ref, got):
        out_ref[part] = (sum_ref[part] + got).astype(bf16)

    @pl.when(step == 0)
    def _():
        each(first)

    @pl.when(jnp.logical_and(step > 0, step < parts - 1))
    def _():
        each(middle)

    @pl.when(step == parts - 1)
    def _():
        each(last)


def ff_join(fo, act, gh, w_up, w_down):
    parts, rows, wide = act.shape
    units = wide // LANES
    features = w_up.shape[0]
    ups = [
        pl.BlockSpec((features, LANES), lambda i, fo, u=u: (0, fo[i * units + u])) for u in range(units)
    ]
    downs = [
        pl.BlockSpec((LANES, features), lambda i, fo, u=u: (fo[i * units + u], 0)) for u in range(units)
    ]
    hidden = pl.BlockSpec((1, rows, wide), lambda i, fo: (i, 0, 0))
    sums = jax.ShapeDtypeStruct((rows, features), bf16)
    return pl.pallas_call(
        functools.partial(ff_join_kernel, units, parts),
        grid_spec=pltpu.PrefetchScalarGridSpec(
            num_scalar_prefetch=1,
            grid=(parts,),
            in_specs=[hidden, hidden] + ups + downs,
            out_specs=[whole(sums.shape), whole(sums.shape)],
            scratch_shapes=[pltpu.VMEM(sums.shape, f32), pltpu.VMEM(sums.shape, f32)],
        ),
        out_shape=[sums, sums],
        name="ff_join",
        compiler_params=params(),
        cost_estimate=cost(28),
    )(fo, act, gh, *([w_up] * units), *([w_down] * units))


def ff_rows_kernel(blocks, src_ref, inv_ref, flag_ref, mixed_ref, back_ref, *refs):
    a_ref, b_ref, c_ref, d_ref, x_ref, branch_ref, mod_ref, bd_ref, wo_ref, att_ref = refs[:10]
    gres_ref, vec_ref, do_ref, own_ref, other_ref, out_ref = refs[10:16]
    stage_ref, gb_ref, sem_ref = refs[16:]
    step = pl.program_id(0)

    @pl.when(step < blocks)
    def _():
        e = step
        block = 4 * PIECE
        part = pl.ds(pl.multiple_of(e * block, block), block)
        mixed = mixed_ref[...].astype(f32) + bd_ref[...]
        back = back_ref[...].astype(f32)
        branch = branch_ref[...].astype(f32)
        gate_one = mod_ref[2:3, :]
        gate_two = mod_ref[5:6, :]
        residual = x_ref[...].astype(f32) + gate_one * branch
        hat_rows, inv_std = hat_of(residual)
        up = jnp.concatenate([r[0] for r in (a_ref, b_ref, c_ref, d_ref)], axis=0).astype(f32)
        stage_ref[part] = (residual + gate_two * mixed).astype(bf16)
        for t in range(4):
            pltpu.make_async_copy(
                stage_ref.at[pl.ds(pl.multiple_of(e * block + t * PIECE, PIECE), PIECE)],
                out_ref.at[src_ref[4 * e + t]],
                sem_ref.at[4 * e + t],
            ).start()
        gres = up + norm_back(back * (1.0 + mod_ref[4:5, :]), hat_rows, inv_std)
        gres_ref[...] = gres.astype(bf16)
        low = (gate_one * gres).astype(bf16)
        gb_ref[part] = low
        do_ref[...] = dot_nt(low, wo_ref[...]).astype(bf16)
        grad_mixed = (gate_two * up).astype(bf16).astype(f32)

        def total(values):
            return jnp.sum(values, axis=0, keepdims=True)

        pieces = jnp.concatenate(
            [
                total(gres * branch),
                total(back),
                total(back * hat_rows),
                total(up * mixed),
                total(low.astype(f32)),
                total(grad_mixed),
                jnp.zeros((2, gate_one.shape[1]), f32),
            ],
            axis=0,
        )

        @pl.when(e == 0)
        def _():
            vec_ref[...] = pieces

        @pl.when(e > 0)
        def _():
            vec_ref[...] += pieces

    @pl.when(step >= blocks)
    def _():
        width = own_ref.shape[1] * LANES
        half = gb_ref.shape[1] // 2
        flag = flag_ref[0]
        for grad_ref, side in ((own_ref, flag), (other_ref, 1 - flag)):
            start = pl.multiple_of(side * half + (step - blocks) * width, width)
            got = dot_tn(att_ref[...], gb_ref[:, pl.ds(start, width)])
            place_rows(inv_ref, grad_ref, got.astype(bf16))

    @pl.when(step == pl.num_programs(0) - 1)
    def _():
        for k in range(sem_ref.shape[0]):
            pltpu.make_async_copy(
                stage_ref.at[pl.ds(k * PIECE, PIECE)], out_ref.at[src_ref[k]], sem_ref.at[k]
            ).wait()


def ff_rows(src, inv, flags, mixed, back, pieces, x_rows, branch, mod, b_down, w_out, attended):
    rows, features = x_rows.shape
    shards = features // LANES
    block = 4 * PIECE
    blocks = rows // block
    ends = features // 2 // UNIT

    def at(i):
        return jnp.minimum(i, blocks - 1)

    rows_spec = pl.BlockSpec((block, features), lambda i, *more: (at(i), 0))
    slots = [
        pl.BlockSpec((1, PIECE, features), lambda i, src, *more, t=t: (src[4 * at(i) + t], 0, 0))
        for t in range(4)
    ]
    grad_spec = pl.BlockSpec(
        (shards, UNIT // LANES, LANES, LANES), lambda i, *more: (0, jnp.maximum(i - blocks, 0), 0, 0)
    )
    grad = jax.ShapeDtypeStruct((shards, features // 2 // LANES, LANES, LANES), bf16)
    rows_shape = jax.ShapeDtypeStruct((rows, features), bf16)
    return pl.pallas_call(
        functools.partial(ff_rows_kernel, blocks),
        grid_spec=pltpu.PrefetchScalarGridSpec(
            num_scalar_prefetch=3,
            grid=(blocks + ends,),
            in_specs=[rows_spec, rows_spec]
            + slots
            + [rows_spec, rows_spec, whole(mod.shape), whole(b_down.shape)]
            + [whole(w_out.shape), whole(attended.shape)],
            out_specs=[
                rows_spec,
                pl.BlockSpec((8, features), lambda i, *more: (0, 0)),
                rows_spec,
                grad_spec,
                grad_spec,
                pl.BlockSpec(memory_space=pl.ANY),
            ],
            scratch_shapes=[
                pltpu.VMEM((rows, features), bf16),
                pltpu.VMEM((rows, features), bf16),
                pltpu.SemaphoreType.DMA((rows // PIECE,)),
            ],
        ),
        out_shape=[
            rows_shape,
            jax.ShapeDtypeStruct((8, features), f32),
            rows_shape,
            grad,
            grad,
            jax.ShapeDtypeStruct(pieces.shape, bf16),
        ],
        name="ff_rows",
        compiler_params=params(),
        cost_estimate=cost(22),
    )(src, inv, flags, mixed, back, *([pieces] * 4), x_rows, branch, mod, b_down, w_out, attended)


def qkv_weight_kernel(inv_ref, flag_ref, n_ref, grad_ref, g0_ref, g1_ref):
    got = dot_tn(n_ref[...], grad_ref[0]).astype(bf16)
    half = got.shape[1] // 2
    own, other = pick(flag_ref[0] == 1, got[:, :half], got[:, half:])
    place_rows(inv_ref, g0_ref, own)
    place_rows(inv_ref, g1_ref, other)


def qkv_weight(inv, flags, normed, grads):
    rows, features = normed.shape
    parts, unused, wide = grads.shape
    shards = features // LANES
    tiles = wide // 2 // LANES
    out_spec = pl.BlockSpec((shards, tiles, LANES, LANES), lambda i, *more: (0, i, 0, 0))
    grad = jax.ShapeDtypeStruct((shards, parts * tiles, LANES, LANES), bf16)
    return pl.pallas_call(
        qkv_weight_kernel,
        grid_spec=pltpu.PrefetchScalarGridSpec(
            num_scalar_prefetch=2,
            grid=(parts,),
            in_specs=[
                whole(normed.shape),
                pl.BlockSpec((1, rows, wide), lambda i, *more: (i, 0, 0)),
            ],
            out_specs=[out_spec, out_spec],
        ),
        out_shape=[grad, grad],
        name="qkv_weight",
        compiler_params=params(),
        cost_estimate=cost(6),
    )(inv, flags, normed, grads)


def qkv_back_kernel(src_ref, *refs):
    count = len(refs) - 11
    grads = refs[:count]
    w_ref, x_ref, gres_ref, mod_ref = refs[count : count + 4]
    out_refs = refs[count + 4 : count + 8]
    vec_ref, stage_ref, sem_ref = refs[count + 8 :]
    per = out_refs[0].shape[0]
    step = pl.program_id(0)
    block = x_ref.shape[0]
    features = x_ref.shape[1]
    back = None
    bias = []
    for part in range(3):
        joined = jnp.concatenate([g[part] for g in grads], axis=1)
        bias.append(jnp.sum(joined.astype(f32), axis=0, keepdims=True))
        got = dot_nt(joined, w_ref[:, part * features : (part + 1) * features])
        back = got if back is None else back + got
    back = back.astype(bf16).astype(f32)
    hat_rows, inv_std = hat_of(x_ref[...].astype(f32))
    grad = gres_ref[...].astype(f32) + norm_back(back * (1.0 + mod_ref[1:2, :]), hat_rows, inv_std)
    stage_ref[pl.ds(pl.multiple_of(step * block, block), block)] = grad.astype(bf16)
    for t in range(4):
        slot = src_ref[4 * step + t]
        for k in range(4):

            @pl.when(slot // per == k)
            def _(k=k, t=t, slot=slot):
                pltpu.make_async_copy(
                    stage_ref.at[pl.ds(pl.multiple_of(step * block + t * PIECE, PIECE), PIECE)],
                    out_refs[k].at[slot - k * per],
                    sem_ref.at[4 * step + t],
                ).start()
    pieces = jnp.concatenate(
        [
            jnp.sum(back, axis=0, keepdims=True),
            jnp.sum(back * hat_rows, axis=0, keepdims=True),
            bias[0],
            bias[2],
            jnp.zeros((4, features), f32),
        ],
        axis=0,
    )

    @pl.when(step == 0)
    def _():
        vec_ref[...] = pieces

    @pl.when(step > 0)
    def _():
        vec_ref[...] += pieces

    @pl.when(step == pl.num_programs(0) - 1)
    def _():
        for k in range(sem_ref.shape[0]):
            pltpu.make_async_copy(
                stage_ref.at[pl.ds(k * PIECE, PIECE)], out_refs[0].at[0], sem_ref.at[k]
            ).wait()


def qkv_backward(src, grads, w_qkv, x_rows, gres, mod):
    rows, features = x_rows.shape
    block = 4 * PIECE
    rows_spec = pl.BlockSpec((block, features), lambda i, src: (i, 0))
    grad_specs = [pl.BlockSpec((3, block, g.shape[2]), lambda i, src: (0, i, 0)) for g in grads]
    return pl.pallas_call(
        qkv_back_kernel,
        grid_spec=pltpu.PrefetchScalarGridSpec(
            num_scalar_prefetch=1,
            grid=(rows // block,),
            in_specs=grad_specs + [whole(w_qkv.shape), rows_spec, rows_spec, whole(mod.shape)],
            out_specs=[
                *[pl.BlockSpec(memory_space=pl.ANY)] * 4,
                pl.BlockSpec((8, features), lambda i, src: (0, 0)),
            ],
            scratch_shapes=[
                pltpu.VMEM((rows, features), bf16),
                pltpu.SemaphoreType.DMA((rows // PIECE,)),
            ],
        ),
        out_shape=[
            *[jax.ShapeDtypeStruct((rows // PIECE // 4, PIECE, features), bf16)] * 4,
            jax.ShapeDtypeStruct((8, features), f32),
        ],
        name="qkv_backward",
        compiler_params=params(),
        cost_estimate=cost(14),
    )(src, *grads, w_qkv, x_rows, gres, mod)


def assemble_kernel(places, counts, core_ref, *refs):
    ins = refs[: 2 * len(counts)]
    outs = refs[2 * len(counts) :]
    swap = core_ref[0] == 1
    at = 0
    for k, count in enumerate(counts):
        for m in range(count):
            pair = pick(swap, ins[2 * k][m], ins[2 * k + 1][m])
            for tile, (out, row, col) in zip(pair, places[at]):
                outs[out][row * LANES : (row + 1) * LANES, col * LANES : (col + 1) * LANES] = tile.astype(f32)
            at += 1


def assemble(core, pairs, places, shapes):
    flat = [array for pair in pairs for array in pair]
    return pl.pallas_call(
        functools.partial(assemble_kernel, places, [own.shape[0] for own, unused in pairs]),
        grid_spec=pltpu.PrefetchScalarGridSpec(
            num_scalar_prefetch=1,
            grid=(1,),
            in_specs=[whole(array.shape) for array in flat],
            out_specs=[whole(shape) for shape in shapes],
        ),
        out_shape=[jax.ShapeDtypeStruct(shape, f32) for shape in shapes],
        name="assemble",
        compiler_params=params(),
        cost_estimate=cost(5),
    )(core, *flat)


def flip(axis, bit):
    size = lax.axis_size(axis)
    return [(i, i ^ (1 << bit)) for i in range(size)]


def trade(array, axis, bit):
    return lax.ppermute(array, axis, flip(axis, bit))


def add_kernel(plans, *refs):
    ins = refs[: 2 * sum(count for count, unused in plans)]
    outs = refs[len(ins) :]
    at = out_at = 0
    for count, halve in plans:
        col = 0
        for k in range(count):
            own_ref, got_ref = ins[at], ins[at + 1]
            at += 2
            n, m = own_ref.shape[:2]
            total = (own_ref[...].astype(f32) + got_ref[...].astype(f32)).astype(bf16)
            if halve:
                outs[out_at][:, col : col + m] = total[: n // 2]
                outs[out_at + 1][:, col : col + m] = total[n // 2 :]
            else:
                outs[out_at][:, col : col + m] = total
            col += m
        out_at += 2 if halve else 1


def add_all(groups):
    steps = 2
    plans, ins, specs, out_shapes, out_specs = [], [], [], [], []

    def spec(shape):
        return pl.BlockSpec(shape[:2] + (shape[2] // steps, shape[3]), lambda i: (0, 0, i, 0))

    for pairs, halve in groups:
        plans.append((len(pairs), halve))
        for own, got in pairs:
            ins += [own, got]
            specs += [spec(own.shape)] * 2
        n, unused, rows, cols = pairs[0][0].shape
        m = sum(own.shape[1] for own, unused in pairs)
        shape = (n // 2 if halve else n, m, rows, cols)
        out_shapes += [jax.ShapeDtypeStruct(shape, bf16)] * (2 if halve else 1)
        out_specs += [spec(shape)] * (2 if halve else 1)
    return pl.pallas_call(
        functools.partial(add_kernel, plans),
        grid=(steps,),
        in_specs=specs,
        out_specs=out_specs,
        out_shape=out_shapes,
        name="add_all",
        compiler_params=params(),
        cost_estimate=cost(2),
    )(*ins)


def prepare(chains):
    groups = []
    for c in chains:
        c.stage += 1
        groups.append((list(zip(c.own, c.got)), c.stage <= c.clip_bits))
    sums = list(add_all(groups))
    for c, (unused, halve) in zip(chains, groups):
        c.own = [sums.pop(0)]
        c.sends = [sums.pop(0)] if halve else c.own


class Chain:
    def __init__(self, clip_bits, own, sends, stage=0):
        self.clip_bits = clip_bits
        self.own = own
        self.sends = sends
        self.stage = stage
        self.got = None

    def launch(self):
        if self.stage == 0 or self.stage == self.clip_bits + 2:
            axis, bit = "win", 0
        elif self.stage == self.clip_bits + 1:
            axis, bit = "win", 1
        else:
            axis, bit = "clip", self.stage - 1
        self.got = [trade(send, axis, bit) for send in self.sends]

    def finish(self):
        while self.stage < self.clip_bits + 2:
            boundary((), [self], [])
        return self.own[0][0], self.got[0][0]


def unite(*chains):
    first = chains[0]
    united = Chain(first.clip_bits, None, None, first.stage)
    united.own = [o for c in chains for o in c.own]
    united.got = [g for c in chains for g in c.got]
    return united


def boundary(inputs, moved, fresh, held=()):
    waited = moved + list(held)
    got = [c.got for c in waited]
    inputs, got = lax.optimization_barrier((inputs, got))
    for c, g in zip(waited, got):
        c.got = g
    if moved:
        prepare(moved)
    chains = moved + fresh
    inputs, sends = lax.optimization_barrier((inputs, [c.sends for c in chains]))
    for c, sent in zip(chains, sends):
        c.sends = sent
        if c.stage >= c.clip_bits + 1:
            c.own = sent
        c.launch()
    return inputs


def to_quadrants(slot_rows):
    local_slots = slot_rows.shape[0]
    channels = slot_rows.shape[-1]
    arranged = slot_rows.reshape(local_slots, 2, WST, 2, WST, channels).transpose(1, 3, 0, 2, 4, 5)
    return arranged.reshape(4, local_slots, PIECE, channels)


def from_quadrants(received):
    local_slots = received.shape[1]
    channels = received.shape[-1]
    arranged = received.reshape(2, 2, local_slots, WST, WST, channels).transpose(2, 0, 3, 1, 4, 5)
    return arranged.reshape(local_slots, 4 * PIECE, channels)


def exchange(quadrants):
    return lax.all_to_all(quadrants, "win", split_axis=0, concat_axis=0, tiled=True)


def local(
    tokens,
    condition,
    slot_order,
    rel_index,
    w_qkv,
    b_query,
    b_value,
    w_out,
    b_out,
    w_up,
    b_up,
    w_down,
    b_down,
    w_ada,
    b_ada,
    rel_table,
    grad_out,
):
    features = tokens.shape[-1]
    clips = lax.axis_size("clip")
    clip_bits = clips.bit_length() - 1
    me = lax.axis_index("clip")
    core = lax.axis_index("win") & 1
    ff = w_up.shape[1]
    fast = features // clips == LANES and ff // clips == FF_PARTS * LANES

    quadrants, rel_index = lax.optimization_barrier((to_quadrants(tokens[0]), rel_index))
    pieces = exchange(quadrants).reshape(-1, PIECE, features)
    grad_quadrants = to_quadrants(grad_out[0])
    slots = pieces.shape[0]
    per_frame = slots // FRAMES
    order_row = slot_order[0]
    window_place = jnp.arange(slots, dtype=jnp.int32)
    wanted = (window_place % FRAMES) * per_frame + window_place // FRAMES
    src = jnp.sum(
        jnp.where(order_row[None, :] == wanted[:, None], window_place[None, :], 0), axis=1
    ).astype(jnp.int32)
    windows = per_frame
    win = FRAMES * PIECE

    half = win // 2
    idx_mine = lax.dynamic_slice_in_dim(rel_index, core * half, half, 0)
    bias_mine = bias_gather(idx_mine, rel_table)
    lifted = jax.nn.silu(condition.astype(f32)).astype(bf16)
    modulation = jnp.dot(lifted, w_ada, preferred_element_type=f32)[0] + b_ada
    mod = jnp.concatenate([modulation.reshape(6, features), jnp.zeros((2, features), f32)])

    grad_quadrants, bias_mine, mod = lax.optimization_barrier((grad_quadrants, bias_mine, mod))
    grad_pieces = exchange(grad_quadrants).reshape(-1, PIECE, features)
    bias_other = trade(bias_mine, "win", 0)

    qkv_bias = jnp.concatenate([b_query, jnp.zeros_like(b_query), b_value]).astype(f32)[None]
    x_rows, normed, qkv = qkv_call(src, pieces, mod, qkv_bias, w_qkv)
    core_arr = core.astype(jnp.int32)[None]
    attended, probs, recips = attn_forward(core_arr, qkv, bias_mine, bias_other, windows)
    branch, normed_two, grad_mixed = out_call(
        src, grad_pieces, attended, x_rows, mod, b_out.astype(f32)[None], w_out
    )

    shards = features // LANES
    natural = jnp.arange(shards, dtype=jnp.int32)
    if fast:
        places = jnp.zeros_like(natural)
        for bit in range(clip_bits):
            places = places | (((natural >> (clip_bits - 1 - bit)) & 1) << bit)
        order = me ^ places
        inv = jnp.zeros_like(natural)
        for bit in range(clip_bits):
            inv = inv | ((((natural ^ me) >> (clip_bits - 1 - bit)) & 1) << bit)
        per_shard = ff // clips // LANES
        fos = [order * per_shard + j for j in range(FF_PARTS)]
        co = order[::2] & (clips // 2 - 1)
        upper = me >> (clip_bits - 1)
        flags = jnp.stack([core, (upper != core).astype(jnp.int32)]).astype(jnp.int32)
    else:
        inv = natural
        per_part = ff // LANES // FF_PARTS
        fos = [jnp.arange(per_part, dtype=jnp.int32) + j * per_part for j in range(FF_PARTS)]
        co = jnp.arange(per_part // 2, dtype=jnp.int32)
        flags = jnp.zeros((2,), jnp.int32)

    def chain(own, sends):
        return Chain(clip_bits, [own], [sends]) if fast else (own, sends)

    def meet(inputs, moved, fresh=(), held=()):
        return boundary(inputs, list(moved), list(fresh), list(held)) if fast else inputs

    def merge(*chains):
        return unite(*chains) if fast else chains

    b_up_rows = b_up.astype(f32).reshape(-1, 1, LANES)
    before, up_sums, ffs = [], [], []
    steps = [((), ()), ((), (0,)), ((0,), (1,)), ((1,), (2,))]
    for j in range(FF_PARTS):
        moved, fresh = steps[j]
        if j:
            normed_two, grad_mixed = meet(
                (normed_two, grad_mixed), [ffs[k] for k in moved], [ffs[k] for k in fresh]
            )
        if j == 3:
            normed_two, grad_mixed = meet((normed_two, grad_mixed), ffs[:1])
        act, gh, own, other, sums = ff_part(
            j, fos[j], co, inv, flags, normed_two, grad_mixed, w_up, b_up_rows, w_down, before
        )
        before = [act, gh]
        up_sums.append(sums.reshape(-1, LANES))
        ffs.append(chain(own, other))
    act, gh = meet((act, gh), ffs[2:3], ffs[3:])
    act, gh = meet((act, gh), ffs[:2])
    mixed, back = ff_join(jnp.concatenate(fos), act, gh, w_up, w_down)
    mixed, back = meet((mixed, back), ffs[1:], held=ffs[:1])
    gres, early, grad_att, out_own, out_other, out_pieces = ff_rows(
        src, inv, flags, mixed, back, grad_pieces, x_rows, branch, mod, b_down.astype(f32)[None], w_out, attended
    )
    local_slots = tokens.shape[1]
    piece_shape = (-1, local_slots, PIECE, features)
    wos = chain(out_own, out_other)
    grad_att, out_pieces = meet((grad_att, out_pieces), ffs[2:3], [wos], held=ffs[1:2])
    grad_att, out_pieces = meet((grad_att, out_pieces), ffs[3:])
    out_pieces = exchange(out_pieces.reshape(piece_shape))
    pairs = probs.shape[0]
    grads_a, mine_a, others_a = attn_backward(core_arr, qkv, attended, grad_att, probs, recips, windows, 0, FIRST_PAIRS)
    grads_a = meet(grads_a, [ffs[3], wos], held=ffs[2:3])
    qa_own, qa_other = qkv_weight(inv, flags, normed, grads_a)
    qas = chain(qa_own, qa_other)
    front = merge(*ffs[:3])
    grad_att, unused, out_pieces = meet((grad_att, qa_own, out_pieces), [wos, front], [qas], held=ffs[3:])
    others_a = trade(others_a, "win", 0)
    grads_b, mine_b, others_b = attn_backward(
        core_arr, qkv, attended, grad_att, probs, recips, windows, FIRST_PAIRS, pairs - FIRST_PAIRS
    )
    grads_b, others_a, others_b = meet((grads_b, others_a, others_b), [qas, wos])
    others_b = trade(others_b, "win", 0)
    qb_own, qb_other = qkv_weight(inv, flags, normed, grads_b)
    qbs = chain(qb_own, qb_other)

    rear = merge(ffs[3], wos)
    others_a, others_b, unused = meet((others_a, others_b, qb_own), [rear, front], [qbs])
    rel_sums = bucket_sums(idx_mine, [mine_a, mine_b], [others_a, others_b], rel_table.shape[0])

    d = features
    tile_rows = d // LANES
    wins = lax.axis_size("win")
    buckets, heads = rel_table.shape
    gres_late, unused = meet((gres, rel_sums), [rear, qas, qbs])
    home = lax.axis_index("win") if fast else 0
    src_back = (((src // local_slots) ^ home) * local_slots + src % local_slots).astype(jnp.int32)
    *token_parts, late = qkv_backward(src_back, (grads_a, grads_b), w_qkv, x_rows, gres_late, mod)
    if fast:
        token_parts, late, early, up_sums, rel_sums, out_pieces = meet(
            (token_parts, late, early, up_sums, rel_sums, out_pieces), [qbs, qas], held=[front, rear]
        )
        moves = [[(i, i ^ k) for i in range(wins)] for k in range(4)]
        far = [lax.ppermute(token_parts[k], "win", moves[k]) for k in (2, 3)]
        near = lax.ppermute(token_parts[1], "win", moves[1])
        near, late, early, up_sums, rel_sums = boundary((near, late, early, up_sums, rel_sums), [qbs], [])
        here = natural[:, None] == order[None, :]
        up_sums = [jnp.sum(jnp.where(here[:, :, None], u[None], 0.0), axis=1) for u in up_sums]
    grad_b_up = jnp.stack(up_sums, axis=1 if fast else 0)
    if fast:
        to_each = [early[:4].reshape(-1, LANES), late[:2].reshape(-1, LANES), lifted[0].astype(f32).reshape(-1, LANES)]
        by_clip = [v.reshape(clips, 1, LANES) for v in (early[4], early[5], late[2], late[3])]
        by_clip += [grad_b_up.reshape(clips, -1, LANES), rel_sums]
        parts = [jnp.broadcast_to(v[None], (clips,) + v.shape) for v in to_each] + by_clip
        packed = jnp.concatenate(parts, axis=1).astype(bf16)
        packed = jnp.broadcast_to(packed[:, None], (clips, wins) + packed.shape[1:])
        packed = packed.reshape((clips * wins,) + packed.shape[2:])
        vectors = lax.all_to_all(packed, ("clip", "win"), split_axis=0, concat_axis=0, tiled=True)
        last = merge(qas, qbs)
        far = boundary(far, [last], [])
        (vectors,) = boundary((vectors,), [last], [])
        token_pieces = jnp.stack([token_parts[0], near] + far).reshape((2, 2) + token_parts[0].shape)
        for axis, bit in ((0, 1), (1, 0)):
            swapped = (home >> bit) & 1 == 1
            token_pieces = jnp.where(swapped, jnp.flip(token_pieces, axis), token_pieces)
        token_pieces = token_pieces.reshape(piece_shape)
        rows_of = jnp.sum(vectors.astype(f32).reshape((clips, wins) + vectors.shape[1:]), axis=1)
        early_terms = rows_of[:, : 4 * tile_rows].reshape(clips, 4 * d)
        late_terms = rows_of[:, 4 * tile_rows : 6 * tile_rows].reshape(clips, 2 * d)
        all_lifted = rows_of[:, 6 * tile_rows : 7 * tile_rows].reshape(clips, d) * (1.0 / wins)
        own = jnp.sum(rows_of[:, 7 * tile_rows :], axis=0)
        sum_bo, sum_bd, sum_bq, sum_bv = own[0], own[1], own[2], own[3]
        at = 4 + ff // clips // LANES
        sum_bu = own[4:at].reshape(-1)
        sum_rel = own[at:].reshape(2, heads, LANES).transpose(0, 2, 1).reshape(buckets // clips, heads)
    else:
        token_pieces = exchange(jnp.stack(token_parts))

        def all_clips(rows):
            return lax.psum(lax.all_gather(rows.reshape(-1), "clip", axis=0), "win")

        def own_sum(vector):
            return lax.psum(lax.psum_scatter(vector, "clip", scatter_dimension=0, tiled=True), "win")

        early_terms, late_terms = all_clips(early[:4]), all_clips(late[:2])
        all_lifted = lax.all_gather(lifted[0].astype(f32), "clip", axis=0)
        sum_bo, sum_bd, sum_bu = own_sum(early[4]), own_sum(early[5]), own_sum(grad_b_up.reshape(-1))
        sum_bq, sum_bv = own_sum(late[2]), own_sum(late[3])
        rel = rel_sums.reshape(-1, 2, heads, LANES).transpose(0, 1, 3, 2).reshape(buckets, heads)
        sum_rel = own_sum(rel)
    all_terms = jnp.concatenate([late_terms, early_terms], axis=1)

    def own_block(vector):
        size = vector.shape[0] // clips
        return lax.dynamic_slice_in_dim(vector, me * size, size, 0)

    ada_rows = d // clips
    lifted_rows = lax.dynamic_slice_in_dim(all_lifted, me * ada_rows, ada_rows, 1)
    grad_w_ada = jnp.dot(lifted_rows.T, all_terms, precision=lax.Precision.HIGHEST)
    grad_b_ada = own_block(jnp.sum(all_terms, axis=0))

    rows = d // clips
    block_out = from_quadrants(out_pieces).reshape(tokens.shape)
    if fast:
        side = shards // 2
        places = []
        for j in range(FF_PARTS):
            places += [[(0, 0, (c * side + m) * FF_PARTS + j) for c in range(2)] for m in range(side)]
            places += [[(1, j, c * side + m) for c in range(2)] for m in range(side)]
        places += [[(2, 0, c * side + m) for c in range(2)] for m in range(side)]
        sum_wu, sum_wd, sum_wo = assemble(
            core_arr, [front.finish(), rear.finish()], places, [(rows, ff), (ff // clips, d), (rows, d)]
        )
        places, first = [], 0
        for count in (FIRST_PAIRS // 2, (pairs - FIRST_PAIRS) // 2):
            for part in range(3):
                places += [
                    [(0, 0, part * shards + first + c * count + m) for c in range(2)] for m in range(count)
                ]
            first += 2 * count
        (sum_qkv,) = assemble(core_arr, [last.finish()], places, [(rows, 3 * d)])
    else:

        def share(whole_grad):
            part = lax.psum_scatter(whole_grad.astype(f32), "clip", scatter_dimension=0, tiled=True)
            return lax.psum(part, "win")

        def flat_rows(blocks):
            return blocks.transpose(0, 2, 1, 3).reshape(d, -1, LANES)

        halves = len(ffs[0][0][0]) // 2
        ups = [jnp.stack([flat_rows(g[:, :halves]) for g in f], axis=2).reshape(d, -1) for f in ffs]
        sum_wu = share(jnp.concatenate(ups, axis=1))
        downs = [jnp.concatenate([flat_rows(g[:, halves:]).reshape(d, -1) for g in f], axis=1) for f in ffs]
        sum_wd = share(jnp.concatenate(downs, axis=0))
        sum_wo = share(jnp.concatenate([flat_rows(g).reshape(d, -1) for g in wos], axis=1))
        parts = [
            jnp.concatenate([flat_rows(g).reshape(d, 3, -1) for g in q], axis=2) for q in (qas, qbs)
        ]
        sum_qkv = share(jnp.concatenate(parts, axis=2).reshape(d, 3 * d))
    grad_tokens = from_quadrants(token_pieces).reshape(tokens.shape)
    return (
        block_out,
        grad_tokens,
        sum_qkv,
        sum_bq,
        sum_bv,
        sum_wo,
        sum_bo,
        sum_wu,
        sum_bu,
        sum_wd,
        sum_bd,
        grad_w_ada,
        grad_b_ada,
        sum_rel,
    )


def solution(mesh):
    placed = (
        P("clip", "win", None, None),
        P("clip", None),
        P("clip", None),
    ) + (P(),) * 13 + (P("clip", "win", None, None),)
    return jax.shard_map(
        local,
        mesh=mesh,
        in_specs=placed,
        out_specs=(
            P("clip", "win", None, None),
            P("clip", "win", None, None),
            P("clip", None),
            P("clip"),
            P("clip"),
            P("clip", None),
            P("clip"),
            P("clip", None),
            P("clip"),
            P("clip", None),
            P("clip"),
            P("clip", None),
            P("clip"),
            P("clip", None),
        ),
        check_vma=False,
    )
```

```python
import functools
import math

import jax
import jax.numpy as jnp
from jax import lax
from jax.experimental import pallas as pl
from jax.experimental.pallas import tpu as pltpu
from jax.sharding import PartitionSpec as P

HEAD = 64
FRAMES = 5
WST = 8
PIECE = WST * WST
UNIT = 256
FF_PARTS = 4
FF_UNITS = 4
FF_BLOCKS = 2
FIRST_PAIRS = 6
LANES = 128
VMEM_LIMIT = 60 * 1024 * 1024
f32 = jnp.float32
bf16 = jnp.bfloat16
GELU_C = math.sqrt(2.0 / math.pi)
GELU_A = 0.044715


def dot_nn(a, b):
    return jnp.dot(a, b, preferred_element_type=f32)


def dot_nt(a, b):
    return lax.dot_general(a, b, (((1,), (1,)), ((), ())), preferred_element_type=f32)


def dot_tn(a, b):
    return lax.dot_general(a, b, (((0,), (0,)), ((), ())), preferred_element_type=f32)


def params():
    return pltpu.CompilerParams(vmem_limit_bytes=VMEM_LIMIT)


def cost(micros):
    return pl.CostEstimate(
        flops=int(micros * 1.0e9), bytes_accessed=int(micros * 2.0e6), transcendentals=0
    )


def pick(swap, first, second):
    return jnp.where(swap, second, first), jnp.where(swap, first, second)


def hat_of(rows):
    average = jnp.mean(rows, axis=-1, keepdims=True)
    centered = rows - average
    variance = jnp.mean(centered * centered, axis=-1, keepdims=True)
    inv_std = lax.rsqrt(variance + 1e-06)
    return centered * inv_std, inv_std


def norm_back(grad_hat, hat_rows, inv_std):
    first_mean = jnp.mean(grad_hat, axis=-1, keepdims=True)
    second_mean = jnp.mean(grad_hat * hat_rows, axis=-1, keepdims=True)
    return inv_std * (grad_hat - first_mean - hat_rows * second_mean)


def whole(shape):
    zeros = (0,) * len(shape)
    return pl.BlockSpec(shape, lambda *unused: zeros, pipeline_mode=pl.Buffered(1))


def bias_kernel(idx_ref, tab_ref, out_ref, scr_ref):
    lows = lax.broadcasted_iota(jnp.int32, (256, idx_ref.shape[1]), 0)
    tab = tab_ref[...]
    half = tab.shape[0] // 2
    heads = 16
    tiles = idx_ref.shape[1] // LANES
    win = out_ref.shape[2] // 2
    for i in range(8):
        idx = idx_ref[pl.ds(i, 1), :]
        low = idx & 255
        high = idx >> 8
        onehot = jnp.where(lows == low, 1.0, 0.0).astype(bf16)
        got = dot_nn(tab, onehot)
        got = got[:half] + got[half:]
        acc = got[:heads]
        for c in range(1, half // heads):
            acc = jnp.where(high == c, got[c * heads : (c + 1) * heads], acc)
        for t in range(tiles):
            scr_ref[t, pl.ds(i, heads, stride=8), :] = acc[:, t * LANES : (t + 1) * LANES]
    for pair in range(heads // 2):
        rows = []
        for h in range(2):
            at = (2 * pair + h) * 8
            rows.append(
                jnp.concatenate([scr_ref[t, at : at + 8, :] for t in range(tiles)], axis=1)[:, :win]
            )
        out_ref[pair] = jnp.concatenate(rows, axis=1)


def bias_gather(idx, table):
    rows, win = idx.shape
    padded = -(-win // LANES) * LANES
    buckets, heads = table.shape
    upper_f = lax.reduce_precision(table, 8, 7)
    lower = (table - upper_f).astype(bf16)

    def arrange(t):
        return t.reshape(-1, 256, heads).transpose(0, 2, 1).reshape(-1, 256)

    tab = jnp.concatenate([arrange(upper_f.astype(bf16)), arrange(lower)], axis=0)
    idx = jnp.pad(idx, ((0, 0), (0, padded - win)))
    return pl.pallas_call(
        bias_kernel,
        grid=(rows // 8,),
        in_specs=[pl.BlockSpec((8, padded), lambda i: (i, 0)), whole(tab.shape)],
        out_specs=pl.BlockSpec((heads // 2, 8, 2 * win), lambda i: (0, i, 0)),
        out_shape=jax.ShapeDtypeStruct((heads // 2, rows, 2 * win), f32),
        scratch_shapes=[pltpu.VMEM((padded // LANES, 8 * heads, LANES), f32)],
        name="bias_gather",
        compiler_params=params(),
        cost_estimate=cost(0.9),
    )(idx, tab)


def bucket_kernel(idx_ref, *refs):
    out_ref, acc_ref, scr_ref = refs[-3:]
    keep_refs = refs[: (len(refs) - 3) // 2]
    got_refs = refs[(len(refs) - 3) // 2 : -3]

    @pl.when(pl.program_id(0) == 0)
    def _():
        acc_ref[...] = jnp.zeros_like(acc_ref)

    padded = idx_ref.shape[1]
    tiles = padded // LANES
    keeps = [(r, k) for r in keep_refs for k in range(r.shape[0])]
    gots = [(r, k) for r in got_refs for k in range(r.shape[0])]
    pairs = len(keeps)
    heads = 2 * pairs
    win = keep_refs[0].shape[2] // 2
    step_rows = idx_ref.shape[0]
    lows = lax.broadcasted_iota(jnp.int32, (256, padded), 0)
    zero = jnp.zeros((step_rows, padded - win), f32)
    for pair in range(pairs):
        (keep_ref, k), (got_ref, unused) = keeps[pair], gots[pair]
        sums = keep_ref[k].astype(f32) + got_ref[k].astype(f32)
        for h in range(2):
            part = jnp.concatenate([sums[:, h * win : (h + 1) * win], zero], axis=1)
            at = (2 * pair + h) * step_rows
            for t in range(tiles):
                scr_ref[t, at : at + step_rows, :] = part[:, t * LANES : (t + 1) * LANES]
    total = acc_ref[...]
    for i in range(step_rows):
        idx = idx_ref[pl.ds(i, 1), :]
        low = idx & 255
        high = idx >> 8
        onehot = jnp.where(lows == low, 1.0, 0.0).astype(bf16)
        sums = jnp.concatenate(
            [scr_ref[t, pl.ds(i, heads, stride=step_rows), :] for t in range(tiles)], axis=1
        )
        spread = jnp.concatenate(
            [jnp.where(high == c, sums, 0.0) for c in range(acc_ref.shape[0] // heads)], axis=0
        )
        total += dot_nt(spread.astype(bf16), onehot)
    acc_ref[...] = total

    @pl.when(pl.program_id(0) == pl.num_programs(0) - 1)
    def _():
        for k in range(out_ref.shape[0]):
            for t in range(2):
                out_ref[k, t * heads : (t + 1) * heads] = total[
                    k * heads : (k + 1) * heads, t * LANES : (t + 1) * LANES
                ]


def bucket_sums(idx, keeps, gots, buckets):
    rows, win = idx.shape
    padded = -(-win // LANES) * LANES
    heads = 2 * sum(k.shape[0] for k in keeps)
    step_rows = 16
    idx = jnp.pad(idx, ((0, 0), (0, padded - win)))
    out_rows = buckets // 256
    sum_specs = [pl.BlockSpec((k.shape[0], step_rows, 2 * win), lambda i: (0, i, 0)) for k in keeps]
    out_shape = jax.ShapeDtypeStruct((out_rows, 2 * heads, LANES), f32)
    return pl.pallas_call(
        bucket_kernel,
        grid=(rows // step_rows,),
        in_specs=[pl.BlockSpec((step_rows, padded), lambda i: (i, 0))] + sum_specs + sum_specs,
        out_specs=pl.BlockSpec(out_shape.shape, lambda i: (0, 0, 0)),
        out_shape=out_shape,
        scratch_shapes=[
            pltpu.VMEM((out_rows * heads, 256), f32),
            pltpu.VMEM((padded // LANES, step_rows * heads, LANES), f32),
        ],
        name="bucket_sums",
        compiler_params=params(),
        cost_estimate=cost(4),
    )(idx, *keeps, *gots)


def qkv_kernel(src_ref, a_ref, b_ref, c_ref, d_ref, mod_ref, bias_ref, w_ref, x_ref, n_ref, o_ref):
    rows = jnp.concatenate([r[0] for r in (a_ref, b_ref, c_ref, d_ref)], axis=0)
    x_ref[...] = rows
    hat_rows, unused = hat_of(rows.astype(f32))
    normed = (hat_rows * (1.0 + mod_ref[1:2, :]) + mod_ref[0:1, :]).astype(bf16)
    n_ref[...] = normed
    features = rows.shape[1]
    for j in range(w_ref.shape[1] // 512):
        cols = slice(j * 512, (j + 1) * 512)
        got = dot_nn(normed, w_ref[:, cols]) + bias_ref[0:1, cols]
        if (j + 1) * 512 <= features:
            got = got.astype(bf16).astype(f32) * (1.0 / math.sqrt(HEAD))
        o_ref[:, cols] = got.astype(bf16)


def slot_spec(features, t):
    return pl.BlockSpec((1, PIECE, features), lambda i, src, t=t: (src[4 * i + t], 0, 0))


def qkv_call(src, pieces, mod, qkv_bias, w_qkv):
    count, unused, features = pieces.shape
    rows = count * PIECE
    wide = w_qkv.shape[1]
    block = 4 * PIECE
    return pl.pallas_call(
        qkv_kernel,
        grid_spec=pltpu.PrefetchScalarGridSpec(
            num_scalar_prefetch=1,
            grid=(count // 4,),
            in_specs=[slot_spec(features, t) for t in range(4)]
            + [whole(mod.shape), whole(qkv_bias.shape), whole(w_qkv.shape)],
            out_specs=[
                pl.BlockSpec((block, features), lambda i, src: (i, 0)),
                pl.BlockSpec((block, features), lambda i, src: (i, 0)),
                pl.BlockSpec((block, wide), lambda i, src: (i, 0)),
            ],
        ),
        out_shape=[
            jax.ShapeDtypeStruct((rows, features), bf16),
            jax.ShapeDtypeStruct((rows, features), bf16),
            jax.ShapeDtypeStruct((rows, wide), bf16),
        ],
        name="norm_qkv",
        compiler_params=params(),
        cost_estimate=cost(0.6),
    )(src, pieces, pieces, pieces, pieces, mod, qkv_bias, w_qkv)


def split_pair(x, left):
    zero = jnp.zeros_like(x)
    return jnp.concatenate([jnp.where(left, x, zero), jnp.where(left, zero, x)], axis=0)


def values_ones(v, left):
    one = jnp.ones_like(v)
    zero = jnp.zeros_like(v)
    marks = jnp.concatenate([jnp.where(left, one, zero), jnp.where(left, zero, one)], axis=0)
    return jnp.concatenate([split_pair(v, left), marks], axis=1)


def attn_kernel(windows, core_ref, q_ref, k_ref, v_ref, mine_ref, other_ref, o_ref, p_ref, r_ref, b_ref):
    win = q_ref.shape[0] // windows
    half = win // 2
    left = lax.broadcasted_iota(jnp.int32, (win, LANES), 1) < HEAD
    first = core_ref[0] == 0
    b_ref[:half] = jnp.where(first, mine_ref[0], other_ref[0])
    b_ref[half:] = jnp.where(first, other_ref[0], mine_ref[0])
    lowest = jnp.float32(-jnp.inf)
    whole_tiles = win // LANES * LANES
    for u in range(windows):
        rows = slice(u * win, (u + 1) * win)
        keys = split_pair(k_ref[rows], left)
        vals = values_ones(v_ref[rows], left)
        s = dot_nt(q_ref[rows], keys) + b_ref[...]
        lo = s[:, :whole_tiles]
        mid = s[:, whole_tiles : whole_tiles + LANES]
        hi = s[:, whole_tiles + LANES :]
        top_lo = jnp.where(left, mid, lowest)
        top_hi = jnp.where(left, lowest, mid)
        for t in range(whole_tiles // LANES):
            cols = slice(t * LANES, (t + 1) * LANES)
            top_lo = jnp.maximum(top_lo, lo[:, cols])
            top_hi = jnp.maximum(top_hi, hi[:, cols])
        top_lo = jnp.max(top_lo, axis=1, keepdims=True)
        top_hi = jnp.max(top_hi, axis=1, keepdims=True)
        e = jnp.concatenate(
            [
                jnp.exp(lo - top_lo),
                jnp.exp(mid - jnp.where(left, top_lo, top_hi)),
                jnp.exp(hi - top_hi),
            ],
            axis=1,
        ).astype(bf16)
        p_ref[0, u] = e
        got = dot_nn(e, vals)
        r = 1.0 / got[:, LANES:]
        r_ref[rows] = r
        o_ref[rows] = (got[:, :LANES] * r).astype(bf16)


def attn_forward(core, qkv, bias_mine, bias_other, windows):
    rows = qkv.shape[0]
    win = rows // windows
    pairs = bias_mine.shape[0]
    features = qkv.shape[1] // 3

    def col(part):
        return pl.BlockSpec((rows, LANES), lambda h, c, part=part: (0, part * pairs + h))

    half_spec = pl.BlockSpec((1, win // 2, 2 * win), lambda h, c: (h, 0, 0))
    return pl.pallas_call(
        functools.partial(attn_kernel, windows),
        grid_spec=pltpu.PrefetchScalarGridSpec(
            num_scalar_prefetch=1,
            grid=(pairs,),
            in_specs=[col(0), col(1), col(2), half_spec, half_spec],
            out_specs=[
                col(0),
                pl.BlockSpec((1, windows, win, 2 * win), lambda h, c: (h, 0, 0, 0)),
                col(0),
            ],
            scratch_shapes=[pltpu.VMEM((win, 2 * win), f32)],
        ),
        out_shape=[
            jax.ShapeDtypeStruct((rows, features), bf16),
            jax.ShapeDtypeStruct((pairs, windows, win, 2 * win), bf16),
            jax.ShapeDtypeStruct((rows, features), f32),
        ],
        name="attn_forward",
        compiler_params=params(),
        cost_estimate=cost(0.9),
    )(core, qkv, qkv, qkv, bias_mine, bias_other)


def fold_delta(dx, lane):
    lower_half = (lane & 32) == 0
    dx = dx + jnp.where(lower_half, pltpu.roll(dx, LANES - 32, 1), pltpu.roll(dx, 32, 1))
    upper = dx.astype(bf16)
    lower = (dx - upper.astype(f32)).astype(bf16)
    return jnp.where(lower_half, upper, lower)


def attn_back_kernel(windows, core_ref, q_ref, k_ref, v_ref, o_ref, do_ref, p_ref, r_ref, g_ref, mine_ref, other_ref):
    win = q_ref.shape[0] // windows
    lane = lax.broadcasted_iota(jnp.int32, (win, LANES), 1)
    left = lane < HEAD
    sums = None
    for u in range(windows):
        rows = slice(u * win, (u + 1) * win)
        keys = split_pair(k_ref[rows], left)
        vals = values_ones(v_ref[rows], left)
        up = (do_ref[rows].astype(f32) * r_ref[rows]).astype(bf16)
        delta = fold_delta(-(up.astype(f32) * o_ref[rows].astype(f32)), lane)
        d = dot_nt(jnp.concatenate([up, delta], axis=1), vals)
        p = p_ref[0, u]
        ds = p.astype(f32) * d
        sums = ds if sums is None else sums + ds
        low = ds.astype(bf16)
        g_ref[0, rows] = (dot_nn(low, keys) * (1.0 / math.sqrt(HEAD))).astype(bf16)
        dk = dot_tn(low, q_ref[rows])
        g_ref[1, rows] = jnp.where(left, dk[:win], dk[win:]).astype(bf16)
        dv = dot_tn(p, up)
        g_ref[2, rows] = jnp.where(left, dv[:win], dv[win:]).astype(bf16)
    half = win // 2
    first, second = sums[:half].astype(bf16), sums[half:].astype(bf16)
    mine_ref[0], other_ref[0] = pick(core_ref[0] == 1, first, second)


def attn_backward(core, qkv, attended, grad_att, probs, recips, windows, first, count):
    rows = qkv.shape[0]
    win = rows // windows
    pairs = probs.shape[0]

    def col(part):
        return pl.BlockSpec((rows, LANES), lambda h, core, part=part: (0, part * pairs + first + h))

    half_spec = pl.BlockSpec((1, win // 2, 2 * win), lambda h, core: (h, 0, 0))
    half_shape = jax.ShapeDtypeStruct((count, win // 2, 2 * win), bf16)
    return pl.pallas_call(
        functools.partial(attn_back_kernel, windows),
        grid_spec=pltpu.PrefetchScalarGridSpec(
            num_scalar_prefetch=1,
            grid=(count,),
            in_specs=[
                col(0),
                col(1),
                col(2),
                col(0),
                col(0),
                pl.BlockSpec((1, windows, win, 2 * win), lambda h, core: (first + h, 0, 0, 0)),
                col(0),
            ],
            out_specs=[
                pl.BlockSpec((3, rows, LANES), lambda h, core: (0, 0, h)),
                half_spec,
                half_spec,
            ],
        ),
        out_shape=[jax.ShapeDtypeStruct((3, rows, count * LANES), bf16), half_shape, half_shape],
        name="attn_backward",
        compiler_params=params(),
        cost_estimate=cost(3 * count),
    )(core, qkv, qkv, qkv, attended, grad_att, probs, recips)


def out_kernel(src_ref, a_ref, b_ref, c_ref, d_ref, att_ref, x_ref, mod_ref, bo_ref, w_ref, branch_ref, n_ref, gm_ref):
    branch = (dot_nn(att_ref[...], w_ref[...]) + bo_ref[...]).astype(bf16)
    branch_ref[...] = branch
    residual = x_ref[...].astype(f32) + mod_ref[2:3, :] * branch.astype(f32)
    hat_rows, unused = hat_of(residual)
    n_ref[...] = (hat_rows * (1.0 + mod_ref[4:5, :]) + mod_ref[3:4, :]).astype(bf16)
    up = jnp.concatenate([r[0] for r in (a_ref, b_ref, c_ref, d_ref)], axis=0)
    gm_ref[...] = (mod_ref[5:6, :] * up.astype(f32)).astype(bf16)


def out_call(src, pieces, attended, x_rows, mod, b_out, w_out):
    count, unused, features = pieces.shape
    rows = count * PIECE
    block = 4 * PIECE
    rows_spec = pl.BlockSpec((block, features), lambda i, src: (i, 0))
    sds = jax.ShapeDtypeStruct((rows, features), bf16)
    return pl.pallas_call(
        out_kernel,
        grid_spec=pltpu.PrefetchScalarGridSpec(
            num_scalar_prefetch=1,
            grid=(count // 4,),
            in_specs=[slot_spec(features, t) for t in range(4)]
            + [rows_spec, rows_spec, whole(mod.shape), whole(b_out.shape), whole(w_out.shape)],
            out_specs=[rows_spec, rows_spec, rows_spec],
        ),
        out_shape=[sds, sds, sds],
        name="out_norm",
        compiler_params=params(),
        cost_estimate=cost(0.3),
    )(src, pieces, pieces, pieces, pieces, attended, x_rows, mod, b_out, w_out)


def place_rows(inv_ref, out_ref, values):
    for k in range(out_ref.shape[0]):
        at = inv_ref[k]
        for m in range(out_ref.shape[1]):
            out_ref[at, m] = values[k * LANES : (k + 1) * LANES, m * LANES : (m + 1) * LANES]


def ff_part_kernel(count, fo_ref, co_ref, inv_ref, flag_ref, n_ref, gm_ref, *refs):
    ups = refs[:count]
    biases = refs[count : 2 * count]
    downs = refs[2 * count : 3 * count]
    act_ref, gh_ref, own_ref, other_ref, sum_ref = refs[-5:]
    step = pl.program_id(0)
    rows = n_ref.shape[0]
    block = rows // FF_BLOCKS
    wu = jnp.concatenate([r[...] for r in ups], axis=1)
    wd = jnp.concatenate([r[...] for r in downs], axis=0)
    bias = jnp.concatenate([r[0] for r in biases], axis=1)
    sums = None
    for c in range(FF_BLOCKS):
        part = slice(c * block, (c + 1) * block)
        v = dot_nn(n_ref[part], wu) + bias
        v2 = v * v
        t = jnp.tanh(v * (GELU_C + (GELU_C * GELU_A) * v2))
        h = 0.5 + 0.5 * t
        slope = h + (0.5 * v) * (1.0 - t * t) * (GELU_C + (3.0 * GELU_C * GELU_A) * v2)
        gh = (dot_nt(gm_ref[part], wd) * slope).astype(bf16)
        act_ref[0, part] = (v * h).astype(bf16)
        gh_ref[0, part] = gh
        piece = jnp.sum(gh.astype(f32), axis=0, keepdims=True)
        sums = piece if sums is None else sums + piece
    sum_ref[0] = sums
    up = dot_tn(n_ref[...], gh_ref[0]).astype(bf16)
    down = dot_tn(act_ref[0], gm_ref[...]).astype(bf16)
    half = down.shape[1] // 2
    blocks = half // LANES
    for p in range(count // 2):
        left = up[:, 2 * p * LANES : (2 * p + 1) * LANES]
        right = up[:, (2 * p + 1) * LANES : (2 * p + 2) * LANES]
        own, other = pick(flag_ref[1] == 1, left, right)
        col = co_ref[step * (count // 2) + p]
        for k in range(own_ref.shape[0]):
            at = inv_ref[k]
            own_ref[at, col] = own[k * LANES : (k + 1) * LANES]
            other_ref[at, col] = other[k * LANES : (k + 1) * LANES]
    own, other = pick(flag_ref[0] == 1, down[:, :half], down[:, half:])
    first = own_ref.shape[1] - blocks
    for k in range(count):
        for m in range(blocks):
            tile = (slice(k * LANES, (k + 1) * LANES), slice(m * LANES, (m + 1) * LANES))
            own_ref[step * count + k, first + m] = own[tile]
            other_ref[step * count + k, first + m] = other[tile]


def ff_part(j, fo, co, inv, flags, normed, grad_mixed, w_up, b_up, w_down, before):
    units = fo.shape[0]
    count = FF_UNITS
    steps = units // count
    rows, features = normed.shape

    def up(k):
        return pl.BlockSpec((features, LANES), lambda i, fo, *more: (0, fo[count * i + k]))

    def bias(k):
        return pl.BlockSpec((1, 1, LANES), lambda i, fo, *more: (fo[count * i + k], 0, 0))

    def down(k):
        return pl.BlockSpec((LANES, features), lambda i, fo, *more: (fo[count * i + k], 0))

    cols = pl.BlockSpec((1, rows, count * LANES), lambda i, *more: (j, 0, i))
    hidden = jax.ShapeDtypeStruct((FF_PARTS, rows, units * LANES), bf16)
    blocks = units // 2 + features // 2 // LANES
    grad = jax.ShapeDtypeStruct((units, blocks, LANES, LANES), bf16)
    ks = range(count)
    at = 4 + 2 + 3 * count
    return pl.pallas_call(
        functools.partial(ff_part_kernel, count),
        grid_spec=pltpu.PrefetchScalarGridSpec(
            num_scalar_prefetch=4,
            grid=(steps,),
            in_specs=[whole(normed.shape), whole(normed.shape)]
            + [up(k) for k in ks]
            + [bias(k) for k in ks]
            + [down(k) for k in ks]
            + [pl.BlockSpec(memory_space=pl.ANY)] * len(before),
            out_specs=[cols, cols, whole(grad.shape), whole(grad.shape)]
            + [pl.BlockSpec((1, 1, count * LANES), lambda i, *more: (i, 0, 0))],
        ),
        out_shape=[hidden, hidden, grad, grad, jax.ShapeDtypeStruct((steps, 1, count * LANES), f32)],
        input_output_aliases={at: 0, at + 1: 1} if before else {},
        name="ff_part",
        compiler_params=params(),
        cost_estimate=cost(20),
    )(fo, co, inv, flags, normed, grad_mixed, *[w_up] * count, *[b_up] * count, *[w_down] * count, *before)


def ff_join_kernel(units, parts, fo_ref, act_ref, gh_ref, *refs):
    up_refs = refs[:units]
    down_refs = refs[units : 2 * units]
    mixed_ref, back_ref, mixed_sum, back_sum = refs[2 * units :]
    step = pl.program_id(0)
    half = mixed_ref.shape[0] // 2

    def each(put):
        wd = jnp.concatenate([r[...] for r in down_refs], axis=0)
        wu = jnp.concatenate([r[...] for r in up_refs], axis=1)
        for k in range(2):
            part = slice(k * half, (k + 1) * half)
            put(part, mixed_ref, mixed_sum, dot_nn(act_ref[0, part], wd))
            put(part, back_ref, back_sum, dot_nt(gh_ref[0, part], wu))

    def first(part, out_ref, sum_ref, got):
        sum_ref[part] = got

    def middle(part, out_ref, sum_ref, got):
        sum_ref[part] += got

    def last(part, out_ref, sum_ref, got):
        out_ref[part] = (sum_ref[part] + got).astype(bf16)

    @pl.when(step == 0)
    def _():
        each(first)

    @pl.when(jnp.logical_and(step > 0, step < parts - 1))
    def _():
        each(middle)

    @pl.when(step == parts - 1)
    def _():
        each(last)


def ff_join(fo, act, gh, w_up, w_down):
    parts, rows, wide = act.shape
    units = wide // LANES
    features = w_up.shape[0]
    ups = [
        pl.BlockSpec((features, LANES), lambda i, fo, u=u: (0, fo[i * units + u])) for u in range(units)
    ]
    downs = [
        pl.BlockSpec((LANES, features), lambda i, fo, u=u: (fo[i * units + u], 0)) for u in range(units)
    ]
    hidden = pl.BlockSpec((1, rows, wide), lambda i, fo: (i, 0, 0))
    sums = jax.ShapeDtypeStruct((rows, features), bf16)
    return pl.pallas_call(
        functools.partial(ff_join_kernel, units, parts),
        grid_spec=pltpu.PrefetchScalarGridSpec(
            num_scalar_prefetch=1,
            grid=(parts,),
            in_specs=[hidden, hidden] + ups + downs,
            out_specs=[whole(sums.shape), whole(sums.shape)],
            scratch_shapes=[pltpu.VMEM(sums.shape, f32), pltpu.VMEM(sums.shape, f32)],
        ),
        out_shape=[sums, sums],
        name="ff_join",
        compiler_params=params(),
        cost_estimate=cost(28),
    )(fo, act, gh, *([w_up] * units), *([w_down] * units))


def ff_rows_kernel(blocks, src_ref, inv_ref, flag_ref, mixed_ref, back_ref, *refs):
    a_ref, b_ref, c_ref, d_ref, x_ref, branch_ref, mod_ref, bd_ref, wo_ref, att_ref = refs[:10]
    gres_ref, vec_ref, do_ref, own_ref, other_ref, out_ref = refs[10:16]
    stage_ref, gb_ref, sem_ref = refs[16:]
    step = pl.program_id(0)

    @pl.when(step < blocks)
    def _():
        e = step
        block = 4 * PIECE
        part = pl.ds(pl.multiple_of(e * block, block), block)
        mixed = mixed_ref[...].astype(f32) + bd_ref[...]
        back = back_ref[...].astype(f32)
        branch = branch_ref[...].astype(f32)
        gate_one = mod_ref[2:3, :]
        gate_two = mod_ref[5:6, :]
        residual = x_ref[...].astype(f32) + gate_one * branch
        hat_rows, inv_std = hat_of(residual)
        up = jnp.concatenate([r[0] for r in (a_ref, b_ref, c_ref, d_ref)], axis=0).astype(f32)
        stage_ref[part] = (residual + gate_two * mixed).astype(bf16)
        for t in range(4):
            pltpu.make_async_copy(
                stage_ref.at[pl.ds(pl.multiple_of(e * block + t * PIECE, PIECE), PIECE)],
                out_ref.at[src_ref[4 * e + t]],
                sem_ref.at[4 * e + t],
            ).start()
        gres = up + norm_back(back * (1.0 + mod_ref[4:5, :]), hat_rows, inv_std)
        gres_ref[...] = gres.astype(bf16)
        low = (gate_one * gres).astype(bf16)
        gb_ref[part] = low
        do_ref[...] = dot_nt(low, wo_ref[...]).astype(bf16)
        grad_mixed = (gate_two * up).astype(bf16).astype(f32)

        def total(values):
            return jnp.sum(values, axis=0, keepdims=True)

        pieces = jnp.concatenate(
            [
                total(gres * branch),
                total(back),
                total(back * hat_rows),
                total(up * mixed),
                total(low.astype(f32)),
                total(grad_mixed),
                jnp.zeros((2, gate_one.shape[1]), f32),
            ],
            axis=0,
        )

        @pl.when(e == 0)
        def _():
            vec_ref[...] = pieces

        @pl.when(e > 0)
        def _():
            vec_ref[...] += pieces

    @pl.when(step >= blocks)
    def _():
        width = own_ref.shape[1] * LANES
        half = gb_ref.shape[1] // 2
        flag = flag_ref[0]
        for grad_ref, side in ((own_ref, flag), (other_ref, 1 - flag)):
            start = pl.multiple_of(side * half + (step - blocks) * width, width)
            got = dot_tn(att_ref[...], gb_ref[:, pl.ds(start, width)])
            place_rows(inv_ref, grad_ref, got.astype(bf16))

    @pl.when(step == pl.num_programs(0) - 1)
    def _():
        for k in range(sem_ref.shape[0]):
            pltpu.make_async_copy(
                stage_ref.at[pl.ds(k * PIECE, PIECE)], out_ref.at[src_ref[k]], sem_ref.at[k]
            ).wait()


def ff_rows(src, inv, flags, mixed, back, pieces, x_rows, branch, mod, b_down, w_out, attended):
    rows, features = x_rows.shape
    shards = features // LANES
    block = 4 * PIECE
    blocks = rows // block
    ends = features // 2 // UNIT

    def at(i):
        return jnp.minimum(i, blocks - 1)

    rows_spec = pl.BlockSpec((block, features), lambda i, *more: (at(i), 0))
    slots = [
        pl.BlockSpec((1, PIECE, features), lambda i, src, *more, t=t: (src[4 * at(i) + t], 0, 0))
        for t in range(4)
    ]
    grad_spec = pl.BlockSpec(
        (shards, UNIT // LANES, LANES, LANES), lambda i, *more: (0, jnp.maximum(i - blocks, 0), 0, 0)
    )
    grad = jax.ShapeDtypeStruct((shards, features // 2 // LANES, LANES, LANES), bf16)
    rows_shape = jax.ShapeDtypeStruct((rows, features), bf16)
    return pl.pallas_call(
        functools.partial(ff_rows_kernel, blocks),
        grid_spec=pltpu.PrefetchScalarGridSpec(
            num_scalar_prefetch=3,
            grid=(blocks + ends,),
            in_specs=[rows_spec, rows_spec]
            + slots
            + [rows_spec, rows_spec, whole(mod.shape), whole(b_down.shape)]
            + [whole(w_out.shape), whole(attended.shape)],
            out_specs=[
                rows_spec,
                pl.BlockSpec((8, features), lambda i, *more: (0, 0)),
                rows_spec,
                grad_spec,
                grad_spec,
                pl.BlockSpec(memory_space=pl.ANY),
            ],
            scratch_shapes=[
                pltpu.VMEM((rows, features), bf16),
                pltpu.VMEM((rows, features), bf16),
                pltpu.SemaphoreType.DMA((rows // PIECE,)),
            ],
        ),
        out_shape=[
            rows_shape,
            jax.ShapeDtypeStruct((8, features), f32),
            rows_shape,
            grad,
            grad,
            jax.ShapeDtypeStruct(pieces.shape, bf16),
        ],
        name="ff_rows",
        compiler_params=params(),
        cost_estimate=cost(22),
    )(src, inv, flags, mixed, back, *([pieces] * 4), x_rows, branch, mod, b_down, w_out, attended)


def qkv_weight_kernel(inv_ref, flag_ref, n_ref, grad_ref, g0_ref, g1_ref):
    got = dot_tn(n_ref[...], grad_ref[0]).astype(bf16)
    half = got.shape[1] // 2
    own, other = pick(flag_ref[0] == 1, got[:, :half], got[:, half:])
    place_rows(inv_ref, g0_ref, own)
    place_rows(inv_ref, g1_ref, other)


def qkv_weight(inv, flags, normed, grads):
    rows, features = normed.shape
    parts, unused, wide = grads.shape
    shards = features // LANES
    tiles = wide // 2 // LANES
    out_spec = pl.BlockSpec((shards, tiles, LANES, LANES), lambda i, *more: (0, i, 0, 0))
    grad = jax.ShapeDtypeStruct((shards, parts * tiles, LANES, LANES), bf16)
    return pl.pallas_call(
        qkv_weight_kernel,
        grid_spec=pltpu.PrefetchScalarGridSpec(
            num_scalar_prefetch=2,
            grid=(parts,),
            in_specs=[
                whole(normed.shape),
                pl.BlockSpec((1, rows, wide), lambda i, *more: (i, 0, 0)),
            ],
            out_specs=[out_spec, out_spec],
        ),
        out_shape=[grad, grad],
        name="qkv_weight",
        compiler_params=params(),
        cost_estimate=cost(6),
    )(inv, flags, normed, grads)


def qkv_back_kernel(src_ref, *refs):
    count = len(refs) - 11
    grads = refs[:count]
    w_ref, x_ref, gres_ref, mod_ref = refs[count : count + 4]
    out_refs = refs[count + 4 : count + 8]
    vec_ref, stage_ref, sem_ref = refs[count + 8 :]
    per = out_refs[0].shape[0]
    step = pl.program_id(0)
    block = x_ref.shape[0]
    features = x_ref.shape[1]
    back = None
    bias = []
    for part in range(3):
        joined = jnp.concatenate([g[part] for g in grads], axis=1)
        bias.append(jnp.sum(joined.astype(f32), axis=0, keepdims=True))
        got = dot_nt(joined, w_ref[:, part * features : (part + 1) * features])
        back = got if back is None else back + got
    back = back.astype(bf16).astype(f32)
    hat_rows, inv_std = hat_of(x_ref[...].astype(f32))
    grad = gres_ref[...].astype(f32) + norm_back(back * (1.0 + mod_ref[1:2, :]), hat_rows, inv_std)
    stage_ref[pl.ds(pl.multiple_of(step * block, block), block)] = grad.astype(bf16)
    for t in range(4):
        slot = src_ref[4 * step + t]
        for k in range(4):

            @pl.when(slot // per == k)
            def _(k=k, t=t, slot=slot):
                pltpu.make_async_copy(
                    stage_ref.at[pl.ds(pl.multiple_of(step * block + t * PIECE, PIECE), PIECE)],
                    out_refs[k].at[slot - k * per],
                    sem_ref.at[4 * step + t],
                ).start()
    pieces = jnp.concatenate(
        [
            jnp.sum(back, axis=0, keepdims=True),
            jnp.sum(back * hat_rows, axis=0, keepdims=True),
            bias[0],
            bias[2],
            jnp.zeros((4, features), f32),
        ],
        axis=0,
    )

    @pl.when(step == 0)
    def _():
        vec_ref[...] = pieces

    @pl.when(step > 0)
    def _():
        vec_ref[...] += pieces

    @pl.when(step == pl.num_programs(0) - 1)
    def _():
        for k in range(sem_ref.shape[0]):
            pltpu.make_async_copy(
                stage_ref.at[pl.ds(k * PIECE, PIECE)], out_refs[0].at[0], sem_ref.at[k]
            ).wait()


def qkv_backward(src, grads, w_qkv, x_rows, gres, mod):
    rows, features = x_rows.shape
    block = 4 * PIECE
    rows_spec = pl.BlockSpec((block, features), lambda i, src: (i, 0))
    grad_specs = [pl.BlockSpec((3, block, g.shape[2]), lambda i, src: (0, i, 0)) for g in grads]
    return pl.pallas_call(
        qkv_back_kernel,
        grid_spec=pltpu.PrefetchScalarGridSpec(
            num_scalar_prefetch=1,
            grid=(rows // block,),
            in_specs=grad_specs + [whole(w_qkv.shape), rows_spec, rows_spec, whole(mod.shape)],
            out_specs=[
                *[pl.BlockSpec(memory_space=pl.ANY)] * 4,
                pl.BlockSpec((8, features), lambda i, src: (0, 0)),
            ],
            scratch_shapes=[
                pltpu.VMEM((rows, features), bf16),
                pltpu.SemaphoreType.DMA((rows // PIECE,)),
            ],
        ),
        out_shape=[
            *[jax.ShapeDtypeStruct((rows // PIECE // 4, PIECE, features), bf16)] * 4,
            jax.ShapeDtypeStruct((8, features), f32),
        ],
        name="qkv_backward",
        compiler_params=params(),
        cost_estimate=cost(14),
    )(src, *grads, w_qkv, x_rows, gres, mod)


def assemble_kernel(places, counts, core_ref, *refs):
    ins = refs[: 2 * len(counts)]
    outs = refs[2 * len(counts) :]
    swap = core_ref[0] == 1
    at = 0
    for k, count in enumerate(counts):
        for m in range(count):
            pair = pick(swap, ins[2 * k][m], ins[2 * k + 1][m])
            for tile, (out, row, col) in zip(pair, places[at]):
                outs[out][row * LANES : (row + 1) * LANES, col * LANES : (col + 1) * LANES] = tile.astype(f32)
            at += 1


def assemble(core, pairs, places, shapes):
    flat = [array for pair in pairs for array in pair]
    return pl.pallas_call(
        functools.partial(assemble_kernel, places, [own.shape[0] for own, unused in pairs]),
        grid_spec=pltpu.PrefetchScalarGridSpec(
            num_scalar_prefetch=1,
            grid=(1,),
            in_specs=[whole(array.shape) for array in flat],
            out_specs=[whole(shape) for shape in shapes],
        ),
        out_shape=[jax.ShapeDtypeStruct(shape, f32) for shape in shapes],
        name="assemble",
        compiler_params=params(),
        cost_estimate=cost(5),
    )(core, *flat)


def flip(axis, bit):
    size = lax.axis_size(axis)
    return [(i, i ^ (1 << bit)) for i in range(size)]


def trade(array, axis, bit):
    return lax.ppermute(array, axis, flip(axis, bit))


def add_kernel(plans, *refs):
    ins = refs[: 2 * sum(count for count, unused in plans)]
    outs = refs[len(ins) :]
    at = out_at = 0
    for count, halve in plans:
        col = 0
        for k in range(count):
            own_ref, got_ref = ins[at], ins[at + 1]
            at += 2
            n, m = own_ref.shape[:2]
            total = (own_ref[...].astype(f32) + got_ref[...].astype(f32)).astype(bf16)
            if halve:
                outs[out_at][:, col : col + m] = total[: n // 2]
                outs[out_at + 1][:, col : col + m] = total[n // 2 :]
            else:
                outs[out_at][:, col : col + m] = total
            col += m
        out_at += 2 if halve else 1


def add_all(groups):
    steps = 2
    plans, ins, specs, out_shapes, out_specs = [], [], [], [], []

    def spec(shape):
        return pl.BlockSpec(shape[:2] + (shape[2] // steps, shape[3]), lambda i: (0, 0, i, 0))

    for pairs, halve in groups:
        plans.append((len(pairs), halve))
        for own, got in pairs:
            ins += [own, got]
            specs += [spec(own.shape)] * 2
        n, unused, rows, cols = pairs[0][0].shape
        m = sum(own.shape[1] for own, unused in pairs)
        shape = (n // 2 if halve else n, m, rows, cols)
        out_shapes += [jax.ShapeDtypeStruct(shape, bf16)] * (2 if halve else 1)
        out_specs += [spec(shape)] * (2 if halve else 1)
    return pl.pallas_call(
        functools.partial(add_kernel, plans),
        grid=(steps,),
        in_specs=specs,
        out_specs=out_specs,
        out_shape=out_shapes,
        name="add_all",
        compiler_params=params(),
        cost_estimate=cost(2),
    )(*ins)


def prepare(chains):
    groups = []
    for c in chains:
        c.stage += 1
        groups.append((list(zip(c.own, c.got)), c.stage <= c.clip_bits))
    sums = list(add_all(groups))
    for c, (unused, halve) in zip(chains, groups):
        c.own = [sums.pop(0)]
        c.sends = [sums.pop(0)] if halve else c.own


class Chain:
    def __init__(self, clip_bits, own, sends, stage=0):
        self.clip_bits = clip_bits
        self.own = own
        self.sends = sends
        self.stage = stage
        self.got = None

    def launch(self):
        if self.stage == 0 or self.stage == self.clip_bits + 2:
            axis, bit = "win", 0
        elif self.stage == self.clip_bits + 1:
            axis, bit = "win", 1
        else:
            axis, bit = "clip", self.stage - 1
        self.got = [trade(send, axis, bit) for send in self.sends]

    def finish(self):
        while self.stage < self.clip_bits + 2:
            boundary((), [self], [])
        return self.own[0][0], self.got[0][0]


def unite(*chains):
    first = chains[0]
    united = Chain(first.clip_bits, None, None, first.stage)
    united.own = [o for c in chains for o in c.own]
    united.got = [g for c in chains for g in c.got]
    return united


def boundary(inputs, moved, fresh, held=()):
    waited = moved + list(held)
    got = [c.got for c in waited]
    inputs, got = lax.optimization_barrier((inputs, got))
    for c, g in zip(waited, got):
        c.got = g
    if moved:
        prepare(moved)
    chains = moved + fresh
    inputs, sends = lax.optimization_barrier((inputs, [c.sends for c in chains]))
    for c, sent in zip(chains, sends):
        c.sends = sent
        if c.stage >= c.clip_bits + 1:
            c.own = sent
        c.launch()
    return inputs


def to_quadrants(slot_rows):
    local_slots = slot_rows.shape[0]
    channels = slot_rows.shape[-1]
    arranged = slot_rows.reshape(local_slots, 2, WST, 2, WST, channels).transpose(1, 3, 0, 2, 4, 5)
    return arranged.reshape(4, local_slots, PIECE, channels)


def from_quadrants(received):
    local_slots = received.shape[1]
    channels = received.shape[-1]
    arranged = received.reshape(2, 2, local_slots, WST, WST, channels).transpose(2, 0, 3, 1, 4, 5)
    return arranged.reshape(local_slots, 4 * PIECE, channels)


def exchange(quadrants):
    return lax.all_to_all(quadrants, "win", split_axis=0, concat_axis=0, tiled=True)


def local(
    tokens,
    condition,
    slot_order,
    rel_index,
    w_qkv,
    b_query,
    b_value,
    w_out,
    b_out,
    w_up,
    b_up,
    w_down,
    b_down,
    w_ada,
    b_ada,
    rel_table,
    grad_out,
):
    features = tokens.shape[-1]
    clips = lax.axis_size("clip")
    clip_bits = clips.bit_length() - 1
    me = lax.axis_index("clip")
    core = lax.axis_index("win") & 1
    ff = w_up.shape[1]
    fast = features // clips == LANES and ff // clips == FF_PARTS * LANES

    quadrants, rel_index = lax.optimization_barrier((to_quadrants(tokens[0]), rel_index))
    pieces = exchange(quadrants).reshape(-1, PIECE, features)
    grad_quadrants = to_quadrants(grad_out[0])
    slots = pieces.shape[0]
    per_frame = slots // FRAMES
    order_row = slot_order[0]
    window_place = jnp.arange(slots, dtype=jnp.int32)
    wanted = (window_place % FRAMES) * per_frame + window_place // FRAMES
    src = jnp.sum(
        jnp.where(order_row[None, :] == wanted[:, None], window_place[None, :], 0), axis=1
    ).astype(jnp.int32)
    windows = per_frame
    win = FRAMES * PIECE

    half = win // 2
    idx_mine = lax.dynamic_slice_in_dim(rel_index, core * half, half, 0)
    bias_mine = bias_gather(idx_mine, rel_table)
    lifted = jax.nn.silu(condition.astype(f32)).astype(bf16)
    modulation = jnp.dot(lifted, w_ada, preferred_element_type=f32)[0] + b_ada
    mod = jnp.concatenate([modulation.reshape(6, features), jnp.zeros((2, features), f32)])

    grad_quadrants, bias_mine, mod = lax.optimization_barrier((grad_quadrants, bias_mine, mod))
    grad_pieces = exchange(grad_quadrants).reshape(-1, PIECE, features)
    bias_other = trade(bias_mine, "win", 0)

    qkv_bias = jnp.concatenate([b_query, jnp.zeros_like(b_query), b_value]).astype(f32)[None]
    x_rows, normed, qkv = qkv_call(src, pieces, mod, qkv_bias, w_qkv)
    core_arr = core.astype(jnp.int32)[None]
    attended, probs, recips = attn_forward(core_arr, qkv, bias_mine, bias_other, windows)
    branch, normed_two, grad_mixed = out_call(
        src, grad_pieces, attended, x_rows, mod, b_out.astype(f32)[None], w_out
    )

    shards = features // LANES
    natural = jnp.arange(shards, dtype=jnp.int32)
    if fast:
        places = jnp.zeros_like(natural)
        for bit in range(clip_bits):
            places = places | (((natural >> (clip_bits - 1 - bit)) & 1) << bit)
        order = me ^ places
        inv = jnp.zeros_like(natural)
        for bit in range(clip_bits):
            inv = inv | ((((natural ^ me) >> (clip_bits - 1 - bit)) & 1) << bit)
        per_shard = ff // clips // LANES
        fos = [order * per_shard + j for j in range(FF_PARTS)]
        co = order[::2] & (clips // 2 - 1)
        upper = me >> (clip_bits - 1)
        flags = jnp.stack([core, (upper != core).astype(jnp.int32)]).astype(jnp.int32)
    else:
        inv = natural
        per_part = ff // LANES // FF_PARTS
        fos = [jnp.arange(per_part, dtype=jnp.int32) + j * per_part for j in range(FF_PARTS)]
        co = jnp.arange(per_part // 2, dtype=jnp.int32)
        flags = jnp.zeros((2,), jnp.int32)

    def chain(own, sends):
        return Chain(clip_bits, [own], [sends]) if fast else (own, sends)

    def meet(inputs, moved, fresh=(), held=()):
        return boundary(inputs, list(moved), list(fresh), list(held)) if fast else inputs

    def merge(*chains):
        return unite(*chains) if fast else chains

    b_up_rows = b_up.astype(f32).reshape(-1, 1, LANES)
    before, up_sums, ffs = [], [], []
    steps = [((), ()), ((), (0,)), ((0,), (1,)), ((1,), (2,))]
    for j in range(FF_PARTS):
        moved, fresh = steps[j]
        if j:
            normed_two, grad_mixed = meet(
                (normed_two, grad_mixed), [ffs[k] for k in moved], [ffs[k] for k in fresh]
            )
        if j == 3:
            normed_two, grad_mixed = meet((normed_two, grad_mixed), ffs[:1])
        act, gh, own, other, sums = ff_part(
            j, fos[j], co, inv, flags, normed_two, grad_mixed, w_up, b_up_rows, w_down, before
        )
        before = [act, gh]
        up_sums.append(sums.reshape(-1, LANES))
        ffs.append(chain(own, other))
    act, gh = meet((act, gh), ffs[2:3], ffs[3:])
    act, gh = meet((act, gh), ffs[:2])
    mixed, back = ff_join(jnp.concatenate(fos), act, gh, w_up, w_down)
    mixed, back = meet((mixed, back), ffs[1:], held=ffs[:1])
    gres, early, grad_att, out_own, out_other, out_pieces = ff_rows(
        src, inv, flags, mixed, back, grad_pieces, x_rows, branch, mod, b_down.astype(f32)[None], w_out, attended
    )
    local_slots = tokens.shape[1]
    piece_shape = (-1, local_slots, PIECE, features)
    wos = chain(out_own, out_other)
    grad_att, out_pieces = meet((grad_att, out_pieces), ffs[2:3], [wos], held=ffs[1:2])
    grad_att, out_pieces = meet((grad_att, out_pieces), ffs[3:])
    out_pieces = exchange(out_pieces.reshape(piece_shape))
    pairs = probs.shape[0]
    grads_a, mine_a, others_a = attn_backward(core_arr, qkv, attended, grad_att, probs, recips, windows, 0, FIRST_PAIRS)
    grads_a = meet(grads_a, [ffs[3], wos], held=ffs[2:3])
    qa_own, qa_other = qkv_weight(inv, flags, normed, grads_a)
    qas = chain(qa_own, qa_other)
    front = merge(*ffs[:3])
    grad_att, qa_own = meet((grad_att, qa_own), [wos], [qas])
    grad_att, unused, out_pieces = meet((grad_att, qa_own, out_pieces), [front], held=ffs[3:])
    others_a = trade(others_a, "win", 0)
    grads_b, mine_b, others_b = attn_backward(
        core_arr, qkv, attended, grad_att, probs, recips, windows, FIRST_PAIRS, pairs - FIRST_PAIRS
    )
    grads_b, others_a, others_b = meet((grads_b, others_a, others_b), [qas, wos])
    others_b = trade(others_b, "win", 0)
    qb_own, qb_other = qkv_weight(inv, flags, normed, grads_b)
    qbs = chain(qb_own, qb_other)

    rear = merge(ffs[3], wos)
    others_a, others_b, unused = meet((others_a, others_b, qb_own), [rear, front], [qbs])
    rel_sums = bucket_sums(idx_mine, [mine_a, mine_b], [others_a, others_b], rel_table.shape[0])

    d = features
    tile_rows = d // LANES
    wins = lax.axis_size("win")
    buckets, heads = rel_table.shape
    gres_late, unused = meet((gres, rel_sums), [rear, qas, qbs])
    home = lax.axis_index("win") if fast else 0
    src_back = (((src // local_slots) ^ home) * local_slots + src % local_slots).astype(jnp.int32)
    *token_parts, late = qkv_backward(src_back, (grads_a, grads_b), w_qkv, x_rows, gres_late, mod)
    if fast:
        token_parts, late, early, up_sums, rel_sums, out_pieces = meet(
            (token_parts, late, early, up_sums, rel_sums, out_pieces), [qbs, qas], held=[front, rear]
        )
        moves = [[(i, i ^ k) for i in range(wins)] for k in range(4)]
        far = [lax.ppermute(token_parts[k], "win", moves[k]) for k in (2, 3)]
        near = lax.ppermute(token_parts[1], "win", moves[1])
        near, late, early, up_sums, rel_sums = boundary((near, late, early, up_sums, rel_sums), [qbs], [])
        here = natural[:, None] == order[None, :]
        up_sums = [jnp.sum(jnp.where(here[:, :, None], u[None], 0.0), axis=1) for u in up_sums]
    grad_b_up = jnp.stack(up_sums, axis=1 if fast else 0)
    if fast:
        to_each = [early[:4].reshape(-1, LANES), late[:2].reshape(-1, LANES), lifted[0].astype(f32).reshape(-1, LANES)]
        by_clip = [v.reshape(clips, 1, LANES) for v in (early[4], early[5], late[2], late[3])]
        by_clip += [grad_b_up.reshape(clips, -1, LANES), rel_sums]
        parts = [jnp.broadcast_to(v[None], (clips,) + v.shape) for v in to_each] + by_clip
        packed = jnp.concatenate(parts, axis=1).astype(bf16)
        packed = jnp.broadcast_to(packed[:, None], (clips, wins) + packed.shape[1:])
        packed = packed.reshape((clips * wins,) + packed.shape[2:])
        vectors = lax.all_to_all(packed, ("clip", "win"), split_axis=0, concat_axis=0, tiled=True)
        last = merge(qas, qbs)
        far = boundary(far, [last], [])
        (vectors,) = boundary((vectors,), [last], [])
        token_pieces = jnp.stack([token_parts[0], near] + far).reshape((2, 2) + token_parts[0].shape)
        for axis, bit in ((0, 1), (1, 0)):
            swapped = (home >> bit) & 1 == 1
            token_pieces = jnp.where(swapped, jnp.flip(token_pieces, axis), token_pieces)
        token_pieces = token_pieces.reshape(piece_shape)
        rows_of = jnp.sum(vectors.astype(f32).reshape((clips, wins) + vectors.shape[1:]), axis=1)
        early_terms = rows_of[:, : 4 * tile_rows].reshape(clips, 4 * d)
        late_terms = rows_of[:, 4 * tile_rows : 6 * tile_rows].reshape(clips, 2 * d)
        all_lifted = rows_of[:, 6 * tile_rows : 7 * tile_rows].reshape(clips, d) * (1.0 / wins)
        own = jnp.sum(rows_of[:, 7 * tile_rows :], axis=0)
        sum_bo, sum_bd, sum_bq, sum_bv = own[0], own[1], own[2], own[3]
        at = 4 + ff // clips // LANES
        sum_bu = own[4:at].reshape(-1)
        sum_rel = own[at:].reshape(2, heads, LANES).transpose(0, 2, 1).reshape(buckets // clips, heads)
    else:
        token_pieces = exchange(jnp.stack(token_parts))

        def all_clips(rows):
            return lax.psum(lax.all_gather(rows.reshape(-1), "clip", axis=0), "win")

        def own_sum(vector):
            return lax.psum(lax.psum_scatter(vector, "clip", scatter_dimension=0, tiled=True), "win")

        early_terms, late_terms = all_clips(early[:4]), all_clips(late[:2])
        all_lifted = lax.all_gather(lifted[0].astype(f32), "clip", axis=0)
        sum_bo, sum_bd, sum_bu = own_sum(early[4]), own_sum(early[5]), own_sum(grad_b_up.reshape(-1))
        sum_bq, sum_bv = own_sum(late[2]), own_sum(late[3])
        rel = rel_sums.reshape(-1, 2, heads, LANES).transpose(0, 1, 3, 2).reshape(buckets, heads)
        sum_rel = own_sum(rel)
    all_terms = jnp.concatenate([late_terms, early_terms], axis=1)

    def own_block(vector):
        size = vector.shape[0] // clips
        return lax.dynamic_slice_in_dim(vector, me * size, size, 0)

    ada_rows = d // clips
    lifted_rows = lax.dynamic_slice_in_dim(all_lifted, me * ada_rows, ada_rows, 1)
    grad_w_ada = jnp.dot(lifted_rows.T, all_terms, precision=lax.Precision.HIGHEST)
    grad_b_ada = own_block(jnp.sum(all_terms, axis=0))

    rows = d // clips
    block_out = from_quadrants(out_pieces).reshape(tokens.shape)
    if fast:
        side = shards // 2
        places = []
        for j in range(FF_PARTS):
            places += [[(0, 0, (c * side + m) * FF_PARTS + j) for c in range(2)] for m in range(side)]
            places += [[(1, j, c * side + m) for c in range(2)] for m in range(side)]
        places += [[(2, 0, c * side + m) for c in range(2)] for m in range(side)]
        sum_wu, sum_wd, sum_wo = assemble(
            core_arr, [front.finish(), rear.finish()], places, [(rows, ff), (ff // clips, d), (rows, d)]
        )
        places, first = [], 0
        for count in (FIRST_PAIRS // 2, (pairs - FIRST_PAIRS) // 2):
            for part in range(3):
                places += [
                    [(0, 0, part * shards + first + c * count + m) for c in range(2)] for m in range(count)
                ]
            first += 2 * count
        (sum_qkv,) = assemble(core_arr, [last.finish()], places, [(rows, 3 * d)])
    else:

        def share(whole_grad):
            part = lax.psum_scatter(whole_grad.astype(f32), "clip", scatter_dimension=0, tiled=True)
            return lax.psum(part, "win")

        def flat_rows(blocks):
            return blocks.transpose(0, 2, 1, 3).reshape(d, -1, LANES)

        halves = len(ffs[0][0][0]) // 2
        ups = [jnp.stack([flat_rows(g[:, :halves]) for g in f], axis=2).reshape(d, -1) for f in ffs]
        sum_wu = share(jnp.concatenate(ups, axis=1))
        downs = [jnp.concatenate([flat_rows(g[:, halves:]).reshape(d, -1) for g in f], axis=1) for f in ffs]
        sum_wd = share(jnp.concatenate(downs, axis=0))
        sum_wo = share(jnp.concatenate([flat_rows(g).reshape(d, -1) for g in wos], axis=1))
        parts = [
            jnp.concatenate([flat_rows(g).reshape(d, 3, -1) for g in q], axis=2) for q in (qas, qbs)
        ]
        sum_qkv = share(jnp.concatenate(parts, axis=2).reshape(d, 3 * d))
    grad_tokens = from_quadrants(token_pieces).reshape(tokens.shape)
    return (
        block_out,
        grad_tokens,
        sum_qkv,
        sum_bq,
        sum_bv,
        sum_wo,
        sum_bo,
        sum_wu,
        sum_bu,
        sum_wd,
        sum_bd,
        grad_w_ada,
        grad_b_ada,
        sum_rel,
    )


def solution(mesh):
    placed = (
        P("clip", "win", None, None),
        P("clip", None),
        P("clip", None),
    ) + (P(),) * 13 + (P("clip", "win", None, None),)
    return jax.shard_map(
        local,
        mesh=mesh,
        in_specs=placed,
        out_specs=(
            P("clip", "win", None, None),
            P("clip", "win", None, None),
            P("clip", None),
            P("clip"),
            P("clip"),
            P("clip", None),
            P("clip"),
            P("clip", None),
            P("clip"),
            P("clip", None),
            P("clip"),
            P("clip", None),
            P("clip"),
            P("clip", None),
        ),
        check_vma=False,
    )
```
